512 devices in a mesh: grp: 4 (over x), row: 16 (over y, z_hi), col: 8 (over z_lo, core).
Axes of the slice: x: 4, y: 4, z: 16 (z_hi: 4, z_lo: 4; z = z_hi * 4 + z_lo), core: 2. Of those that a mesh axis runs over, the one named last changes fastest.
Arguments:
- physical_values: bfloat16 [512, 100, 2688], P(('grp', 'row', 'col')), may hold values from -6 to 6
- samples_per_parallel: int32 [512], replicated, may hold values from 20 to 2688, as said below
- associated_polynomials: bfloat16 [640, 512, 640], P(('row', 'col'), 'grp'), may hold values from -4 to 4
- heat_salt_anomalies: float32 [2, 8, 256, 1024], P(None, None, ('grp', 'row'), 'col'), may hold values from -6 to 6
- courant_numbers: float32 [2, 8, 256, 1024], P(None, None, ('grp', 'row'), 'col'), may hold values from -0.35 to 0.35
- water_indicator: int32 [256, 1024], P(('grp', 'row'), 'col'), may hold values 0 or 1
- air_to_sea_coefficients: bfloat16 [256, 2, 1024, 128], P(('grp', 'row'), None, 'col'), may hold values from -0.375 to 0.375
- air_partner_span: int32 [256, 8, 2], P(('grp', 'row'), 'col'), may hold values from 0 to 167
- sea_to_air_coefficients: bfloat16 [512, 21, 128, 128], P(('grp', 'row', 'col')), may hold values from -0.5 to 0.5
- sea_partner_span: int32 [512, 21], P(('grp', 'row', 'col')), may hold values from 0 to 31
Outputs:
- spectral: bfloat16 [100, 2, 640, 640], P(None, None, ('row', 'col'), 'grp')
- tracers_out: float32 [2, 8, 256, 1024], P(None, None, ('grp', 'row'), 'col')
The draws below stay inside these ranges and needn't reach their ends.
Inputs may be any that keep to these rules, and one draw needn't show every extreme that they name: `samples_per_parallel`: a multiple of 4; some row has exactly 2688 points.
All inputs are finite; a program needn't handle non-finite values. No bound on the sum of `water_indicator` on one device may be relied on, other than what follows from the above.
Results may differ from the reference program's by a relative error of at most 0.013.
Values may be sent and summed in bfloat16 or wider, within the bound.
A program may use at most 64 MiB of HBM per device.

```python
import math
import jax
import jax.numpy as jnp
from jax import lax

LEV = 10
WIDEST_PARALLEL = 2688
M = 640
NDEG = 640
REGRID_SPAN = 128
KSRC = 2
PATCH_LINES = 4
LEV_O = 8
TSTEPS = 2
FL = 100
SPANS_PER_CIRCLE = 21
PARALLEL_CIRCLES = 512
OX = 256
OY = 1024
N_GRP = 4
N_ROW = 16
N_COL = 8


def draw_samples_per_parallel(key, part):
    key = jax.random.fold_in(key, 11)
    first_key, second_key = jax.random.split(key)
    steps_drawn = jax.random.randint(first_key, (PARALLEL_CIRCLES,), 0, (WIDEST_PARALLEL - 20) // 4 + 1)
    counts = 20 + 4 * steps_drawn
    fullest = jax.random.randint(second_key, (), 0, PARALLEL_CIRCLES)
    return jnp.where(jnp.arange(PARALLEL_CIRCLES) == fullest, WIDEST_PARALLEL, counts).astype(jnp.int32)


def touch_ends(drawn, own_key, smallest, largest):
    dims = drawn.shape
    spot = [jax.random.randint(jax.random.fold_in(own_key, axis), (), 0, dims[axis]) for axis in range(len(dims))]
    drawn = drawn.at[tuple(spot)].set(smallest)
    longest = dims.index(max(dims))
    spot[longest] = (spot[longest] + 1) % dims[longest]
    return drawn.at[tuple(spot)].set(largest)


def shard_levels(key, shape, shards, smallest, top_value):
    factor_of = 1.0
    for axis_at, shards_of in shards:
        heights = jax.random.uniform(jax.random.fold_in(jax.random.fold_in(key, 6), axis_at), (shards_of,), jnp.float32, smallest / len(shards), top_value / len(shards))
        factor_of = factor_of * jnp.repeat(jnp.exp(heights), shape[axis_at] // shards_of).reshape((-1,) + (1,) * (len(shape) - 1 - axis_at))
    return factor_of


def centred(own_key, shape, width, most, shards=(), held_as=jnp.bfloat16):
    entries = jax.random.normal(own_key, shape, jnp.float32) * width
    if len(shards) > 0:
        entries = shard_levels(own_key, shape, shards, -0.22, 0.18) * entries
    return jnp.clip(entries, min=-most, max=most).astype(held_as)


def setup_inputs(seed: int = 0) -> dict:
    key_list = jax.random.split(jax.random.key(seed), 11)
    return {
        "physical_values": centred(key_list[0], (PARALLEL_CIRCLES, FL, WIDEST_PARALLEL), 1.0, 6.0, ((0, 512),)),
        "samples_per_parallel": draw_samples_per_parallel(jax.random.fold_in(key_list[10], 71), 0),
        "associated_polynomials": centred(key_list[2], (M, PARALLEL_CIRCLES, NDEG), 1.0, 4.0, ((0, 128), (1, 4))),
        "heat_salt_anomalies": centred(key_list[3], (2, LEV_O, OX, OY), 1.0, 6.0, ((2, 64), (3, 8)), jnp.float32),
        "courant_numbers": jnp.clip(jax.random.uniform(key_list[4], (2, LEV_O, OX, OY), jnp.float32, -0.35, 0.35) * shard_levels(key_list[4], (2, LEV_O, OX, OY), ((2, 64), (3, 8)), -0.4, 0.0), -0.35, 0.35),
        "water_indicator": touch_ends((jax.random.randint(key_list[5], (OX, OY), 0, 5) < 4).astype(jnp.int32), jax.random.fold_in(key_list[5], 1), 0, 1),
        "air_to_sea_coefficients": centred(key_list[6], (OX, KSRC, OY, REGRID_SPAN), (KSRC * REGRID_SPAN) ** -0.5, 0.375, ((0, 64), (2, 8))),
        "air_partner_span": touch_ends(jax.random.randint(key_list[7], (OX, N_COL, KSRC), 0, N_COL * SPANS_PER_CIRCLE), jax.random.fold_in(key_list[7], 1), 0, (N_COL * SPANS_PER_CIRCLE) - 1).astype(jnp.int32),
        "sea_to_air_coefficients": centred(key_list[8], (PARALLEL_CIRCLES, SPANS_PER_CIRCLE, REGRID_SPAN, REGRID_SPAN), REGRID_SPAN ** -0.5, 0.5, ((0, 512),)),
        "sea_partner_span": touch_ends(jax.random.randint(key_list[9], (PARALLEL_CIRCLES, SPANS_PER_CIRCLE), 0, N_COL * PATCH_LINES), jax.random.fold_in(key_list[9], 1), 0, (N_COL * PATCH_LINES) - 1).astype(jnp.int32),
    }


DIFFUSION = 0.07
COUPLE = 0.5
BLOCK_POINTS = 512


def fourier_table(block_start, point_count, wave_count):
    places = block_start + lax.broadcasted_iota(jnp.int32, (BLOCK_POINTS, wave_count), 0)
    orders = lax.broadcasted_iota(jnp.int32, (BLOCK_POINTS, wave_count), 1)
    phase_index = (places * orders) % point_count
    angles = phase_index.astype(jnp.float32) * (2.0 * math.pi) / point_count.astype(jnp.float32)
    return jnp.concatenate([jnp.cos(angles), -jnp.sin(angles)], axis=1).astype(jnp.bfloat16)


def fourier_part(padded_row, point_count, range_low, range_high, wave_count):
    plane_count = padded_row.shape[0]
    block_total = (range_high - range_low + BLOCK_POINTS - 1) // BLOCK_POINTS

    def add_block(block_index, running):
        block_start = (range_low + block_index * BLOCK_POINTS).astype(jnp.int32)
        segment = lax.dynamic_slice_in_dim(padded_row, block_start, BLOCK_POINTS, 1)
        places = block_start + lax.broadcasted_iota(jnp.int32, (1, BLOCK_POINTS), 1)
        segment = jnp.where(places < range_high, segment, jnp.zeros_like(segment))
        wave_table = fourier_table(block_start, point_count, wave_count)
        return running + jnp.dot(segment, wave_table, preferred_element_type=jnp.float32)

    return lax.fori_loop(0, block_total, add_block, jnp.zeros((plane_count, 2 * wave_count), jnp.float32))


def finish(running, point_count, wave_count):
    plane_count = running.shape[0]
    scaled = (running / point_count.astype(jnp.float32)).reshape(plane_count, 2, wave_count)
    orders = lax.broadcasted_iota(jnp.int32, (1, 1, wave_count), 2)
    return jnp.where(2 * orders < point_count, scaled, jnp.zeros_like(scaled)).astype(jnp.bfloat16)


def advance(tracer_ext, static_ext, levels):
    span_x = tracer_ext.shape[1]
    span_y = tracer_ext.shape[2]
    tracer_all = tracer_ext.reshape(2, levels, span_x, span_y)
    eastward = static_ext[:levels]
    northward = static_ext[levels:2 * levels]
    wet_cells = static_ext[2 * levels]
    forcing = static_ext[2 * levels + 1:2 * levels + 3]
    pair_x = wet_cells[:-1, :] * wet_cells[1:, :]
    lower_x = tracer_all[:, :, :-1, :]
    upper_x = tracer_all[:, :, 1:, :]
    speed_x = eastward[:, :-1, :]
    flow_x = pair_x * (jnp.maximum(speed_x, 0.0) * lower_x + jnp.minimum(speed_x, 0.0) * upper_x - DIFFUSION * (upper_x - lower_x))
    pair_y = wet_cells[:, :-1] * wet_cells[:, 1:]
    lower_y = tracer_all[:, :, :, :-1]
    upper_y = tracer_all[:, :, :, 1:]
    speed_y = northward[:, :, :-1]
    flow_y = pair_y * (jnp.maximum(speed_y, 0.0) * lower_y + jnp.minimum(speed_y, 0.0) * upper_y - DIFFUSION * (upper_y - lower_y))
    spread = flow_x[:, :, 1:, 1:-1] - flow_x[:, :, :-1, 1:-1] + flow_y[:, :, 1:-1, 1:] - flow_y[:, :, 1:-1, :-1]
    push = COUPLE * forcing[:, 1:-1, 1:-1]
    source_levels = jnp.concatenate([push[:, None], jnp.zeros((2, levels - 1, span_x - 2, span_y - 2), push.dtype)], axis=1)
    updated = tracer_all[:, :, 1:-1, 1:-1] + wet_cells[1:-1, 1:-1] * (source_levels - spread)
    return updated.reshape(2 * levels, span_x - 2, span_y - 2)


def reference(physical_values, samples_per_parallel, associated_polynomials, heat_salt_anomalies, courant_numbers, water_indicator, air_to_sea_coefficients, air_partner_span, sea_to_air_coefficients, sea_partner_span):
    stretch_number = N_GRP * N_ROW
    positions = jnp.arange(WIDEST_PARALLEL, dtype=jnp.int32)
    is_live = positions[None, None, :] < samples_per_parallel[:, None, None]
    flux_planes = jnp.stack([physical_values[:, LEV], physical_values[:, 2 * LEV]], axis=1)
    flux_planes = jnp.where(is_live, flux_planes, jnp.zeros_like(flux_planes))
    flux_flat = flux_planes.reshape(stretch_number, N_COL, 2, SPANS_PER_CIRCLE, REGRID_SPAN).transpose(0, 1, 3, 2, 4).reshape(stretch_number * N_COL * SPANS_PER_CIRCLE, 2, REGRID_SPAN)
    tile_band = jnp.arange(OX, dtype=jnp.int32) // PATCH_LINES
    flux_index = (tile_band[:, None, None] * (N_COL * SPANS_PER_CIRCLE) + air_partner_span).astype(jnp.int32)
    picked = jnp.take(flux_flat, flux_index, axis=0)
    weights = air_to_sea_coefficients.reshape(OX, KSRC, N_COL, REGRID_SPAN, REGRID_SPAN).astype(jnp.float32)
    forcing = jnp.einsum("xkcyj,xckqj->qxcy", weights, picked.astype(jnp.float32), precision=lax.Precision.HIGHEST).reshape(2, OX, OY)
    ocean_state = heat_salt_anomalies.reshape(2 * LEV_O, OX, OY)
    static = jnp.concatenate([courant_numbers.reshape(2 * LEV_O, OX, OY), water_indicator.astype(jnp.float32)[None], forcing])
    pad_width = ((0, 0), (1, 1), (1, 1))
    static_ext = jnp.pad(static, pad_width)
    for step_index in range(TSTEPS):
        ocean_state = advance(jnp.pad(ocean_state, pad_width), static_ext, LEV_O)
    lowest_level_quantity = ocean_state[0].astype(jnp.bfloat16)
    sea_warmth_linear = lowest_level_quantity.reshape(stretch_number, PATCH_LINES, N_COL, REGRID_SPAN).transpose(0, 2, 1, 3).reshape(stretch_number * N_COL * PATCH_LINES, REGRID_SPAN)
    parallel_stretch = jnp.arange(PARALLEL_CIRCLES, dtype=jnp.int32) // N_COL
    sea_warmth_position = (parallel_stretch[:, None] * (N_COL * PATCH_LINES) + sea_partner_span).astype(jnp.int32)
    sea_warmth_selected = jnp.take(sea_warmth_linear, sea_warmth_position, axis=0)
    sea_warmth_samples = jnp.einsum("mifk,mik->mif", sea_to_air_coefficients.astype(jnp.float32), sea_warmth_selected.astype(jnp.float32), precision=lax.Precision.HIGHEST).reshape(PARALLEL_CIRCLES, WIDEST_PARALLEL)
    interface_heat_layer = (physical_values[:, 0].astype(jnp.float32) + sea_warmth_samples).astype(jnp.bfloat16)
    lowest_level_parallels = jnp.concatenate([interface_heat_layer[:, None], physical_values[:, 1:]], axis=1)
    lowest_level_parallels = jnp.pad(lowest_level_parallels, ((0, 0), (0, 0), (0, BLOCK_POINTS)))

    def transform(inputs):
        one_row, point_count = inputs
        running = fourier_part(one_row, point_count, jnp.int32(0), point_count, M)
        return finish(running, point_count, M)

    fourier = lax.map(transform, (lowest_level_parallels, samples_per_parallel))
    group_rows = N_ROW * N_COL
    spectral = jnp.zeros((FL, 2, M, NDEG), jnp.float32)
    for group_index in range(N_GRP):
        part_rows = fourier[group_index * group_rows:(group_index + 1) * group_rows].astype(jnp.float32)
        part_table = associated_polynomials[:, group_index * group_rows:(group_index + 1) * group_rows].astype(jnp.float32)
        partial_value = jnp.einsum("lfcm,mln->fcmn", part_rows, part_table, precision=lax.Precision.HIGHEST)
        spectral = spectral + partial_value.astype(jnp.bfloat16).astype(jnp.float32)
    return spectral.astype(jnp.bfloat16), ocean_state.reshape(2, LEV_O, OX, OY)
```

```python
import math

import jax
import jax.numpy as jnp
from jax import lax
from jax.experimental import pallas as pl
from jax.experimental.pallas import tpu as pltpu
from jax.sharding import PartitionSpec as P

MESH = pl.DeviceIdType.MESH
F32 = jnp.float32
BF16 = jnp.bfloat16

NX, NY, NZ, NCORE = 4, 4, 16, 2
NROW, NCOL = 16, 8
CHIPS = NY * NZ

LEV = 10
PLANES = 100
POINTS = 2688
SPANS = 21
SPAN = 128
WAVES = 5
DEGREES = 160
LATS = 128
LINES = 4
TRACER_ROWS = 64
DIFFUSION = 0.07
COUPLE = 0.5

SEG = 256
SEGS = 11
PITCH = 112
PART = 25
PARTS = 4
PACKED = 8


def sincos(turns4):
    quarter = jnp.floor(turns4 + 0.5)
    y = (turns4 - quarter) * (0.5 * math.pi)
    y2 = y * y
    s = y * (1.0 + y2 * (-1.0 / 6 + y2 * (1.0 / 120 + y2 * (-1.0 / 5040 + y2 * (1.0 / 362880)))))
    c = 1.0 + y2 * (
        -0.5 + y2 * (1.0 / 24 + y2 * (-1.0 / 720 + y2 * (1.0 / 40320 + y2 * (-1.0 / 3628800))))
    )
    odd = (quarter == 1.0) | (quarter == 3.0)
    cos_sign = jnp.where((quarter == 1.0) | (quarter == 2.0), -1.0, 1.0)
    sin_sign = jnp.where((quarter == 2.0) | (quarter == 3.0), -1.0, 1.0)
    return cos_sign * jnp.where(odd, s, c), sin_sign * jnp.where(odd, c, s)


def dot_t(a, b):
    return lax.dot_general(a, b, (((1,), (1,)), ((), ())), preferred_element_type=F32)


def kernel(
    phys_hbm,
    poly_hbm,
    s2a_hbm,
    a2s_hbm,
    tracer_ref,
    courant_ref,
    water_ref,
    points_ref,
    air_ref,
    sea_ref,
    spectral_ref,
    tracer_out_ref,
    xv,
    pv,
    s2av,
    a2sv,
    x32,
    flux32,
    flux_got32,
    sst_got32,
    rows32,
    cells32,
    shifted,
    tops,
    bottoms,
    forced,
    table_c,
    table_s,
    waves,
    segments,
    product,
    fourier,
    row0,
    parts,
    packed32,
    out32,
    right_hand,
    got32,
    product2,
    poly_t,
    flux_send,
    flux_got,
    down_send,
    up_send,
    cells_send,
    top1,
    bottom1,
    left1,
    right1,
    down2_send,
    up2_send,
    cells2_send,
    top2,
    bottom2,
    left2,
    right2,
    sst_send,
    sst_got,
    poly_got,
    core_send,
    core_got,
    outbox,
    inbox,
    local_sem,
    flux_ss,
    flux_rs,
    halo_ss,
    halo_rs,
    halo2_ss,
    halo2_rs,
    sst_ss,
    sst_rs,
    poly_ss,
    poly_rs,
    core_ss,
    core_rs,
    all_ss,
    all_rs,
    ring_ss,
    ring_rs,
    ready,
):
    x = lax.axis_index("grp")
    row = lax.axis_index("row")
    col = lax.axis_index("col")
    y = row // 4
    z = lax.rem(row, 4) * 4 + col // 2
    core = lax.rem(col, 2)
    strip = x * NROW + row

    def at(xx, yy, zz, cc):
        return (xx, yy * 4 + zz // 4, lax.rem(zz, 4) * 2 + cc)

    def remote(src, dst, ss, rs, device):
        return pltpu.make_async_remote_copy(
            src_ref=src, dst_ref=dst, send_sem=ss, recv_sem=rs, device_id=device, device_id_type=MESH
        )

    def strip_at(other):
        return (other // NROW, lax.rem(other, NROW), col)

    below = strip_at(lax.rem(strip + 1, NX * NROW))
    above = strip_at(lax.rem(strip + NX * NROW - 1, NX * NROW))
    band = [(x, row, lax.rem(col + i, NCOL)) for i in range(1, NCOL)]
    after = band[0]
    before = band[-1]
    z_ring = [at(x, y, lax.rem(z + i, NZ), core) for i in range(1, NZ)]
    y_ring = [at(x, lax.rem(y + i, NY), z, core) for i in range(1, NY)]
    x_ring = [at(lax.rem(x + i, NX), y, z, core) for i in range(1, NX)]
    sibling = at(x, y, z, 1 - core)

    ins = [
        pltpu.make_async_copy(phys_hbm, xv, local_sem.at[0]),
        pltpu.make_async_copy(poly_hbm, pv, local_sem.at[1]),
        pltpu.make_async_copy(a2s_hbm, a2sv, local_sem.at[2]),
        pltpu.make_async_copy(s2a_hbm, s2av, local_sem.at[3]),
    ]
    for copy in ins:
        copy.start()
    barrier = pltpu.get_barrier_semaphore()
    greeted = band + [below, above, sibling] + x_ring + y_ring + z_ring
    for device in greeted:
        pl.semaphore_signal(barrier, inc=1, device_id=device, device_id_type=MESH)

    own = strip * NCOL + col
    n = points_ref[own]
    lane = lax.broadcasted_iota(jnp.int32, (1, SPAN), 1)

    ins[0].wait()
    x32[...] = xv[0, 0:32, :].astype(F32)
    flux32[...] = jnp.zeros_like(flux32)
    for b in range(SPANS):
        live = lane + b * SPAN < n
        for q in range(2):
            line = x32[(q + 1) * LEV : (q + 1) * LEV + 1, b * SPAN : (b + 1) * SPAN]
            flux32[q * 24 + b : q * 24 + b + 1, :] = jnp.where(live, line, 0.0)
    flux_send[...] = flux32[...].astype(BF16)
    flux_got[pl.ds(col, 1)] = flux_send[...][None]

    wet = water_ref[...].astype(F32)
    for i in range(16):
        cells32[96 + 4 * i : 100 + 4 * i, :] = wet
    cells32[0:64, :] = tracer_ref[...]
    cells32[64:96, :] = courant_ref[32:64, :]
    cells_send[...] = cells32[...].astype(BF16)
    rows32[...] = jnp.zeros_like(rows32)
    rows32[0:16, :] = tracer_ref[pl.ds(3, 16, stride=4), :]
    rows32[16:24, :] = courant_ref[pl.ds(3, 8, stride=4), :]
    rows32[24:25, :] = wet[3:4, :]
    down_send[...] = rows32[...].astype(BF16)
    rows32[0:16, :] = tracer_ref[pl.ds(0, 16, stride=4), :]
    rows32[24:25, :] = wet[0:1, :]
    up_send[...] = rows32[...].astype(BF16)

    pl.semaphore_wait(barrier, len(greeted))
    flux_copies = [
        remote(flux_send, flux_got.at[col], flux_ss.at[i], flux_rs.at[i], device)
        for i, device in enumerate(band)
    ]
    halo_copies = [
        remote(down_send, top1, halo_ss.at[0], halo_rs.at[0], below),
        remote(up_send, bottom1, halo_ss.at[1], halo_rs.at[1], above),
        remote(cells_send, left1, halo_ss.at[2], halo_rs.at[2], after),
        remote(cells_send, right1, halo_ss.at[3], halo_rs.at[3], before),
    ]
    for copy in flux_copies + halo_copies:
        copy.start()
    for device in y_ring:
        pl.semaphore_signal(ready, inc=1, device_id=device, device_id_type=MESH)

    shape = (WAVES, 48, SPAN)
    k_of = lax.broadcasted_iota(jnp.int32, shape, 0)
    p_row = lax.broadcasted_iota(jnp.int32, shape, 1)
    d_of = lax.broadcasted_iota(jnp.int32, shape, 2)
    owner = (d_of & 3) * 32 + ((d_of >> 2) & 15) * 2 + (d_of >> 6)
    orders = owner * WAVES + k_of
    places = jnp.where(
        p_row < 16, p_row, jnp.where(p_row < 32, (p_row - 16) * 16, (p_row - 32) * SEG)
    )
    count = jnp.full(shape, n, jnp.int32).astype(F32)
    inverse = 1.0 / count
    turns = orders.astype(F32) * places.astype(F32)
    phase = turns - jnp.floor(turns * inverse) * count
    phase = jnp.where(phase < 0.0, phase + count, phase)
    phase = jnp.where(phase >= count, phase - count, phase)
    cosine, sine = sincos(phase * (4.0 * inverse))
    table_c[...] = cosine
    table_s[...] = -sine

    def fill_waves(a, _):
        start = pl.multiple_of(a * 16, 16)
        for k in range(WAVES):
            ac = table_c[k, pl.ds(16 + a, 1), :]
            as_ = table_s[k, pl.ds(16 + a, 1), :]
            bc = table_c[k, 0:16, :]
            bs = table_s[k, 0:16, :]
            waves[k, pl.ds(start, 16), 0:SPAN] = (ac * bc - as_ * bs).astype(BF16)
            waves[k, pl.ds(start, 16), SPAN : 2 * SPAN] = (ac * bs + as_ * bc).astype(BF16)
        return 0

    lax.fori_loop(0, 16, fill_waves, 0)

    for i in range(SEGS):
        width = min(SEG, POINTS - i * SEG)
        pos = i * SEG + lax.broadcasted_iota(jnp.int32, (1, width), 1)
        values = xv[0, :, i * SEG : i * SEG + width].astype(F32)
        values = jnp.where(pos < n, values, 0.0).astype(BF16)
        segments[i * PITCH + 96 : (i + 1) * PITCH, :] = jnp.zeros((16, SEG), BF16)
        if width < SEG:
            segments[i * PITCH : (i + 1) * PITCH, width:SEG] = jnp.zeros((PITCH, SEG - width), BF16)
        segments[i * PITCH : i * PITCH + PLANES, 0:width] = values

    ins[1].wait()
    for k in range(WAVES):
        turned = pv[k].astype(F32).T.astype(BF16)
        for g in range(NX):
            poly_t[g, k * DEGREES : (k + 1) * DEGREES, :] = turned[g * DEGREES : (g + 1) * DEGREES]
    poly_got[0] = poly_t[x]
    poly_copies = [
        remote(
            poly_t.at[lax.rem(x + i, NX)],
            poly_got.at[i],
            poly_ss.at[i - 1],
            poly_rs.at[i - 1],
            x_ring[i - 1],
        )
        for i in range(1, NX)
    ]
    for copy in poly_copies:
        copy.start()

    ins[2].wait()
    for copy in flux_copies:
        copy.wait_recv()
    flux_got32[...] = flux_got[...].astype(F32)
    two = lax.broadcasted_iota(jnp.int32, (16, SPAN), 0)
    forced[...] = jnp.zeros_like(forced)
    for line in range(LINES):
        total = jnp.zeros((16, SPAN), F32)
        for k in range(2):
            span = air_ref[0, k, line]
            source = lax.div(span, SPANS)
            block = lax.rem(span, SPANS)
            first = flux_got32[source, pl.ds(block, 1), :]
            second = flux_got32[source, pl.ds(block + 24, 1), :]
            pair = jnp.where(
                two == 0, jnp.broadcast_to(first, (16, SPAN)), jnp.broadcast_to(second, (16, SPAN))
            )
            total = total + dot_t(pair.astype(BF16), a2sv[line, k])
        forced[line : line + 1, :] = COUPLE * total[0:1, :]
        forced[32 + line : 33 + line, :] = COUPLE * total[1:2, :]

    has_top = jnp.where(strip > 0, 1.0, 0.0).astype(F32)
    has_bottom = jnp.where(strip < NX * NROW - 1, 1.0, 0.0).astype(F32)
    has_left = jnp.where(col > 0, 1.0, 0.0).astype(F32)
    has_right = jnp.where(col < NCOL - 1, 1.0, 0.0).astype(F32)
    line_of = lax.broadcasted_iota(jnp.int32, (TRACER_ROWS, SPAN), 0) & 3
    lane_of = lax.broadcasted_iota(jnp.int32, (TRACER_ROWS, SPAN), 1)

    def from_above(value, edge):
        shifted[8:72, :] = value
        tops[pl.ds(0, 16, stride=4), :] = edge
        return jnp.where(line_of == 0, tops[...], shifted[7:71, :])

    def from_below(value, edge):
        shifted[8:72, :] = value
        bottoms[pl.ds(3, 16, stride=4), :] = edge
        return jnp.where(line_of == 3, bottoms[...], shifted[9:73, :])

    def from_left(value, tile):
        return jnp.where(lane_of == 0, pltpu.roll(tile, 1, 1), pltpu.roll(value, 1, 1))

    def from_right(value, tile):
        return jnp.where(
            lane_of == SPAN - 1, pltpu.roll(tile, SPAN - 1, 1), pltpu.roll(value, SPAN - 1, 1)
        )

    def twice(value):
        return jnp.concatenate([value, value], axis=0)

    for copy in halo_copies:
        copy.wait_recv()
    shifted[...] = jnp.zeros_like(shifted)
    tops[...] = jnp.zeros_like(tops)
    bottoms[...] = jnp.zeros_like(bottoms)
    top = top1[...].astype(F32) * has_top
    bottom = bottom1[...].astype(F32) * has_bottom
    left = left1[...].astype(F32) * has_left
    right = right1[...].astype(F32) * has_right
    wet64 = cells32[96:160, :]
    east = twice(courant_ref[0:32, :])
    north = twice(courant_ref[32:64, :])
    east_up = from_above(east, twice(top[16:24, :]))
    north_left = from_left(north, twice(left[64:96, :]))
    pair_up = wet64 * from_above(wet64, jnp.broadcast_to(top[24:25, :], (16, SPAN)))
    pair_down = wet64 * from_below(wet64, jnp.broadcast_to(bottom[24:25, :], (16, SPAN)))
    pair_left = wet64 * from_left(wet64, left[96:160, :])
    pair_right = wet64 * from_right(wet64, right[96:160, :])

    def flow(pair, speed, low, high):
        return pair * (
            jnp.maximum(speed, 0.0) * low
            + jnp.minimum(speed, 0.0) * high
            - DIFFUSION * (high - low)
        )

    def advance(q, edge_top, edge_bottom, tile_left, tile_right):
        spread = (
            flow(pair_down, east, q, from_below(q, edge_bottom))
            - flow(pair_up, east_up, from_above(q, edge_top), q)
            + flow(pair_right, north, q, from_right(q, tile_right))
            - flow(pair_left, north_left, from_left(q, tile_left), q)
        )
        return q + wet64 * (forced[...] - spread)

    state = advance(
        tracer_ref[...], top[0:16, :], bottom[0:16, :], left[0:64, :], right[0:64, :]
    )
    tracer_out_ref[...] = state
    cells2_send[...] = state.astype(BF16)
    down2_send[...] = tracer_out_ref[pl.ds(3, 16, stride=4), :].astype(BF16)
    up2_send[...] = tracer_out_ref[pl.ds(0, 16, stride=4), :].astype(BF16)
    halo2_copies = [
        remote(down2_send, top2, halo2_ss.at[0], halo2_rs.at[0], below),
        remote(up2_send, bottom2, halo2_ss.at[1], halo2_rs.at[1], above),
        remote(cells2_send, left2, halo2_ss.at[2], halo2_rs.at[2], after),
        remote(cells2_send, right2, halo2_ss.at[3], halo2_rs.at[3], before),
    ]
    for copy in halo2_copies:
        copy.start()

    inverse_row = 1.0 / jnp.full((1, SPAN), n, jnp.int32).astype(F32)
    d_row = lax.broadcasted_iota(jnp.int32, (1, SPAN), 1)
    owner_row = (d_row & 3) * 32 + ((d_row >> 2) & 15) * 2 + (d_row >> 6)

    def scale_of(k):
        return jnp.where(2 * (owner_row * WAVES + k) < n, inverse_row, 0.0)

    def transform(k, _):
        product[...] = jnp.dot(segments[...], waves[k], preferred_element_type=F32)
        real = jnp.zeros((PITCH, SPAN), F32)
        imag = jnp.zeros((PITCH, SPAN), F32)
        for i in range(SEGS):
            wc = table_c[k, 32 + i : 33 + i, :]
            ws = table_s[k, 32 + i : 33 + i, :]
            yc = product[i * PITCH : (i + 1) * PITCH, 0:SPAN]
            ys = product[i * PITCH : (i + 1) * PITCH, SPAN : 2 * SPAN]
            real = real + (yc * wc - ys * ws)
            imag = imag + (yc * ws + ys * wc)
        scale = scale_of(k)
        fourier[k, 0] = real * scale
        fourier[k, 1] = imag * scale
        return 0

    lax.fori_loop(0, 3, transform, 0)

    for copy in halo2_copies:
        copy.wait_recv()
    state = advance(
        tracer_out_ref[...],
        top2[...].astype(F32) * has_top,
        bottom2[...].astype(F32) * has_bottom,
        left2[...].astype(F32) * has_left,
        right2[...].astype(F32) * has_right,
    )
    tracer_out_ref[...] = state
    sst_send[...] = state[0:16, :].astype(BF16)
    sst_got[pl.ds(col, 1)] = sst_send[...][None]
    sst_copies = [
        remote(sst_send, sst_got.at[col], sst_ss.at[i], sst_rs.at[i], device)
        for i, device in enumerate(band)
    ]
    for copy in sst_copies:
        copy.start()

    lax.fori_loop(3, WAVES, transform, 0)

    ins[3].wait()
    for copy in sst_copies:
        copy.wait_recv()
    sst_got32[...] = sst_got[...].astype(F32)
    row0[...] = jnp.zeros_like(row0)
    for b in range(SPANS):
        span = sea_ref[0, b]
        source = lax.div(span, LINES)
        line = lax.rem(span, LINES)
        warmth = jnp.broadcast_to(sst_got32[source, pl.ds(line, 1), :], (16, SPAN))
        sampled = dot_t(warmth.astype(BF16), s2av[0, b])[0:1, :]
        plane = x32[0:1, b * SPAN : (b + 1) * SPAN] + sampled
        plane = jnp.where(lane + b * SPAN < n, plane, 0.0)
        half = (b % 2) * SPAN
        row0[b // 2 : b // 2 + 1, half : half + SPAN] = plane
    surface = row0[...].astype(BF16)
    for k in range(WAVES):
        part = jnp.dot(surface, waves[k], preferred_element_type=F32)
        wc = table_c[k, 32:48, :]
        ws = table_s[k, 32:48, :]
        yc = part[:, 0:SPAN]
        ys = part[:, SPAN : 2 * SPAN]
        scale = scale_of(k)
        fourier[k, 0, 0:1, :] = jnp.sum(yc * wc - ys * ws, axis=0, keepdims=True) * scale
        fourier[k, 1, 0:1, :] = jnp.sum(yc * ws + ys * wc, axis=0, keepdims=True) * scale

    for c in range(2):
        for q in range(PARTS):
            r = c * PARTS + q
            parts[r, 120:128, :] = jnp.zeros((8, SPAN), F32)
            for k in range(WAVES):
                parts[r, k * PART : (k + 1) * PART, :] = fourier[
                    k, c, q * PART : (q + 1) * PART, :
                ]
            packed32[pl.ds(r, LATS, stride=PACKED), :] = parts[r].T

    half_rows = CHIPS * PACKED
    core_send[...] = packed32[pl.ds(pl.multiple_of((1 - core) * half_rows, 8), half_rows), :].astype(
        BF16
    )
    core_copy = remote(core_send, core_got, core_ss, core_rs, sibling)
    core_copy.start()
    mine = packed32[pl.ds(pl.multiple_of(core * half_rows, 8), half_rows), :].reshape(
        CHIPS, PACKED, SPAN
    )
    core_copy.wait_recv()
    theirs = core_got[...].astype(F32).reshape(CHIPS, PACKED, SPAN)
    is_first = core == 0
    out32[:, 0:PACKED, :] = jnp.where(is_first, mine, theirs)
    out32[:, PACKED : 2 * PACKED, :] = jnp.where(is_first, theirs, mine)
    outbox[...] = out32[...].astype(BF16)
    pl.semaphore_wait(ready, NY - 1)
    me = y * NZ + z

    def post(i, _):
        zz = lax.rem(z + i, NZ)
        for j in range(NY):
            yy = lax.rem(y + j, NY)
            remote(
                outbox.at[zz * NY + yy], inbox.at[0, me], all_ss, all_rs, at(x, yy, zz, core)
            ).start()
        return 0

    lax.fori_loop(1, NZ, post, 0)
    for j in range(1, NY):
        yy = lax.rem(y + j, NY)
        remote(outbox.at[z * NY + yy], inbox.at[0, me], all_ss, all_rs, at(x, yy, z, core)).start()
    inbox[0, pl.ds(me, 1)] = outbox[pl.ds(z * NY + y, 1)]

    for copy in flux_copies + halo_copies + halo2_copies + sst_copies + poly_copies:
        copy.wait_send()
    core_copy.wait_send()
    for copy in poly_copies:
        copy.wait_recv()
    degrees = jnp.concatenate([poly_got[i] for i in range(NX)], axis=1)

    every = remote(
        outbox.at[pl.ds(0, CHIPS - 1)],
        inbox.at[0, pl.ds(0, CHIPS - 1)],
        all_ss,
        all_rs,
        sibling,
    )
    every.wait_recv()
    next_x = x_ring[0]
    last_x = x_ring[-1]
    ring_right = remote(inbox.at[0], inbox.at[1], ring_ss.at[0], ring_rs.at[0], next_x)
    ring_left = remote(inbox.at[0], inbox.at[3], ring_ss.at[1], ring_rs.at[1], last_x)
    ring_right.start()
    ring_left.start()

    def unpack(slot):
        got32[...] = inbox[slot].astype(F32).reshape(CHIPS * 2 * PACKED, SPAN)
        for r in range(PACKED):
            right_hand[slot * LATS : (slot + 1) * LATS, r * SPAN : (r + 1) * SPAN] = got32[
                pl.ds(r, LATS, stride=PACKED), :
            ].astype(BF16)

    unpack(0)
    middle = CHIPS // 2
    ring_right.wait_recv()
    on_right = remote(
        inbox.at[1, pl.ds(0, middle)],
        inbox.at[2, pl.ds(0, middle)],
        ring_ss.at[2],
        ring_rs.at[2],
        next_x,
    )
    on_right.start()
    ring_left.wait_recv()
    on_left = remote(
        inbox.at[3, pl.ds(middle, middle)],
        inbox.at[2, pl.ds(middle, middle)],
        ring_ss.at[3],
        ring_rs.at[3],
        last_x,
    )
    on_left.start()
    unpack(1)
    unpack(3)
    on_right.wait_recv()
    on_left.wait_recv()
    unpack(2)

    lanes = lax.broadcasted_iota(jnp.int32, (DEGREES, SPAN), 1)
    for c in range(2):
        for pair in range(2):
            start = (c * PARTS + pair * 2) * SPAN
            product2[:, pair * 2 * SPAN : (pair + 1) * 2 * SPAN] = jnp.dot(
                degrees, right_hand[:, start : start + 2 * SPAN], preferred_element_type=F32
            )
        for k in range(WAVES):
            total = jnp.zeros((DEGREES, SPAN), F32)
            for q in range(PARTS):
                block = product2[k * DEGREES : (k + 1) * DEGREES, q * SPAN : (q + 1) * SPAN]
                turn = (PART * (q - k)) % SPAN
                if turn:
                    block = pltpu.roll(block, turn, 1)
                keep = (lanes >= q * PART) & (lanes < (q + 1) * PART)
                total = jnp.where(keep, block, total)
            spectral_ref[c, k] = total[:, 0:PLANES].astype(BF16)

    every.wait_send()
    for copy in (ring_right, ring_left, on_right, on_left):
        copy.wait_send()


def local(
    physical_values,
    samples_per_parallel,
    associated_polynomials,
    heat_salt_anomalies,
    courant_numbers,
    water_indicator,
    air_to_sea_coefficients,
    air_partner_span,
    sea_to_air_coefficients,
    sea_partner_span,
):
    vmem = pl.BlockSpec(memory_space=pltpu.VMEM)
    smem = pl.BlockSpec(memory_space=pltpu.SMEM)
    anywhere = pl.BlockSpec(memory_space=pl.ANY)
    dma = pltpu.SemaphoreType.DMA
    scratch = [
        pltpu.VMEM((1, PLANES, POINTS), BF16),
        pltpu.VMEM((WAVES, LATS, NX * DEGREES), BF16),
        pltpu.VMEM((1, SPANS, SPAN, SPAN), BF16),
        pltpu.VMEM((LINES, 2, SPAN, SPAN), BF16),
        pltpu.VMEM((32, POINTS), F32),
        pltpu.VMEM((48, SPAN), F32),
        pltpu.VMEM((NCOL, 48, SPAN), F32),
        pltpu.VMEM((NCOL, 16, SPAN), F32),
        pltpu.VMEM((32, SPAN), F32),
        pltpu.VMEM((160, SPAN), F32),
        pltpu.VMEM((80, SPAN), F32),
        pltpu.VMEM((TRACER_ROWS, SPAN), F32),
        pltpu.VMEM((TRACER_ROWS, SPAN), F32),
        pltpu.VMEM((TRACER_ROWS, SPAN), F32),
        pltpu.VMEM((WAVES, 48, SPAN), F32),
        pltpu.VMEM((WAVES, 48, SPAN), F32),
        pltpu.VMEM((WAVES, SEG, 2 * SPAN), BF16),
        pltpu.VMEM((SEGS * PITCH, SEG), BF16),
        pltpu.VMEM((SEGS * PITCH, 2 * SPAN), F32),
        pltpu.VMEM((WAVES, 2, PITCH, SPAN), F32),
        pltpu.VMEM((16, SEG), F32),
        pltpu.VMEM((PACKED, SPAN, SPAN), F32),
        pltpu.VMEM((LATS * PACKED, SPAN), F32),
        pltpu.VMEM((CHIPS, 2 * PACKED, SPAN), F32),
        pltpu.VMEM((NX * LATS, PACKED * SPAN), BF16),
        pltpu.VMEM((LATS * PACKED, SPAN), F32),
        pltpu.VMEM((WAVES * DEGREES, PARTS * SPAN), F32),
        pltpu.VMEM((NX, WAVES * DEGREES, LATS), BF16),
        pltpu.VMEM((48, SPAN), BF16),
        pltpu.VMEM((NCOL, 48, SPAN), BF16),
        pltpu.VMEM((32, SPAN), BF16),
        pltpu.VMEM((32, SPAN), BF16),
        pltpu.VMEM((160, SPAN), BF16),
        pltpu.VMEM((32, SPAN), BF16),
        pltpu.VMEM((32, SPAN), BF16),
        pltpu.VMEM((160, SPAN), BF16),
        pltpu.VMEM((160, SPAN), BF16),
        pltpu.VMEM((16, SPAN), BF16),
        pltpu.VMEM((16, SPAN), BF16),
        pltpu.VMEM((64, SPAN), BF16),
        pltpu.VMEM((16, SPAN), BF16),
        pltpu.VMEM((16, SPAN), BF16),
        pltpu.VMEM((64, SPAN), BF16),
        pltpu.VMEM((64, SPAN), BF16),
        pltpu.VMEM((16, SPAN), BF16),
        pltpu.VMEM((NCOL, 16, SPAN), BF16),
        pltpu.VMEM((NX, WAVES * DEGREES, LATS), BF16),
        pltpu.VMEM((CHIPS * PACKED, SPAN), BF16),
        pltpu.VMEM((CHIPS * PACKED, SPAN), BF16),
        pltpu.VMEM((CHIPS, 2 * PACKED, SPAN), BF16),
        pltpu.VMEM((NX, CHIPS, 2 * PACKED, SPAN), BF16),
        dma((4,)),
        dma((NCOL - 1,)),
        dma((NCOL - 1,)),
        dma((4,)),
        dma((4,)),
        dma((4,)),
        dma((4,)),
        dma((NCOL - 1,)),
        dma((NCOL - 1,)),
        dma((NX - 1,)),
        dma((NX - 1,)),
        dma,
        dma,
        dma,
        dma,
        dma((4,)),
        dma((4,)),
        pltpu.SemaphoreType.REGULAR,
    ]
    spectral, tracers = pl.pallas_call(
        kernel,
        out_shape=(
            jax.ShapeDtypeStruct((2, WAVES, DEGREES, PLANES), BF16),
            jax.ShapeDtypeStruct((TRACER_ROWS, SPAN), F32),
        ),
        in_specs=[anywhere] * 4 + [vmem] * 3 + [smem] * 3,
        out_specs=(vmem, vmem),
        scratch_shapes=scratch,
        compiler_params=pltpu.CompilerParams(
            collective_id=0, has_side_effects=True, vmem_limit_bytes=48 * 2**20
        ),
        cost_estimate=pl.CostEstimate(
            flops=1_000_000_000, bytes_accessed=3_000_000, transcendentals=0
        ),
    )(
        physical_values,
        associated_polynomials,
        sea_to_air_coefficients,
        air_to_sea_coefficients,
        heat_salt_anomalies.reshape(TRACER_ROWS, SPAN),
        courant_numbers.reshape(TRACER_ROWS, SPAN),
        water_indicator,
        samples_per_parallel,
        jnp.transpose(air_partner_span, (1, 2, 0)),
        sea_partner_span,
    )
    return spectral.transpose(3, 0, 1, 2), tracers.reshape(2, 8, LINES, SPAN)


def solution(mesh):
    placed = (
        P(("grp", "row", "col"), None, None),
        P(),
        P(("row", "col"), "grp", None),
        P(None, None, ("grp", "row"), "col"),
        P(None, None, ("grp", "row"), "col"),
        P(("grp", "row"), "col"),
        P(("grp", "row"), None, "col", None),
        P(("grp", "row"), "col", None),
        P(("grp", "row", "col"), None, None, None),
        P(("grp", "row", "col"), None),
    )
    return jax.shard_map(
        local,
        mesh=mesh,
        in_specs=placed,
        out_specs=(P(None, None, ("row", "col"), "grp"), P(None, None, ("grp", "row"), "col")),
        check_vma=False,
    )
```

```python
import math

import jax
import jax.numpy as jnp
from jax import lax
from jax.experimental import pallas as pl
from jax.experimental.pallas import tpu as pltpu
from jax.sharding import PartitionSpec as P

MESH = pl.DeviceIdType.MESH
F32 = jnp.float32
BF16 = jnp.bfloat16

NX, NY, NZ, NCORE = 4, 4, 16, 2
NROW, NCOL = 16, 8
CHIPS = NY * NZ

LEV = 10
PLANES = 100
POINTS = 2688
SPANS = 21
SPAN = 128
WAVES = 5
DEGREES = 160
LATS = 128
LINES = 4
TRACER_ROWS = 64
DIFFUSION = 0.07
COUPLE = 0.5

SEG = 256
SEGS = 11
PITCH = 112
PART = 25
PARTS = 4
PACKED = 8


def sincos(turns4):
    quarter = jnp.floor(turns4 + 0.5)
    y = (turns4 - quarter) * (0.5 * math.pi)
    y2 = y * y
    s = y * (1.0 + y2 * (-1.0 / 6 + y2 * (1.0 / 120 + y2 * (-1.0 / 5040 + y2 * (1.0 / 362880)))))
    c = 1.0 + y2 * (
        -0.5 + y2 * (1.0 / 24 + y2 * (-1.0 / 720 + y2 * (1.0 / 40320 + y2 * (-1.0 / 3628800))))
    )
    odd = (quarter == 1.0) | (quarter == 3.0)
    cos_sign = jnp.where((quarter == 1.0) | (quarter == 2.0), -1.0, 1.0)
    sin_sign = jnp.where((quarter == 2.0) | (quarter == 3.0), -1.0, 1.0)
    return cos_sign * jnp.where(odd, s, c), sin_sign * jnp.where(odd, c, s)


def dot_t(a, b):
    return lax.dot_general(a, b, (((1,), (1,)), ((), ())), preferred_element_type=F32)


def kernel(
    phys_hbm,
    poly_hbm,
    s2a_hbm,
    a2s_hbm,
    tracer_ref,
    courant_ref,
    water_ref,
    points_ref,
    air_ref,
    sea_ref,
    spectral_ref,
    tracer_out_ref,
    xv,
    pv,
    s2av,
    a2sv,
    x32,
    flux32,
    flux_got32,
    sst_got32,
    rows32,
    cells32,
    shifted,
    tops,
    bottoms,
    forced,
    table_c,
    table_s,
    waves,
    segments,
    product,
    fourier,
    row0,
    parts,
    packed32,
    out32,
    right_hand,
    got32,
    product2,
    product0,
    plane32,
    select_z,
    select_y,
    poly_t,
    flux_send,
    flux_got,
    down_send,
    up_send,
    cells_send,
    top1,
    bottom1,
    left1,
    right1,
    down2_send,
    up2_send,
    cells2_send,
    top2,
    bottom2,
    left2,
    right2,
    sst_send,
    sst_got,
    poly_got,
    core_send,
    core_got,
    outbox,
    inbox,
    plane_send,
    plane_got,
    mixed_send,
    mixed_got,
    local_sem,
    flux_ss,
    flux_rs,
    halo_ss,
    halo_rs,
    halo2_ss,
    halo2_rs,
    sst_ss,
    sst_rs,
    poly_ss,
    poly_rs,
    core_ss,
    core_rs,
    all_ss,
    all_rs,
    ring_ss,
    ring_rs,
    plane_ss,
    plane_rs,
    mixed_ss,
    mixed_rs,
    ready,
    ready2,
):
    x = lax.axis_index("grp")
    row = lax.axis_index("row")
    col = lax.axis_index("col")
    y = row // 4
    z = lax.rem(row, 4) * 4 + col // 2
    core = lax.rem(col, 2)
    strip = x * NROW + row

    def at(xx, yy, zz, cc):
        return (xx, yy * 4 + zz // 4, lax.rem(zz, 4) * 2 + cc)

    def remote(src, dst, ss, rs, device):
        return pltpu.make_async_remote_copy(
            src_ref=src, dst_ref=dst, send_sem=ss, recv_sem=rs, device_id=device, device_id_type=MESH
        )

    def strip_at(other):
        return (other // NROW, lax.rem(other, NROW), col)

    below = strip_at(lax.rem(strip + 1, NX * NROW))
    above = strip_at(lax.rem(strip + NX * NROW - 1, NX * NROW))
    band = [(x, row, lax.rem(col + i, NCOL)) for i in range(1, NCOL)]
    after = band[0]
    before = band[-1]
    z_ring = [at(x, y, lax.rem(z + i, NZ), core) for i in range(1, NZ)]
    y_ring = [at(x, lax.rem(y + i, NY), z, core) for i in range(1, NY)]
    x_ring = [at(lax.rem(x + i, NX), y, z, core) for i in range(1, NX)]
    sibling = at(x, y, z, 1 - core)

    ins = [
        pltpu.make_async_copy(phys_hbm, xv, local_sem.at[0]),
        pltpu.make_async_copy(poly_hbm, pv, local_sem.at[1]),
        pltpu.make_async_copy(a2s_hbm, a2sv, local_sem.at[2]),
        pltpu.make_async_copy(s2a_hbm, s2av, local_sem.at[3]),
    ]
    for copy in ins:
        copy.start()
    barrier = pltpu.get_barrier_semaphore()
    greeted = band + [below, above, sibling] + x_ring + y_ring + z_ring
    for device in greeted:
        pl.semaphore_signal(barrier, inc=1, device_id=device, device_id_type=MESH)

    own = strip * NCOL + col
    n = points_ref[own]
    lane = lax.broadcasted_iota(jnp.int32, (1, SPAN), 1)

    ins[0].wait()
    x32[...] = xv[0, 0:32, :].astype(F32)
    flux32[...] = jnp.zeros_like(flux32)
    for b in range(SPANS):
        live = lane + b * SPAN < n
        for q in range(2):
            line = x32[(q + 1) * LEV : (q + 1) * LEV + 1, b * SPAN : (b + 1) * SPAN]
            flux32[q * 24 + b : q * 24 + b + 1, :] = jnp.where(live, line, 0.0)
    flux_send[...] = flux32[...].astype(BF16)
    flux_got[pl.ds(col, 1)] = flux_send[...][None]

    wet = water_ref[...].astype(F32)
    for i in range(16):
        cells32[96 + 4 * i : 100 + 4 * i, :] = wet
    cells32[0:64, :] = tracer_ref[...]
    cells32[64:96, :] = courant_ref[32:64, :]
    cells_send[...] = cells32[...].astype(BF16)
    rows32[...] = jnp.zeros_like(rows32)
    rows32[0:16, :] = tracer_ref[pl.ds(3, 16, stride=4), :]
    rows32[16:24, :] = courant_ref[pl.ds(3, 8, stride=4), :]
    rows32[24:25, :] = wet[3:4, :]
    down_send[...] = rows32[...].astype(BF16)
    rows32[0:16, :] = tracer_ref[pl.ds(0, 16, stride=4), :]
    rows32[24:25, :] = wet[0:1, :]
    up_send[...] = rows32[...].astype(BF16)

    pl.semaphore_wait(barrier, len(greeted))
    flux_copies = [
        remote(flux_send, flux_got.at[col], flux_ss.at[i], flux_rs.at[i], device)
        for i, device in enumerate(band)
    ]
    halo_copies = [
        remote(down_send, top1, halo_ss.at[0], halo_rs.at[0], below),
        remote(up_send, bottom1, halo_ss.at[1], halo_rs.at[1], above),
        remote(cells_send, left1, halo_ss.at[2], halo_rs.at[2], after),
        remote(cells_send, right1, halo_ss.at[3], halo_rs.at[3], before),
    ]
    for copy in flux_copies + halo_copies:
        copy.start()
    for device in y_ring:
        pl.semaphore_signal(ready, inc=1, device_id=device, device_id_type=MESH)

    shape = (WAVES, 48, SPAN)
    k_of = lax.broadcasted_iota(jnp.int32, shape, 0)
    p_row = lax.broadcasted_iota(jnp.int32, shape, 1)
    d_of = lax.broadcasted_iota(jnp.int32, shape, 2)
    owner = (d_of & 3) * 32 + ((d_of >> 2) & 15) * 2 + (d_of >> 6)
    orders = owner * WAVES + k_of
    places = jnp.where(
        p_row < 16, p_row, jnp.where(p_row < 32, (p_row - 16) * 16, (p_row - 32) * SEG)
    )
    count = jnp.full(shape, n, jnp.int32).astype(F32)
    inverse = 1.0 / count
    turns = orders.astype(F32) * places.astype(F32)
    phase = turns - jnp.floor(turns * inverse) * count
    phase = jnp.where(phase < 0.0, phase + count, phase)
    phase = jnp.where(phase >= count, phase - count, phase)
    cosine, sine = sincos(phase * (4.0 * inverse))
    table_c[...] = cosine
    table_s[...] = -sine

    def fill_waves(a, _):
        start = pl.multiple_of(a * 16, 16)
        for k in range(WAVES):
            ac = table_c[k, pl.ds(16 + a, 1), :]
            as_ = table_s[k, pl.ds(16 + a, 1), :]
            bc = table_c[k, 0:16, :]
            bs = table_s[k, 0:16, :]
            waves[k, pl.ds(start, 16), 0:SPAN] = (ac * bc - as_ * bs).astype(BF16)
            waves[k, pl.ds(start, 16), SPAN : 2 * SPAN] = (ac * bs + as_ * bc).astype(BF16)
        return 0

    lax.fori_loop(0, 16, fill_waves, 0)

    for i in range(SEGS):
        width = min(SEG, POINTS - i * SEG)
        pos = i * SEG + lax.broadcasted_iota(jnp.int32, (1, width), 1)
        values = xv[0, :, i * SEG : i * SEG + width].astype(F32)
        values = jnp.where(pos < n, values, 0.0).astype(BF16)
        segments[i * PITCH + 96 : (i + 1) * PITCH, :] = jnp.zeros((16, SEG), BF16)
        if width < SEG:
            segments[i * PITCH : (i + 1) * PITCH, width:SEG] = jnp.zeros((PITCH, SEG - width), BF16)
        segments[i * PITCH : i * PITCH + PLANES, 0:width] = values

    inverse_row = 1.0 / jnp.full((1, SPAN), n, jnp.int32).astype(F32)
    d_row = lax.broadcasted_iota(jnp.int32, (1, SPAN), 1)
    owner_row = (d_row & 3) * 32 + ((d_row >> 2) & 15) * 2 + (d_row >> 6)

    def scale_of(k):
        return jnp.where(2 * (owner_row * WAVES + k) < n, inverse_row, 0.0)

    def transform(k, _):
        product[...] = jnp.dot(segments[...], waves[k], preferred_element_type=F32)
        real = jnp.zeros((PITCH, SPAN), F32)
        imag = jnp.zeros((PITCH, SPAN), F32)
        for i in range(SEGS):
            wc = table_c[k, 32 + i : 33 + i, :]
            ws = table_s[k, 32 + i : 33 + i, :]
            yc = product[i * PITCH : (i + 1) * PITCH, 0:SPAN]
            ys = product[i * PITCH : (i + 1) * PITCH, SPAN : 2 * SPAN]
            real = real + (yc * wc - ys * ws)
            imag = imag + (yc * ws + ys * wc)
        scale = scale_of(k)
        fourier[k, 0] = real * scale
        fourier[k, 1] = imag * scale
        return 0

    lax.fori_loop(0, WAVES, transform, 0)

    for c in range(2):
        for q in range(PARTS):
            r = c * PARTS + q
            parts[r, 120:128, :] = jnp.zeros((8, SPAN), F32)
            for k in range(WAVES):
                parts[r, k * PART : (k + 1) * PART, :] = fourier[
                    k, c, q * PART : (q + 1) * PART, :
                ]
            packed32[pl.ds(r, LATS, stride=PACKED), :] = parts[r].T

    half_rows = CHIPS * PACKED
    core_send[...] = packed32[pl.ds(pl.multiple_of((1 - core) * half_rows, 8), half_rows), :].astype(
        BF16
    )
    core_copy = remote(core_send, core_got, core_ss, core_rs, sibling)
    core_copy.start()
    mine = packed32[pl.ds(pl.multiple_of(core * half_rows, 8), half_rows), :].reshape(
        CHIPS, PACKED, SPAN
    )
    ins[2].wait()
    for copy in flux_copies:
        copy.wait_recv()
    flux_got32[...] = flux_got[...].astype(F32)
    two = lax.broadcasted_iota(jnp.int32, (16, SPAN), 0)
    forced[...] = jnp.zeros_like(forced)
    for line in range(LINES):
        total = jnp.zeros((16, SPAN), F32)
        for k in range(2):
            span = air_ref[0, k, line]
            source = lax.div(span, SPANS)
            block = lax.rem(span, SPANS)
            first = flux_got32[source, pl.ds(block, 1), :]
            second = flux_got32[source, pl.ds(block + 24, 1), :]
            pair = jnp.where(
                two == 0, jnp.broadcast_to(first, (16, SPAN)), jnp.broadcast_to(second, (16, SPAN))
            )
            total = total + dot_t(pair.astype(BF16), a2sv[line, k])
        forced[line : line + 1, :] = COUPLE * total[0:1, :]
        forced[32 + line : 33 + line, :] = COUPLE * total[1:2, :]

    has_top = jnp.where(strip > 0, 1.0, 0.0).astype(F32)
    has_bottom = jnp.where(strip < NX * NROW - 1, 1.0, 0.0).astype(F32)
    has_left = jnp.where(col > 0, 1.0, 0.0).astype(F32)
    has_right = jnp.where(col < NCOL - 1, 1.0, 0.0).astype(F32)
    line_of = lax.broadcasted_iota(jnp.int32, (TRACER_ROWS, SPAN), 0) & 3
    lane_of = lax.broadcasted_iota(jnp.int32, (TRACER_ROWS, SPAN), 1)

    def from_above(value, edge):
        shifted[8:72, :] = value
        tops[pl.ds(0, 16, stride=4), :] = edge
        return jnp.where(line_of == 0, tops[...], shifted[7:71, :])

    def from_below(value, edge):
        shifted[8:72, :] = value
        bottoms[pl.ds(3, 16, stride=4), :] = edge
        return jnp.where(line_of == 3, bottoms[...], shifted[9:73, :])

    def from_left(value, tile):
        return jnp.where(lane_of == 0, pltpu.roll(tile, 1, 1), pltpu.roll(value, 1, 1))

    def from_right(value, tile):
        return jnp.where(
            lane_of == SPAN - 1, pltpu.roll(tile, SPAN - 1, 1), pltpu.roll(value, SPAN - 1, 1)
        )

    def twice(value):
        return jnp.concatenate([value, value], axis=0)

    for copy in halo_copies:
        copy.wait_recv()
    shifted[...] = jnp.zeros_like(shifted)
    tops[...] = jnp.zeros_like(tops)
    bottoms[...] = jnp.zeros_like(bottoms)
    top = top1[...].astype(F32) * has_top
    bottom = bottom1[...].astype(F32) * has_bottom
    left = left1[...].astype(F32) * has_left
    right = right1[...].astype(F32) * has_right
    wet64 = cells32[96:160, :]
    east = twice(courant_ref[0:32, :])
    north = twice(courant_ref[32:64, :])
    east_up = from_above(east, twice(top[16:24, :]))
    north_left = from_left(north, twice(left[64:96, :]))
    pair_up = wet64 * from_above(wet64, jnp.broadcast_to(top[24:25, :], (16, SPAN)))
    pair_down = wet64 * from_below(wet64, jnp.broadcast_to(bottom[24:25, :], (16, SPAN)))
    pair_left = wet64 * from_left(wet64, left[96:160, :])
    pair_right = wet64 * from_right(wet64, right[96:160, :])

    def flow(pair, speed, low, high):
        return pair * (
            jnp.maximum(speed, 0.0) * low
            + jnp.minimum(speed, 0.0) * high
            - DIFFUSION * (high - low)
        )

    def advance(q, edge_top, edge_bottom, tile_left, tile_right):
        spread = (
            flow(pair_down, east, q, from_below(q, edge_bottom))
            - flow(pair_up, east_up, from_above(q, edge_top), q)
            + flow(pair_right, north, q, from_right(q, tile_right))
            - flow(pair_left, north_left, from_left(q, tile_left), q)
        )
        return q + wet64 * (forced[...] - spread)

    state = advance(
        tracer_ref[...], top[0:16, :], bottom[0:16, :], left[0:64, :], right[0:64, :]
    )
    tracer_out_ref[...] = state
    cells2_send[...] = state.astype(BF16)
    down2_send[...] = tracer_out_ref[pl.ds(3, 16, stride=4), :].astype(BF16)
    up2_send[...] = tracer_out_ref[pl.ds(0, 16, stride=4), :].astype(BF16)
    halo2_copies = [
        remote(down2_send, top2, halo2_ss.at[0], halo2_rs.at[0], below),
        remote(up2_send, bottom2, halo2_ss.at[1], halo2_rs.at[1], above),
        remote(cells2_send, left2, halo2_ss.at[2], halo2_rs.at[2], after),
        remote(cells2_send, right2, halo2_ss.at[3], halo2_rs.at[3], before),
    ]
    for copy in halo2_copies:
        copy.start()

    core_copy.wait_recv()
    theirs = core_got[...].astype(F32).reshape(CHIPS, PACKED, SPAN)
    is_first = core == 0
    out32[:, 0:PACKED, :] = jnp.where(is_first, mine, theirs)
    out32[:, PACKED : 2 * PACKED, :] = jnp.where(is_first, theirs, mine)
    outbox[...] = out32[...].astype(BF16)
    pl.semaphore_wait(ready, NY - 1)
    for device in x_ring:
        pl.semaphore_signal(ready2, inc=1, device_id=device, device_id_type=MESH)

    def post(i, _):
        zz = lax.rem(z + i, NZ)
        for j in range(NY):
            yy = lax.rem(y + j, NY)
            remote(
                outbox.at[zz * NY + yy],
                inbox.at[0, y, z],
                all_ss,
                all_rs.at[j],
                at(x, yy, zz, core),
            ).start()
        return 0

    lax.fori_loop(1, NZ, post, 0)
    for j in range(1, NY):
        yy = lax.rem(y + j, NY)
        remote(
            outbox.at[z * NY + yy], inbox.at[0, y, z], all_ss, all_rs.at[j], at(x, yy, z, core)
        ).start()
    inbox[0, pl.ds(y, 1), pl.ds(z, 1)] = outbox[pl.ds(z * NY + y, 1)][None]

    ins[1].wait()
    for k in range(WAVES):
        turned = pv[k].astype(F32).T.astype(BF16)
        for g in range(NX):
            poly_t[g, k * DEGREES : (k + 1) * DEGREES, :] = turned[g * DEGREES : (g + 1) * DEGREES]
    poly_got[0] = poly_t[x]
    poly_copies = [
        remote(
            poly_t.at[lax.rem(x + i, NX)],
            poly_got.at[i],
            poly_ss.at[i - 1],
            poly_rs.at[i - 1],
            x_ring[i - 1],
        )
        for i in range(1, NX)
    ]
    for copy in poly_copies:
        copy.start()

    rows_a = lax.broadcasted_iota(jnp.int32, (NZ * SPAN, SPAN), 0)
    lanes_a = lax.broadcasted_iota(jnp.int32, (NZ * SPAN, SPAN), 1)
    wanted = ((lanes_a >> 2) & 1) * CHIPS + z * NY + (lanes_a & 3)
    chosen = ((rows_a >> 7) == (lanes_a >> 3)) & ((rows_a & 127) == wanted)
    select_z[...] = jnp.where(chosen, 1.0, 0.0).astype(BF16)
    rows_b = lax.broadcasted_iota(jnp.int32, (8 * SPAN, SPAN), 0)
    lanes_b = lax.broadcasted_iota(jnp.int32, (8 * SPAN, SPAN), 1)
    lane_in = rows_b & 127
    wanted = (rows_b >> 8) * 32 + (lane_in >> 3) * 2 + ((rows_b >> 7) & 1)
    chosen = ((lane_in & 7) == core * 4 + y) & (lanes_b == wanted)
    select_y[...] = jnp.where(chosen, 1.0, 0.0).astype(BF16)

    for copy in halo2_copies:
        copy.wait_recv()
    state = advance(
        tracer_out_ref[...],
        top2[...].astype(F32) * has_top,
        bottom2[...].astype(F32) * has_bottom,
        left2[...].astype(F32) * has_left,
        right2[...].astype(F32) * has_right,
    )
    tracer_out_ref[...] = state
    sst_send[...] = state[0:16, :].astype(BF16)
    sst_got[pl.ds(col, 1)] = sst_send[...][None]
    sst_copies = [
        remote(sst_send, sst_got.at[col], sst_ss.at[i], sst_rs.at[i], device)
        for i, device in enumerate(band)
    ]
    for copy in sst_copies:
        copy.start()

    ins[3].wait()
    for copy in sst_copies:
        copy.wait_recv()
    sst_got32[...] = sst_got[...].astype(F32)
    row0[...] = jnp.zeros_like(row0)
    for b in range(SPANS):
        span = sea_ref[0, b]
        source = lax.div(span, LINES)
        line = lax.rem(span, LINES)
        warmth = jnp.broadcast_to(sst_got32[source, pl.ds(line, 1), :], (16, SPAN))
        sampled = dot_t(warmth.astype(BF16), s2av[0, b])[0:1, :]
        plane = x32[0:1, b * SPAN : (b + 1) * SPAN] + sampled
        plane = jnp.where(lane + b * SPAN < n, plane, 0.0)
        half = (b % 2) * SPAN
        row0[b // 2 : b // 2 + 1, half : half + SPAN] = plane
    surface = row0[...].astype(BF16)
    plane32[...] = jnp.zeros_like(plane32)
    for k in range(WAVES):
        part = jnp.dot(surface, waves[k], preferred_element_type=F32)
        wc = table_c[k, 32:48, :]
        ws = table_s[k, 32:48, :]
        yc = part[:, 0:SPAN]
        ys = part[:, SPAN : 2 * SPAN]
        scale = scale_of(k)
        plane32[2 * k : 2 * k + 1, :] = jnp.sum(yc * wc - ys * ws, axis=0, keepdims=True) * scale
        plane32[2 * k + 1 : 2 * k + 2, :] = (
            jnp.sum(yc * ws + ys * wc, axis=0, keepdims=True) * scale
        )

    plane_send[...] = plane32[...].astype(BF16)
    plane_got[pl.ds(z, 1)] = plane_send[...][None]
    for device in z_ring:
        remote(plane_send, plane_got.at[z], plane_ss, plane_rs, device).start()

    next_x = x_ring[0]
    last_x = x_ring[-1]
    ring_right = []
    ring_left = []
    ring_on = []

    def circulate(j):
        count = NZ - 1 if j == 0 else NZ
        arrived = remote(
            outbox.at[pl.ds(0, count)],
            inbox.at[0, 0, pl.ds(0, count)],
            all_ss,
            all_rs.at[j],
            sibling,
        )
        arrived.wait_recv()
        yy = lax.rem(y + NY - j, NY)
        to_right = remote(
            inbox.at[0, yy], inbox.at[1, yy], ring_ss.at[0, j], ring_rs.at[0, j], next_x
        )
        to_left = remote(
            inbox.at[0, yy], inbox.at[3, yy], ring_ss.at[1, j], ring_rs.at[1, j], last_x
        )
        to_right.start()
        to_left.start()
        ring_right.append(to_right)
        ring_left.append(to_left)

    def pass_on(j):
        yy = lax.rem(y + NY - j, NY)
        ring_right[j].wait_recv()
        ring_left[j].wait_recv()
        slot, device = (1, next_x) if j % 2 == 0 else (3, last_x)
        copy = remote(
            inbox.at[slot, yy], inbox.at[2, yy], ring_ss.at[2, j], ring_rs.at[2, j], device
        )
        copy.start()
        ring_on.append(copy)

    circulate(0)
    circulate(1)
    circulate(2)
    pass_on(0)
    circulate(3)
    pass_on(1)

    def many(copies, device):
        return remote(
            plane_got.at[pl.ds(0, copies)],
            plane_got.at[pl.ds(0, copies)],
            plane_ss,
            plane_rs,
            device,
        )

    many(NZ - 1, sibling).wait_recv()
    stretch = jnp.concatenate([plane_got[i] for i in range(NZ)], axis=1)
    mixed = jnp.dot(stretch, select_z[...], preferred_element_type=F32).astype(BF16)
    mixed_send[...] = mixed
    pl.semaphore_wait(ready2, NX - 1)
    mixed_got[pl.ds(y * 2 + core, 1)] = mixed[None]
    for i in range(1, NX * NY * NCORE):
        dx, dy, dc = i // 8, (i // 2) % 4, i % 2
        cc = 1 - core if dc else core
        remote(
            mixed_send,
            mixed_got.at[dx * 8 + y * 2 + core],
            mixed_ss,
            mixed_rs,
            at(lax.rem(x + dx, NX), lax.rem(y + dy, NY), z, cc),
        ).start()

    def unpack(slot):
        got32[...] = inbox[slot].astype(F32).reshape(CHIPS * 2 * PACKED, SPAN)
        for r in range(PACKED):
            right_hand[slot * LATS : (slot + 1) * LATS, r * SPAN : (r + 1) * SPAN] = got32[
                pl.ds(r, LATS, stride=PACKED), :
            ].astype(BF16)

    unpack(0)
    pass_on(2)
    pass_on(3)
    unpack(1)
    unpack(3)
    for copy in poly_copies:
        copy.wait_recv()
    degrees = jnp.concatenate([poly_got[i] for i in range(NX)], axis=1)
    for copy in ring_on:
        copy.wait_recv()
    unpack(2)

    for c in range(2):
        for pair in range(2):
            start = (c * PARTS + pair * 2) * SPAN
            product2[:, start : start + 2 * SPAN] = jnp.dot(
                degrees, right_hand[:, start : start + 2 * SPAN], preferred_element_type=F32
            )
    remote(
        mixed_got.at[pl.ds(0, 31)], mixed_got.at[pl.ds(0, 31)], mixed_ss, mixed_rs, sibling
    ).wait_recv()
    stacked = jnp.concatenate(
        [
            jnp.concatenate([mixed_got[slot * 8 + i] for i in range(8)], axis=1)
            for slot in range(NX)
        ],
        axis=0,
    )
    sorted_rows = jnp.dot(stacked, select_y[...], preferred_element_type=F32).astype(BF16)
    surface_rows = jnp.concatenate(
        [sorted_rows[slot * 16 : (slot + 1) * 16, :] for slot in range(NX)], axis=1
    )
    surface_rows = jnp.concatenate(
        [surface_rows, jnp.zeros((SPAN - 16, NX * LATS), BF16)], axis=0
    )
    product0[...] = dot_t(degrees, surface_rows)
    lanes = lax.broadcasted_iota(jnp.int32, (DEGREES, SPAN), 1)
    for c in range(2):
        for k in range(WAVES):
            total = jnp.zeros((DEGREES, SPAN), F32)
            for q in range(PARTS):
                r = c * PARTS + q
                block = product2[k * DEGREES : (k + 1) * DEGREES, r * SPAN : (r + 1) * SPAN]
                turn = (PART * (q - k)) % SPAN
                if turn:
                    block = pltpu.roll(block, turn, 1)
                keep = (lanes >= q * PART) & (lanes < (q + 1) * PART)
                total = jnp.where(keep, block, total)
            block = product0[k * DEGREES : (k + 1) * DEGREES, :]
            turn = (-(2 * k + c)) % SPAN
            if turn:
                block = pltpu.roll(block, turn, 1)
            total = jnp.where(lanes == 0, block, total)
            spectral_ref[c, k] = total[:, 0:PLANES].astype(BF16)

    for copy in flux_copies + halo_copies + halo2_copies + sst_copies + poly_copies:
        copy.wait_send()
    core_copy.wait_send()
    remote(
        outbox.at[pl.ds(0, CHIPS - 1)],
        outbox.at[pl.ds(0, CHIPS - 1)],
        all_ss,
        all_rs.at[0],
        sibling,
    ).wait_send()
    many(NZ - 1, sibling).wait_send()
    remote(
        mixed_got.at[pl.ds(0, 31)], mixed_got.at[pl.ds(0, 31)], mixed_ss, mixed_rs, sibling
    ).wait_send()
    for copy in ring_right + ring_left + ring_on:
        copy.wait_send()


def local(
    physical_values,
    samples_per_parallel,
    associated_polynomials,
    heat_salt_anomalies,
    courant_numbers,
    water_indicator,
    air_to_sea_coefficients,
    air_partner_span,
    sea_to_air_coefficients,
    sea_partner_span,
):
    vmem = pl.BlockSpec(memory_space=pltpu.VMEM)
    smem = pl.BlockSpec(memory_space=pltpu.SMEM)
    anywhere = pl.BlockSpec(memory_space=pl.ANY)
    dma = pltpu.SemaphoreType.DMA
    scratch = [
        pltpu.VMEM((1, PLANES, POINTS), BF16),
        pltpu.VMEM((WAVES, LATS, NX * DEGREES), BF16),
        pltpu.VMEM((1, SPANS, SPAN, SPAN), BF16),
        pltpu.VMEM((LINES, 2, SPAN, SPAN), BF16),
        pltpu.VMEM((32, POINTS), F32),
        pltpu.VMEM((48, SPAN), F32),
        pltpu.VMEM((NCOL, 48, SPAN), F32),
        pltpu.VMEM((NCOL, 16, SPAN), F32),
        pltpu.VMEM((32, SPAN), F32),
        pltpu.VMEM((160, SPAN), F32),
        pltpu.VMEM((80, SPAN), F32),
        pltpu.VMEM((TRACER_ROWS, SPAN), F32),
        pltpu.VMEM((TRACER_ROWS, SPAN), F32),
        pltpu.VMEM((TRACER_ROWS, SPAN), F32),
        pltpu.VMEM((WAVES, 48, SPAN), F32),
        pltpu.VMEM((WAVES, 48, SPAN), F32),
        pltpu.VMEM((WAVES, SEG, 2 * SPAN), BF16),
        pltpu.VMEM((SEGS * PITCH, SEG), BF16),
        pltpu.VMEM((SEGS * PITCH, 2 * SPAN), F32),
        pltpu.VMEM((WAVES, 2, PITCH, SPAN), F32),
        pltpu.VMEM((16, SEG), F32),
        pltpu.VMEM((PACKED, SPAN, SPAN), F32),
        pltpu.VMEM((LATS * PACKED, SPAN), F32),
        pltpu.VMEM((CHIPS, 2 * PACKED, SPAN), F32),
        pltpu.VMEM((NX * LATS, PACKED * SPAN), BF16),
        pltpu.VMEM((LATS * PACKED, SPAN), F32),
        pltpu.VMEM((WAVES * DEGREES, PACKED * SPAN), F32),
        pltpu.VMEM((WAVES * DEGREES, SPAN), F32),
        pltpu.VMEM((16, SPAN), F32),
        pltpu.VMEM((NZ * SPAN, SPAN), BF16),
        pltpu.VMEM((8 * SPAN, SPAN), BF16),
        pltpu.VMEM((NX, WAVES * DEGREES, LATS), BF16),
        pltpu.VMEM((48, SPAN), BF16),
        pltpu.VMEM((NCOL, 48, SPAN), BF16),
        pltpu.VMEM((32, SPAN), BF16),
        pltpu.VMEM((32, SPAN), BF16),
        pltpu.VMEM((160, SPAN), BF16),
        pltpu.VMEM((32, SPAN), BF16),
        pltpu.VMEM((32, SPAN), BF16),
        pltpu.VMEM((160, SPAN), BF16),
        pltpu.VMEM((160, SPAN), BF16),
        pltpu.VMEM((16, SPAN), BF16),
        pltpu.VMEM((16, SPAN), BF16),
        pltpu.VMEM((64, SPAN), BF16),
        pltpu.VMEM((16, SPAN), BF16),
        pltpu.VMEM((16, SPAN), BF16),
        pltpu.VMEM((64, SPAN), BF16),
        pltpu.VMEM((64, SPAN), BF16),
        pltpu.VMEM((16, SPAN), BF16),
        pltpu.VMEM((NCOL, 16, SPAN), BF16),
        pltpu.VMEM((NX, WAVES * DEGREES, LATS), BF16),
        pltpu.VMEM((CHIPS * PACKED, SPAN), BF16),
        pltpu.VMEM((CHIPS * PACKED, SPAN), BF16),
        pltpu.VMEM((CHIPS, 2 * PACKED, SPAN), BF16),
        pltpu.VMEM((NX, NY, NZ, 2 * PACKED, SPAN), BF16),
        pltpu.VMEM((16, SPAN), BF16),
        pltpu.VMEM((NZ, 16, SPAN), BF16),
        pltpu.VMEM((16, SPAN), BF16),
        pltpu.VMEM((NX * NY * NCORE, 16, SPAN), BF16),
        dma((4,)),
        dma((NCOL - 1,)),
        dma((NCOL - 1,)),
        dma((4,)),
        dma((4,)),
        dma((4,)),
        dma((4,)),
        dma((NCOL - 1,)),
        dma((NCOL - 1,)),
        dma((NX - 1,)),
        dma((NX - 1,)),
        dma,
        dma,
        dma,
        dma((NY,)),
        dma((3, NY)),
        dma((3, NY)),
        dma,
        dma,
        dma,
        dma,
        pltpu.SemaphoreType.REGULAR,
        pltpu.SemaphoreType.REGULAR,
    ]
    spectral, tracers = pl.pallas_call(
        kernel,
        out_shape=(
            jax.ShapeDtypeStruct((2, WAVES, DEGREES, PLANES), BF16),
            jax.ShapeDtypeStruct((TRACER_ROWS, SPAN), F32),
        ),
        in_specs=[anywhere] * 4 + [vmem] * 3 + [smem] * 3,
        out_specs=(vmem, vmem),
        scratch_shapes=scratch,
        compiler_params=pltpu.CompilerParams(
            collective_id=0, has_side_effects=True, vmem_limit_bytes=64 * 2**20
        ),
        cost_estimate=pl.CostEstimate(
            flops=1_000_000_000, bytes_accessed=3_000_000, transcendentals=0
        ),
    )(
        physical_values,
        associated_polynomials,
        sea_to_air_coefficients,
        air_to_sea_coefficients,
        heat_salt_anomalies.reshape(TRACER_ROWS, SPAN),
        courant_numbers.reshape(TRACER_ROWS, SPAN),
        water_indicator,
        samples_per_parallel,
        jnp.transpose(air_partner_span, (1, 2, 0)),
        sea_partner_span,
    )
    return spectral.transpose(3, 0, 1, 2), tracers.reshape(2, 8, LINES, SPAN)


def solution(mesh):
    placed = (
        P(("grp", "row", "col"), None, None),
        P(),
        P(("row", "col"), "grp", None),
        P(None, None, ("grp", "row"), "col"),
        P(None, None, ("grp", "row"), "col"),
        P(("grp", "row"), "col"),
        P(("grp", "row"), None, "col", None),
        P(("grp", "row"), "col", None),
        P(("grp", "row", "col"), None, None, None),
        P(("grp", "row", "col"), None),
    )
    return jax.shard_map(
        local,
        mesh=mesh,
        in_specs=placed,
        out_specs=(P(None, None, ("row", "col"), "grp"), P(None, None, ("grp", "row"), "col")),
        check_vma=False,
    )
```

```python
import math

import jax
import jax.numpy as jnp
from jax import lax
from jax.experimental import pallas as pl
from jax.experimental.pallas import tpu as pltpu
from jax.sharding import PartitionSpec as P

MESH = pl.DeviceIdType.MESH
F32 = jnp.float32
BF16 = jnp.bfloat16

NX, NY, NZ, NCORE = 4, 4, 16, 2
NROW, NCOL = 16, 8
CHIPS = NY * NZ

LEV = 10
PLANES = 100
POINTS = 2688
SPANS = 21
SPAN = 128
WAVES = 5
DEGREES = 160
LATS = 128
LINES = 4
TRACER_ROWS = 64
DIFFUSION = 0.07
COUPLE = 0.5

SEG = 256
SEGS = 11
PITCH = 112
PART = 25
PARTS = 4
PACKED = 8


def sincos(turns4):
    quarter = jnp.floor(turns4 + 0.5)
    y = (turns4 - quarter) * (0.5 * math.pi)
    y2 = y * y
    s = y * (1.0 + y2 * (-1.0 / 6 + y2 * (1.0 / 120 + y2 * (-1.0 / 5040 + y2 * (1.0 / 362880)))))
    c = 1.0 + y2 * (
        -0.5 + y2 * (1.0 / 24 + y2 * (-1.0 / 720 + y2 * (1.0 / 40320 + y2 * (-1.0 / 3628800))))
    )
    odd = (quarter == 1.0) | (quarter == 3.0)
    cos_sign = jnp.where((quarter == 1.0) | (quarter == 2.0), -1.0, 1.0)
    sin_sign = jnp.where((quarter == 2.0) | (quarter == 3.0), -1.0, 1.0)
    return cos_sign * jnp.where(odd, s, c), sin_sign * jnp.where(odd, c, s)


def dot_t(a, b):
    return lax.dot_general(a, b, (((1,), (1,)), ((), ())), preferred_element_type=F32)


def kernel(
    phys_hbm,
    poly_hbm,
    s2a_hbm,
    a2s_hbm,
    tracer_hbm,
    courant_hbm,
    water_hbm,
    points_hbm,
    air_hbm,
    sea_hbm,
    spectral_hbm,
    tracer_out_hbm,
    spectral_ref,
    tracer_out_ref,
    tracer_ref,
    courant_ref,
    water_ref,
    points_ref,
    air_ref,
    sea_ref,
    xv,
    xtop,
    pv,
    s2av,
    a2sv,
    x32,
    flux32,
    flux_got32,
    sst_got32,
    rows32,
    cells32,
    shifted,
    tops,
    bottoms,
    forced,
    table_c,
    table_s,
    waves,
    segments,
    product,
    fourier,
    row0,
    parts,
    packed32,
    out32,
    right_hand,
    got32,
    product2,
    product0,
    plane32,
    select_y,
    bulk,
    poly_t,
    flux_send,
    flux_got,
    down_send,
    up_send,
    cells_send,
    top1,
    bottom1,
    left1,
    right1,
    down2_send,
    up2_send,
    cells2_send,
    top2,
    bottom2,
    left2,
    right2,
    sst_send,
    sst_got,
    poly_got,
    core_send,
    core_got,
    outbox,
    inbox,
    plane_send,
    plane_got,
    mixed_send,
    mixed_got,
    local_sem,
    flux_ss,
    flux_rs,
    halo_ss,
    halo_rs,
    halo2_ss,
    halo2_rs,
    sst_ss,
    sst_rs,
    poly_ss,
    poly_rs,
    core_ss,
    core_rs,
    all_ss,
    all_rs,
    ring_ss,
    ring_rs,
    plane_ss,
    plane_rs,
    mixed_ss,
    mixed_rs,
    ready,
    ready2,
):
    x = lax.axis_index("grp")
    row = lax.axis_index("row")
    col = lax.axis_index("col")
    y = row // 4
    z = lax.rem(row, 4) * 4 + col // 2
    core = lax.rem(col, 2)
    strip = x * NROW + row

    def at(xx, yy, zz, cc):
        return (xx, yy * 4 + zz // 4, lax.rem(zz, 4) * 2 + cc)

    def remote(src, dst, ss, rs, device):
        return pltpu.make_async_remote_copy(
            src_ref=src, dst_ref=dst, send_sem=ss, recv_sem=rs, device_id=device, device_id_type=MESH
        )

    def strip_at(other):
        return (other // NROW, lax.rem(other, NROW), col)

    below = strip_at(lax.rem(strip + 1, NX * NROW))
    above = strip_at(lax.rem(strip + NX * NROW - 1, NX * NROW))
    band = [(x, row, lax.rem(col + i, NCOL)) for i in range(1, NCOL)]
    after = band[0]
    before = band[-1]
    z_ring = [at(x, y, lax.rem(z + i, NZ), core) for i in range(1, NZ)]
    y_ring = [at(x, lax.rem(y + i, NY), z, core) for i in range(1, NY)]
    x_ring = [at(lax.rem(x + i, NX), y, z, core) for i in range(1, NX)]
    sibling = at(x, y, z, 1 - core)

    moves = [
        (phys_hbm, xv),
        (poly_hbm, pv),
        (a2s_hbm, a2sv),
        (s2a_hbm, s2av),
        (points_hbm, points_ref),
        (phys_hbm.at[0, pl.ds(0, 32)], xtop),
        (tracer_hbm, tracer_ref),
        (courant_hbm, courant_ref),
        (water_hbm, water_ref),
        (air_hbm, air_ref),
        (sea_hbm, sea_ref),
    ]
    ins = [
        pltpu.make_async_copy(source, target, local_sem.at[i])
        for i, (source, target) in enumerate(moves)
    ]
    for i in (4, 5, 6, 7, 8, 0, 9, 2, 10, 3, 1):
        ins[i].start()
    barrier = pltpu.get_barrier_semaphore()
    greeted = band + [below, above, sibling] + x_ring + y_ring + z_ring
    for device in greeted:
        pl.semaphore_signal(barrier, inc=1, device_id=device, device_id_type=MESH)

    own = strip * NCOL + col
    ins[4].wait()
    n = points_ref[own]
    lane = lax.broadcasted_iota(jnp.int32, (1, SPAN), 1)

    ins[5].wait()
    x32[...] = xtop[...].astype(F32)
    flux32[...] = jnp.zeros_like(flux32)
    for b in range(SPANS):
        live = lane + b * SPAN < n
        for q in range(2):
            line = x32[(q + 1) * LEV : (q + 1) * LEV + 1, b * SPAN : (b + 1) * SPAN]
            flux32[q * 24 + b : q * 24 + b + 1, :] = jnp.where(live, line, 0.0)
    flux_send[...] = flux32[...].astype(BF16)
    flux_got[pl.ds(col, 1)] = flux_send[...][None]

    for i in (6, 7, 8):
        ins[i].wait()
    wet = water_ref[...].astype(F32)
    for i in range(16):
        cells32[96 + 4 * i : 100 + 4 * i, :] = wet
    cells32[0:64, :] = tracer_ref[...]
    cells32[64:96, :] = courant_ref[32:64, :]
    cells_send[...] = cells32[...].astype(BF16)
    rows32[...] = jnp.zeros_like(rows32)
    rows32[0:16, :] = tracer_ref[pl.ds(3, 16, stride=4), :]
    rows32[16:24, :] = courant_ref[pl.ds(3, 8, stride=4), :]
    rows32[24:25, :] = wet[3:4, :]
    down_send[...] = rows32[...].astype(BF16)
    rows32[0:16, :] = tracer_ref[pl.ds(0, 16, stride=4), :]
    rows32[24:25, :] = wet[0:1, :]
    up_send[...] = rows32[...].astype(BF16)

    pl.semaphore_wait(barrier, len(greeted))
    flux_copies = [
        remote(flux_send, flux_got.at[col], flux_ss.at[i], flux_rs.at[i], device)
        for i, device in enumerate(band)
    ]
    halo_copies = [
        remote(down_send, top1, halo_ss.at[0], halo_rs.at[0], below),
        remote(up_send, bottom1, halo_ss.at[1], halo_rs.at[1], above),
        remote(cells_send, left1, halo_ss.at[2], halo_rs.at[2], after),
        remote(cells_send, right1, halo_ss.at[3], halo_rs.at[3], before),
    ]
    for copy in flux_copies + halo_copies:
        copy.start()
    for device in y_ring:
        pl.semaphore_signal(ready, inc=1, device_id=device, device_id_type=MESH)

    shape = (WAVES, 48, SPAN)
    k_of = lax.broadcasted_iota(jnp.int32, shape, 0)
    p_row = lax.broadcasted_iota(jnp.int32, shape, 1)
    d_of = lax.broadcasted_iota(jnp.int32, shape, 2)
    owner = (d_of & 3) * 32 + ((d_of >> 2) & 15) * 2 + (d_of >> 6)
    orders = owner * WAVES + k_of
    places = jnp.where(
        p_row < 16, p_row, jnp.where(p_row < 32, (p_row - 16) * 16, (p_row - 32) * SEG)
    )
    count = jnp.full(shape, n, jnp.int32).astype(F32)
    inverse = 1.0 / count
    turns = orders.astype(F32) * places.astype(F32)
    phase = turns - jnp.floor(turns * inverse) * count
    phase = jnp.where(phase < 0.0, phase + count, phase)
    phase = jnp.where(phase >= count, phase - count, phase)
    cosine, sine = sincos(phase * (4.0 * inverse))
    table_c[...] = cosine
    table_s[...] = -sine

    def fill_waves(a, _):
        start = pl.multiple_of(a * 16, 16)
        for k in range(WAVES):
            ac = table_c[k, pl.ds(16 + a, 1), :]
            as_ = table_s[k, pl.ds(16 + a, 1), :]
            bc = table_c[k, 0:16, :]
            bs = table_s[k, 0:16, :]
            waves[k, pl.ds(start, 16), 0:SPAN] = (ac * bc - as_ * bs).astype(BF16)
            waves[k, pl.ds(start, 16), SPAN : 2 * SPAN] = (ac * bs + as_ * bc).astype(BF16)
        return 0

    lax.fori_loop(0, 16, fill_waves, 0)

    ins[0].wait()
    for i in range(SEGS):
        width = min(SEG, POINTS - i * SEG)
        pos = i * SEG + lax.broadcasted_iota(jnp.int32, (1, width), 1)
        values = xv[0, :, i * SEG : i * SEG + width].astype(F32)
        values = jnp.where(pos < n, values, 0.0).astype(BF16)
        segments[i * PITCH + 96 : (i + 1) * PITCH, :] = jnp.zeros((16, SEG), BF16)
        if width < SEG:
            segments[i * PITCH : (i + 1) * PITCH, width:SEG] = jnp.zeros((PITCH, SEG - width), BF16)
        segments[i * PITCH : i * PITCH + PLANES, 0:width] = values

    inverse_row = 1.0 / jnp.full((1, SPAN), n, jnp.int32).astype(F32)
    d_row = lax.broadcasted_iota(jnp.int32, (1, SPAN), 1)
    owner_row = (d_row & 3) * 32 + ((d_row >> 2) & 15) * 2 + (d_row >> 6)

    def scale_of(k):
        return jnp.where(2 * (owner_row * WAVES + k) < n, inverse_row, 0.0)

    def transform(k, _):
        product[...] = jnp.dot(segments[...], waves[k], preferred_element_type=F32)
        real = jnp.zeros((PITCH, SPAN), F32)
        imag = jnp.zeros((PITCH, SPAN), F32)
        for i in range(SEGS):
            wc = table_c[k, 32 + i : 33 + i, :]
            ws = table_s[k, 32 + i : 33 + i, :]
            yc = product[i * PITCH : (i + 1) * PITCH, 0:SPAN]
            ys = product[i * PITCH : (i + 1) * PITCH, SPAN : 2 * SPAN]
            real = real + (yc * wc - ys * ws)
            imag = imag + (yc * ws + ys * wc)
        scale = scale_of(k)
        fourier[k, 0] = real * scale
        fourier[k, 1] = imag * scale
        return 0

    lax.fori_loop(0, WAVES, transform, 0)

    for c in range(2):
        for q in range(PARTS):
            r = c * PARTS + q
            parts[r, 120:128, :] = jnp.zeros((8, SPAN), F32)
            for k in range(WAVES):
                parts[r, k * PART : (k + 1) * PART, :] = fourier[
                    k, c, q * PART : (q + 1) * PART, :
                ]
            packed32[pl.ds(r, LATS, stride=PACKED), :] = parts[r].T

    half_rows = CHIPS * PACKED
    core_send[...] = packed32[pl.ds(pl.multiple_of((1 - core) * half_rows, 8), half_rows), :].astype(
        BF16
    )
    core_copy = remote(core_send, core_got, core_ss, core_rs, sibling)
    core_copy.start()
    mine = packed32[pl.ds(pl.multiple_of(core * half_rows, 8), half_rows), :].reshape(
        CHIPS, PACKED, SPAN
    )
    ins[2].wait()
    ins[9].wait()
    for copy in flux_copies:
        copy.wait_recv()
    flux_got32[...] = flux_got[...].astype(F32)
    two = lax.broadcasted_iota(jnp.int32, (16, SPAN), 0)
    forced[...] = jnp.zeros_like(forced)
    for line in range(LINES):
        total = jnp.zeros((16, SPAN), F32)
        for k in range(2):
            span = air_ref[0, k, line]
            source = lax.div(span, SPANS)
            block = lax.rem(span, SPANS)
            first = flux_got32[source, pl.ds(block, 1), :]
            second = flux_got32[source, pl.ds(block + 24, 1), :]
            pair = jnp.where(
                two == 0, jnp.broadcast_to(first, (16, SPAN)), jnp.broadcast_to(second, (16, SPAN))
            )
            total = total + dot_t(pair.astype(BF16), a2sv[line, k])
        forced[line : line + 1, :] = COUPLE * total[0:1, :]
        forced[32 + line : 33 + line, :] = COUPLE * total[1:2, :]

    has_top = jnp.where(strip > 0, 1.0, 0.0).astype(F32)
    has_bottom = jnp.where(strip < NX * NROW - 1, 1.0, 0.0).astype(F32)
    has_left = jnp.where(col > 0, 1.0, 0.0).astype(F32)
    has_right = jnp.where(col < NCOL - 1, 1.0, 0.0).astype(F32)
    line_of = lax.broadcasted_iota(jnp.int32, (TRACER_ROWS, SPAN), 0) & 3
    lane_of = lax.broadcasted_iota(jnp.int32, (TRACER_ROWS, SPAN), 1)

    def from_above(value, edge):
        shifted[8:72, :] = value
        tops[pl.ds(0, 16, stride=4), :] = edge
        return jnp.where(line_of == 0, tops[...], shifted[7:71, :])

    def from_below(value, edge):
        shifted[8:72, :] = value
        bottoms[pl.ds(3, 16, stride=4), :] = edge
        return jnp.where(line_of == 3, bottoms[...], shifted[9:73, :])

    def from_left(value, tile):
        return jnp.where(lane_of == 0, pltpu.roll(tile, 1, 1), pltpu.roll(value, 1, 1))

    def from_right(value, tile):
        return jnp.where(
            lane_of == SPAN - 1, pltpu.roll(tile, SPAN - 1, 1), pltpu.roll(value, SPAN - 1, 1)
        )

    def twice(value):
        return jnp.concatenate([value, value], axis=0)

    for copy in halo_copies:
        copy.wait_recv()
    shifted[...] = jnp.zeros_like(shifted)
    tops[...] = jnp.zeros_like(tops)
    bottoms[...] = jnp.zeros_like(bottoms)
    top = top1[...].astype(F32) * has_top
    bottom = bottom1[...].astype(F32) * has_bottom
    left = left1[...].astype(F32) * has_left
    right = right1[...].astype(F32) * has_right
    wet64 = cells32[96:160, :]
    east = twice(courant_ref[0:32, :])
    north = twice(courant_ref[32:64, :])
    east_up = from_above(east, twice(top[16:24, :]))
    north_left = from_left(north, twice(left[64:96, :]))
    pair_up = wet64 * from_above(wet64, jnp.broadcast_to(top[24:25, :], (16, SPAN)))
    pair_down = wet64 * from_below(wet64, jnp.broadcast_to(bottom[24:25, :], (16, SPAN)))
    pair_left = wet64 * from_left(wet64, left[96:160, :])
    pair_right = wet64 * from_right(wet64, right[96:160, :])

    def flow(pair, speed, low, high):
        return pair * (
            jnp.maximum(speed, 0.0) * low
            + jnp.minimum(speed, 0.0) * high
            - DIFFUSION * (high - low)
        )

    def advance(q, edge_top, edge_bottom, tile_left, tile_right):
        spread = (
            flow(pair_down, east, q, from_below(q, edge_bottom))
            - flow(pair_up, east_up, from_above(q, edge_top), q)
            + flow(pair_right, north, q, from_right(q, tile_right))
            - flow(pair_left, north_left, from_left(q, tile_left), q)
        )
        return q + wet64 * (forced[...] - spread)

    state = advance(
        tracer_ref[...], top[0:16, :], bottom[0:16, :], left[0:64, :], right[0:64, :]
    )
    tracer_out_ref[...] = state
    cells2_send[...] = state.astype(BF16)
    down2_send[...] = tracer_out_ref[pl.ds(3, 16, stride=4), :].astype(BF16)
    up2_send[...] = tracer_out_ref[pl.ds(0, 16, stride=4), :].astype(BF16)
    halo2_copies = [
        remote(down2_send, top2, halo2_ss.at[0], halo2_rs.at[0], below),
        remote(up2_send, bottom2, halo2_ss.at[1], halo2_rs.at[1], above),
        remote(cells2_send, left2, halo2_ss.at[2], halo2_rs.at[2], after),
        remote(cells2_send, right2, halo2_ss.at[3], halo2_rs.at[3], before),
    ]
    for copy in halo2_copies:
        copy.start()

    core_copy.wait_recv()
    theirs = core_got[...].astype(F32).reshape(CHIPS, PACKED, SPAN)
    is_first = core == 0
    out32[:, 0:PACKED, :] = jnp.where(is_first, mine, theirs)
    out32[:, PACKED : 2 * PACKED, :] = jnp.where(is_first, theirs, mine)
    outbox[...] = out32[...].astype(BF16)
    pl.semaphore_wait(ready, NY - 1)
    for device in x_ring:
        pl.semaphore_signal(ready2, inc=1, device_id=device, device_id_type=MESH)

    for j in range(NY):
        yy = lax.rem(y + j, NY)

        def post(i, _, j=j, yy=yy):
            zz = lax.rem(z + i, NZ)
            remote(
                outbox.at[zz * NY + yy],
                inbox.at[0, y, z],
                all_ss,
                all_rs.at[j],
                at(x, yy, zz, core),
            ).start()
            return 0

        lax.fori_loop(1, NZ, post, 0)
        if j:
            post(0, 0)
    inbox[0, pl.ds(y, 1), pl.ds(z, 1)] = outbox[pl.ds(z * NY + y, 1)][None]

    ins[1].wait()
    for k in range(WAVES):
        turned = pv[k].astype(F32).T.astype(BF16)
        for g in range(NX):
            poly_t[g, k * DEGREES : (k + 1) * DEGREES, :] = turned[g * DEGREES : (g + 1) * DEGREES]
    poly_got[0] = poly_t[x]
    poly_copies = [
        remote(
            poly_t.at[lax.rem(x + i, NX)],
            poly_got.at[i],
            poly_ss.at[i - 1],
            poly_rs.at[i - 1],
            x_ring[i - 1],
        )
        for i in range(1, NX)
    ]
    for copy in poly_copies:
        copy.start()

    rows_b = lax.broadcasted_iota(jnp.int32, (8 * SPAN, SPAN), 0)
    lanes_b = lax.broadcasted_iota(jnp.int32, (8 * SPAN, SPAN), 1)
    lane_in = rows_b & 127
    wanted = (rows_b >> 8) * 32 + (lane_in >> 3) * 2 + ((rows_b >> 7) & 1)
    chosen = ((lane_in & 7) == core * 4 + y) & (lanes_b == wanted)
    select_y[...] = jnp.where(chosen, 1.0, 0.0).astype(BF16)

    for copy in halo2_copies:
        copy.wait_recv()
    state = advance(
        tracer_out_ref[...],
        top2[...].astype(F32) * has_top,
        bottom2[...].astype(F32) * has_bottom,
        left2[...].astype(F32) * has_left,
        right2[...].astype(F32) * has_right,
    )
    tracer_out_ref[...] = state
    tracer_leave = pltpu.make_async_copy(tracer_out_ref, tracer_out_hbm, local_sem.at[11])
    tracer_leave.start()
    sst_send[...] = state[0:16, :].astype(BF16)
    sst_got[pl.ds(col, 1)] = sst_send[...][None]
    sst_copies = [
        remote(sst_send, sst_got.at[col], sst_ss.at[i], sst_rs.at[i], device)
        for i, device in enumerate(band)
    ]
    for copy in sst_copies:
        copy.start()

    next_x = x_ring[0]
    last_x = x_ring[-1]
    ring_right = []
    ring_left = []
    ring_on = []

    def circulate(j):
        count = NZ - 1 if j == 0 else NZ
        arrived = remote(
            outbox.at[pl.ds(0, count)],
            inbox.at[0, 0, pl.ds(0, count)],
            all_ss,
            all_rs.at[j],
            sibling,
        )
        arrived.wait_recv()
        yy = lax.rem(y + NY - j, NY)
        to_right = remote(
            inbox.at[0, yy], inbox.at[1, yy], ring_ss.at[0, j], ring_rs.at[0, j], next_x
        )
        to_left = remote(
            inbox.at[0, yy], inbox.at[3, yy], ring_ss.at[1, j], ring_rs.at[1, j], last_x
        )
        to_right.start()
        to_left.start()
        ring_right.append(to_right)
        ring_left.append(to_left)

    def pass_on(j):
        yy = lax.rem(y + NY - j, NY)
        ring_right[j].wait_recv()
        ring_left[j].wait_recv()
        slot, device = (1, next_x) if j % 2 == 0 else (3, last_x)
        copy = remote(
            inbox.at[slot, yy], inbox.at[2, yy], ring_ss.at[2, j], ring_rs.at[2, j], device
        )
        copy.start()
        ring_on.append(copy)

    circulate(0)
    circulate(1)

    ins[3].wait()
    ins[10].wait()
    for copy in sst_copies:
        copy.wait_recv()
    sst_got32[...] = sst_got[...].astype(F32)
    row0[...] = jnp.zeros_like(row0)
    for b in range(SPANS):
        span = sea_ref[0, b]
        source = lax.div(span, LINES)
        line = lax.rem(span, LINES)
        warmth = jnp.broadcast_to(sst_got32[source, pl.ds(line, 1), :], (16, SPAN))
        sampled = dot_t(warmth.astype(BF16), s2av[0, b])[0:1, :]
        plane = x32[0:1, b * SPAN : (b + 1) * SPAN] + sampled
        plane = jnp.where(lane + b * SPAN < n, plane, 0.0)
        half = (b % 2) * SPAN
        row0[b // 2 : b // 2 + 1, half : half + SPAN] = plane
    surface = row0[...].astype(BF16)
    plane32[...] = jnp.zeros_like(plane32)
    for k in range(WAVES):
        part = jnp.dot(surface, waves[k], preferred_element_type=F32)
        wc = table_c[k, 32:48, :]
        ws = table_s[k, 32:48, :]
        yc = part[:, 0:SPAN]
        ys = part[:, SPAN : 2 * SPAN]
        scale = scale_of(k)
        plane32[2 * k : 2 * k + 1, :] = jnp.sum(yc * wc - ys * ws, axis=0, keepdims=True) * scale
        plane32[2 * k + 1 : 2 * k + 2, :] = (
            jnp.sum(yc * ws + ys * wc, axis=0, keepdims=True) * scale
        )

    plane_send[...] = plane32[...].astype(BF16)
    plane_got[pl.ds(z, 1)] = plane_send[...][None]
    for device in z_ring:
        remote(plane_send, plane_got.at[z], plane_ss, plane_rs, device).start()

    circulate(2)
    pass_on(0)
    circulate(3)
    pass_on(1)

    def many(copies, device):
        return remote(
            plane_got.at[pl.ds(0, copies)],
            plane_got.at[pl.ds(0, copies)],
            plane_ss,
            plane_rs,
            device,
        )

    many(NZ - 1, sibling).wait_recv()
    stretch = plane_got[...].astype(F32).reshape(NZ * 16, SPAN)
    stretch = pltpu.roll(stretch, lax.rem(SPAN - NY * z, SPAN), 1)
    place = lax.broadcasted_iota(jnp.int32, (16, SPAN), 1) >> 2
    mixed = jnp.zeros((16, SPAN), F32)
    for i in range(NZ):
        tile = stretch[i * 16 : (i + 1) * 16, :]
        low = pltpu.roll(tile, 8 * i, 1) if i else tile
        high = pltpu.roll(tile, (8 * i + 4 + CHIPS) % SPAN, 1)
        mixed = jnp.where(place == 2 * i, low, jnp.where(place == 2 * i + 1, high, mixed))
    mixed = mixed.astype(BF16)
    mixed_send[...] = mixed
    pl.semaphore_wait(ready2, NX - 1)
    mixed_got[pl.ds(y * 2 + core, 1)] = mixed[None]
    for i in range(1, NX * NY * NCORE):
        dx, dy, dc = i // 8, (i // 2) % 4, i % 2
        cc = 1 - core if dc else core
        remote(
            mixed_send,
            mixed_got.at[dx * 8 + y * 2 + core],
            mixed_ss,
            mixed_rs,
            at(lax.rem(x + dx, NX), lax.rem(y + dy, NY), z, cc),
        ).start()

    def unpack(slot):
        got32[...] = inbox[slot].astype(F32).reshape(CHIPS * 2 * PACKED, SPAN)
        for r in range(PACKED):
            right_hand[slot * LATS : (slot + 1) * LATS, r * SPAN : (r + 1) * SPAN] = got32[
                pl.ds(r, LATS, stride=PACKED), :
            ].astype(BF16)

    unpack(0)
    pass_on(2)
    pass_on(3)
    unpack(1)
    unpack(3)
    for copy in poly_copies:
        copy.wait_recv()
    degrees = jnp.concatenate([poly_got[i] for i in range(NX)], axis=1)
    for copy in ring_on:
        copy.wait_recv()
    unpack(2)

    for c in range(2):
        for pair in range(2):
            start = (c * PARTS + pair * 2) * SPAN
            product2[:, start : start + 2 * SPAN] = jnp.dot(
                degrees, right_hand[:, start : start + 2 * SPAN], preferred_element_type=F32
            )
    lanes = lax.broadcasted_iota(jnp.int32, (DEGREES, SPAN), 1)
    for c in range(2):
        for k in range(WAVES):
            total = jnp.zeros((DEGREES, SPAN), F32)
            for q in range(PARTS):
                r = c * PARTS + q
                block = product2[k * DEGREES : (k + 1) * DEGREES, r * SPAN : (r + 1) * SPAN]
                turn = (PART * (q - k)) % SPAN
                if turn:
                    block = pltpu.roll(block, turn, 1)
                keep = (lanes >= q * PART) & (lanes < (q + 1) * PART)
                total = jnp.where(keep, block, total)
            bulk[c, k] = total

    remote(
        mixed_got.at[pl.ds(0, 31)], mixed_got.at[pl.ds(0, 31)], mixed_ss, mixed_rs, sibling
    ).wait_recv()
    stacked = jnp.concatenate(
        [
            jnp.concatenate([mixed_got[slot * 8 + i] for i in range(8)], axis=1)
            for slot in range(NX)
        ],
        axis=0,
    )
    sorted_rows = jnp.dot(stacked, select_y[...], preferred_element_type=F32).astype(BF16)
    surface_rows = jnp.concatenate(
        [sorted_rows[slot * 16 : (slot + 1) * 16, :] for slot in range(NX)], axis=1
    )
    surface_rows = jnp.concatenate(
        [surface_rows, jnp.zeros((SPAN - 16, NX * LATS), BF16)], axis=0
    )
    product0[...] = dot_t(degrees, surface_rows)
    leaves = [tracer_leave]
    for c in range(2):
        for k in range(WAVES):
            block = product0[k * DEGREES : (k + 1) * DEGREES, :]
            turn = (-(2 * k + c)) % SPAN
            if turn:
                block = pltpu.roll(block, turn, 1)
            total = jnp.where(lanes == 0, block, bulk[c, k])
            spectral_ref[c, k] = total[:, 0:PLANES].astype(BF16)
        leave = pltpu.make_async_copy(
            spectral_ref.at[c], spectral_hbm.at[c], local_sem.at[12 + c]
        )
        leave.start()
        leaves.append(leave)

    for copy in flux_copies + halo_copies + halo2_copies + sst_copies + poly_copies:
        copy.wait_send()
    core_copy.wait_send()
    remote(
        outbox.at[pl.ds(0, CHIPS - 1)],
        outbox.at[pl.ds(0, CHIPS - 1)],
        all_ss,
        all_rs.at[0],
        sibling,
    ).wait_send()
    many(NZ - 1, sibling).wait_send()
    remote(
        mixed_got.at[pl.ds(0, 31)], mixed_got.at[pl.ds(0, 31)], mixed_ss, mixed_rs, sibling
    ).wait_send()
    for copy in ring_right + ring_left + ring_on:
        copy.wait_send()
    for copy in leaves:
        copy.wait()


def local(
    physical_values,
    samples_per_parallel,
    associated_polynomials,
    heat_salt_anomalies,
    courant_numbers,
    water_indicator,
    air_to_sea_coefficients,
    air_partner_span,
    sea_to_air_coefficients,
    sea_partner_span,
):
    hbm = pl.BlockSpec(memory_space=pltpu.HBM)
    dma = pltpu.SemaphoreType.DMA
    scratch = [
        pltpu.VMEM((2, WAVES, DEGREES, PLANES), BF16),
        pltpu.VMEM((TRACER_ROWS, SPAN), F32),
        pltpu.VMEM((TRACER_ROWS, SPAN), F32),
        pltpu.VMEM((TRACER_ROWS, SPAN), F32),
        pltpu.VMEM((LINES, SPAN), jnp.int32),
        pltpu.SMEM((512,), jnp.int32),
        pltpu.SMEM((1, 2, LINES), jnp.int32),
        pltpu.SMEM((1, SPANS), jnp.int32),
        pltpu.VMEM((1, PLANES, POINTS), BF16),
        pltpu.VMEM((32, POINTS), BF16),
        pltpu.VMEM((WAVES, LATS, NX * DEGREES), BF16),
        pltpu.VMEM((1, SPANS, SPAN, SPAN), BF16),
        pltpu.VMEM((LINES, 2, SPAN, SPAN), BF16),
        pltpu.VMEM((32, POINTS), F32),
        pltpu.VMEM((48, SPAN), F32),
        pltpu.VMEM((NCOL, 48, SPAN), F32),
        pltpu.VMEM((NCOL, 16, SPAN), F32),
        pltpu.VMEM((32, SPAN), F32),
        pltpu.VMEM((160, SPAN), F32),
        pltpu.VMEM((80, SPAN), F32),
        pltpu.VMEM((TRACER_ROWS, SPAN), F32),
        pltpu.VMEM((TRACER_ROWS, SPAN), F32),
        pltpu.VMEM((TRACER_ROWS, SPAN), F32),
        pltpu.VMEM((WAVES, 48, SPAN), F32),
        pltpu.VMEM((WAVES, 48, SPAN), F32),
        pltpu.VMEM((WAVES, SEG, 2 * SPAN), BF16),
        pltpu.VMEM((SEGS * PITCH, SEG), BF16),
        pltpu.VMEM((SEGS * PITCH, 2 * SPAN), F32),
        pltpu.VMEM((WAVES, 2, PITCH, SPAN), F32),
        pltpu.VMEM((16, SEG), F32),
        pltpu.VMEM((PACKED, SPAN, SPAN), F32),
        pltpu.VMEM((LATS * PACKED, SPAN), F32),
        pltpu.VMEM((CHIPS, 2 * PACKED, SPAN), F32),
        pltpu.VMEM((NX * LATS, PACKED * SPAN), BF16),
        pltpu.VMEM((LATS * PACKED, SPAN), F32),
        pltpu.VMEM((WAVES * DEGREES, PACKED * SPAN), F32),
        pltpu.VMEM((WAVES * DEGREES, SPAN), F32),
        pltpu.VMEM((16, SPAN), F32),
        pltpu.VMEM((8 * SPAN, SPAN), BF16),
        pltpu.VMEM((2, WAVES, DEGREES, SPAN), F32),
        pltpu.VMEM((NX, WAVES * DEGREES, LATS), BF16),
        pltpu.VMEM((48, SPAN), BF16),
        pltpu.VMEM((NCOL, 48, SPAN), BF16),
        pltpu.VMEM((32, SPAN), BF16),
        pltpu.VMEM((32, SPAN), BF16),
        pltpu.VMEM((160, SPAN), BF16),
        pltpu.VMEM((32, SPAN), BF16),
        pltpu.VMEM((32, SPAN), BF16),
        pltpu.VMEM((160, SPAN), BF16),
        pltpu.VMEM((160, SPAN), BF16),
        pltpu.VMEM((16, SPAN), BF16),
        pltpu.VMEM((16, SPAN), BF16),
        pltpu.VMEM((64, SPAN), BF16),
        pltpu.VMEM((16, SPAN), BF16),
        pltpu.VMEM((16, SPAN), BF16),
        pltpu.VMEM((64, SPAN), BF16),
        pltpu.VMEM((64, SPAN), BF16),
        pltpu.VMEM((16, SPAN), BF16),
        pltpu.VMEM((NCOL, 16, SPAN), BF16),
        pltpu.VMEM((NX, WAVES * DEGREES, LATS), BF16),
        pltpu.VMEM((CHIPS * PACKED, SPAN), BF16),
        pltpu.VMEM((CHIPS * PACKED, SPAN), BF16),
        pltpu.VMEM((CHIPS, 2 * PACKED, SPAN), BF16),
        pltpu.VMEM((NX, NY, NZ, 2 * PACKED, SPAN), BF16),
        pltpu.VMEM((16, SPAN), BF16),
        pltpu.VMEM((NZ, 16, SPAN), BF16),
        pltpu.VMEM((16, SPAN), BF16),
        pltpu.VMEM((NX * NY * NCORE, 16, SPAN), BF16),
        dma((14,)),
        dma((NCOL - 1,)),
        dma((NCOL - 1,)),
        dma((4,)),
        dma((4,)),
        dma((4,)),
        dma((4,)),
        dma((NCOL - 1,)),
        dma((NCOL - 1,)),
        dma((NX - 1,)),
        dma((NX - 1,)),
        dma,
        dma,
        dma,
        dma((NY,)),
        dma((3, NY)),
        dma((3, NY)),
        dma,
        dma,
        dma,
        dma,
        pltpu.SemaphoreType.REGULAR,
        pltpu.SemaphoreType.REGULAR,
    ]
    spectral, tracers = pl.pallas_call(
        kernel,
        out_shape=(
            jax.ShapeDtypeStruct((2, WAVES, DEGREES, PLANES), BF16),
            jax.ShapeDtypeStruct((TRACER_ROWS, SPAN), F32),
        ),
        in_specs=[hbm] * 10,
        out_specs=(hbm, hbm),
        scratch_shapes=scratch,
        compiler_params=pltpu.CompilerParams(
            collective_id=0, has_side_effects=True, vmem_limit_bytes=64 * 2**20
        ),
        cost_estimate=pl.CostEstimate(
            flops=1_000_000_000, bytes_accessed=3_000_000, transcendentals=0
        ),
    )(
        physical_values,
        associated_polynomials,
        sea_to_air_coefficients,
        air_to_sea_coefficients,
        heat_salt_anomalies.reshape(TRACER_ROWS, SPAN),
        courant_numbers.reshape(TRACER_ROWS, SPAN),
        water_indicator,
        samples_per_parallel,
        jnp.transpose(air_partner_span, (1, 2, 0)),
        sea_partner_span,
    )
    return spectral.transpose(3, 0, 1, 2), tracers.reshape(2, 8, LINES, SPAN)


def solution(mesh):
    placed = (
        P(("grp", "row", "col"), None, None),
        P(),
        P(("row", "col"), "grp", None),
        P(None, None, ("grp", "row"), "col"),
        P(None, None, ("grp", "row"), "col"),
        P(("grp", "row"), "col"),
        P(("grp", "row"), None, "col", None),
        P(("grp", "row"), "col", None),
        P(("grp", "row", "col"), None, None, None),
        P(("grp", "row", "col"), None),
    )
    return jax.shard_map(
        local,
        mesh=mesh,
        in_specs=placed,
        out_specs=(P(None, None, ("row", "col"), "grp"), P(None, None, ("grp", "row"), "col")),
        check_vma=False,
    )
```

```python
import math

import jax
import jax.numpy as jnp
from jax import lax
from jax.experimental import pallas as pl
from jax.experimental.pallas import tpu as pltpu
from jax.sharding import PartitionSpec as P

MESH = pl.DeviceIdType.MESH
F32 = jnp.float32
BF16 = jnp.bfloat16

NX, NY, NZ, NCORE = 4, 4, 16, 2
NROW, NCOL = 16, 8
CHIPS = NY * NZ

LEV = 10
PLANES = 100
POINTS = 2688
SPANS = 21
SPAN = 128
WAVES = 5
DEGREES = 160
LATS = 128
LINES = 4
TRACER_ROWS = 64
DIFFUSION = 0.07
COUPLE = 0.5

SEG = 256
SEGS = 11
PITCH = 112
PART = 25
PARTS = 4
PACKED = 8


def sincos(turns4):
    quarter = jnp.floor(turns4 + 0.5)
    y = (turns4 - quarter) * (0.5 * math.pi)
    y2 = y * y
    s = y * (1.0 + y2 * (-1.0 / 6 + y2 * (1.0 / 120 + y2 * (-1.0 / 5040 + y2 * (1.0 / 362880)))))
    c = 1.0 + y2 * (
        -0.5 + y2 * (1.0 / 24 + y2 * (-1.0 / 720 + y2 * (1.0 / 40320 + y2 * (-1.0 / 3628800))))
    )
    odd = (quarter == 1.0) | (quarter == 3.0)
    cos_sign = jnp.where((quarter == 1.0) | (quarter == 2.0), -1.0, 1.0)
    sin_sign = jnp.where((quarter == 2.0) | (quarter == 3.0), -1.0, 1.0)
    return cos_sign * jnp.where(odd, s, c), sin_sign * jnp.where(odd, c, s)


def dot_t(a, b):
    return lax.dot_general(a, b, (((1,), (1,)), ((), ())), preferred_element_type=F32)


def kernel(
    phys_hbm,
    poly_hbm,
    s2a_hbm,
    a2s_hbm,
    tracer_hbm,
    courant_hbm,
    water_hbm,
    points_hbm,
    air_hbm,
    sea_hbm,
    spectral_hbm,
    tracer_out_hbm,
    spectral_ref,
    tracer_out_ref,
    tracer_ref,
    courant_ref,
    water_ref,
    points_ref,
    air_ref,
    sea_ref,
    xv,
    xtop,
    pv,
    s2av,
    a2sv,
    x32,
    flux32,
    flux_got32,
    sst_got32,
    rows32,
    cells32,
    shifted,
    tops,
    bottoms,
    forced,
    table_c,
    table_s,
    waves,
    segments,
    product,
    fourier,
    row0,
    parts,
    packed32,
    out32,
    right_hand,
    got32,
    product2,
    product0,
    degrees_all,
    plane32,
    select_y,
    bulk,
    poly_t,
    flux_send,
    flux_got,
    down_send,
    up_send,
    cells_send,
    top1,
    bottom1,
    left1,
    right1,
    down2_send,
    up2_send,
    cells2_send,
    top2,
    bottom2,
    left2,
    right2,
    sst_send,
    sst_got,
    poly_got,
    core_send,
    core_got,
    outbox,
    inbox,
    plane_send,
    plane_got,
    mixed_send,
    mixed_got,
    local_sem,
    flux_ss,
    flux_rs,
    halo_ss,
    halo_rs,
    halo2_ss,
    halo2_rs,
    sst_ss,
    sst_rs,
    poly_ss,
    poly_rs,
    core_ss,
    core_rs,
    all_ss,
    all_rs,
    ring_ss,
    ring_rs,
    plane_ss,
    plane_rs,
    mixed_ss,
    mixed_rs,
    ready,
    ready2,
):
    x = lax.axis_index("grp")
    row = lax.axis_index("row")
    col = lax.axis_index("col")
    y = row // 4
    z = lax.rem(row, 4) * 4 + col // 2
    core = lax.rem(col, 2)
    strip = x * NROW + row

    def at(xx, yy, zz, cc):
        return (xx, yy * 4 + zz // 4, lax.rem(zz, 4) * 2 + cc)

    def remote(src, dst, ss, rs, device):
        return pltpu.make_async_remote_copy(
            src_ref=src, dst_ref=dst, send_sem=ss, recv_sem=rs, device_id=device, device_id_type=MESH
        )

    def strip_at(other):
        return (other // NROW, lax.rem(other, NROW), col)

    below = strip_at(lax.rem(strip + 1, NX * NROW))
    above = strip_at(lax.rem(strip + NX * NROW - 1, NX * NROW))
    band = [(x, row, lax.rem(col + i, NCOL)) for i in range(1, NCOL)]
    after = band[0]
    before = band[-1]
    z_ring = [
        at(x, y, lax.rem(z + i, NZ), core)
        for i in (8, 7, 9, 6, 10, 5, 11, 4, 12, 3, 13, 2, 14, 1, 15)
    ]
    y_ring = [at(x, lax.rem(y + i, NY), z, core) for i in range(1, NY)]
    x_ring = [at(lax.rem(x + i, NX), y, z, core) for i in range(1, NX)]
    sibling = at(x, y, z, 1 - core)

    moves = [
        (phys_hbm, xv),
        (poly_hbm, pv),
        (a2s_hbm, a2sv),
        (s2a_hbm, s2av),
        (points_hbm, points_ref),
        (phys_hbm.at[0, pl.ds(0, 32)], xtop),
        (tracer_hbm, tracer_ref),
        (courant_hbm, courant_ref),
        (water_hbm, water_ref),
        (air_hbm, air_ref),
        (sea_hbm, sea_ref),
    ]
    ins = [
        pltpu.make_async_copy(source, target, local_sem.at[i])
        for i, (source, target) in enumerate(moves)
    ]
    for i in (4, 5, 6, 7, 8, 0, 9, 2, 10, 3, 1):
        ins[i].start()
    barrier = pltpu.get_barrier_semaphore()
    greeted = band + [below, above, sibling] + x_ring + y_ring + z_ring
    for device in greeted:
        pl.semaphore_signal(barrier, inc=1, device_id=device, device_id_type=MESH)

    own = strip * NCOL + col
    ins[4].wait()
    n = points_ref[own]
    lane = lax.broadcasted_iota(jnp.int32, (1, SPAN), 1)

    ins[5].wait()
    x32[...] = xtop[...].astype(F32)
    flux32[...] = jnp.zeros_like(flux32)
    for b in range(SPANS):
        live = lane + b * SPAN < n
        for q in range(2):
            line = x32[(q + 1) * LEV : (q + 1) * LEV + 1, b * SPAN : (b + 1) * SPAN]
            flux32[q * 24 + b : q * 24 + b + 1, :] = jnp.where(live, line, 0.0)
    flux_send[...] = flux32[...].astype(BF16)
    flux_got[pl.ds(col, 1)] = flux_send[...][None]

    for i in (6, 7, 8):
        ins[i].wait()
    wet = water_ref[...].astype(F32)
    for i in range(16):
        cells32[96 + 4 * i : 100 + 4 * i, :] = wet
    cells32[0:64, :] = tracer_ref[...]
    cells32[64:96, :] = courant_ref[32:64, :]
    cells_send[...] = cells32[...].astype(BF16)
    rows32[...] = jnp.zeros_like(rows32)
    rows32[0:16, :] = tracer_ref[pl.ds(3, 16, stride=4), :]
    rows32[16:24, :] = courant_ref[pl.ds(3, 8, stride=4), :]
    rows32[24:25, :] = wet[3:4, :]
    down_send[...] = rows32[...].astype(BF16)
    rows32[0:16, :] = tracer_ref[pl.ds(0, 16, stride=4), :]
    rows32[24:25, :] = wet[0:1, :]
    up_send[...] = rows32[...].astype(BF16)

    pl.semaphore_wait(barrier, len(greeted))
    flux_copies = [
        remote(flux_send, flux_got.at[col], flux_ss.at[i], flux_rs.at[i], device)
        for i, device in enumerate(band)
    ]
    halo_copies = [
        remote(down_send, top1, halo_ss.at[0], halo_rs.at[0], below),
        remote(up_send, bottom1, halo_ss.at[1], halo_rs.at[1], above),
        remote(cells_send, left1, halo_ss.at[2], halo_rs.at[2], after),
        remote(cells_send, right1, halo_ss.at[3], halo_rs.at[3], before),
    ]
    for copy in flux_copies + halo_copies:
        copy.start()
    for device in y_ring:
        pl.semaphore_signal(ready, inc=1, device_id=device, device_id_type=MESH)

    shape = (WAVES, 48, SPAN)
    k_of = lax.broadcasted_iota(jnp.int32, shape, 0)
    p_row = lax.broadcasted_iota(jnp.int32, shape, 1)
    d_of = lax.broadcasted_iota(jnp.int32, shape, 2)
    owner = (d_of & 3) * 32 + ((d_of >> 2) & 15) * 2 + (d_of >> 6)
    orders = owner * WAVES + k_of
    places = jnp.where(
        p_row < 16, p_row, jnp.where(p_row < 32, (p_row - 16) * 16, (p_row - 32) * SEG)
    )
    count = jnp.full(shape, n, jnp.int32).astype(F32)
    inverse = 1.0 / count
    turns = orders.astype(F32) * places.astype(F32)
    phase = turns - jnp.floor(turns * inverse) * count
    phase = jnp.where(phase < 0.0, phase + count, phase)
    phase = jnp.where(phase >= count, phase - count, phase)
    cosine, sine = sincos(phase * (4.0 * inverse))
    table_c[...] = cosine
    table_s[...] = -sine

    def fill_waves(a, _):
        start = pl.multiple_of(a * 16, 16)
        for k in range(WAVES):
            ac = table_c[k, pl.ds(16 + a, 1), :]
            as_ = table_s[k, pl.ds(16 + a, 1), :]
            bc = table_c[k, 0:16, :]
            bs = table_s[k, 0:16, :]
            waves[k, pl.ds(start, 16), 0:SPAN] = (ac * bc - as_ * bs).astype(BF16)
            waves[k, pl.ds(start, 16), SPAN : 2 * SPAN] = (ac * bs + as_ * bc).astype(BF16)
        return 0

    lax.fori_loop(0, 16, fill_waves, 0)

    ins[0].wait()
    for i in range(SEGS):
        width = min(SEG, POINTS - i * SEG)
        pos = i * SEG + lax.broadcasted_iota(jnp.int32, (1, width), 1)
        values = xv[0, :, i * SEG : i * SEG + width].astype(F32)
        values = jnp.where(pos < n, values, 0.0).astype(BF16)
        segments[i * PITCH + 96 : (i + 1) * PITCH, :] = jnp.zeros((16, SEG), BF16)
        if width < SEG:
            segments[i * PITCH : (i + 1) * PITCH, width:SEG] = jnp.zeros((PITCH, SEG - width), BF16)
        segments[i * PITCH : i * PITCH + PLANES, 0:width] = values

    inverse_row = 1.0 / jnp.full((1, SPAN), n, jnp.int32).astype(F32)
    d_row = lax.broadcasted_iota(jnp.int32, (1, SPAN), 1)
    owner_row = (d_row & 3) * 32 + ((d_row >> 2) & 15) * 2 + (d_row >> 6)

    def scale_of(k):
        return jnp.where(2 * (owner_row * WAVES + k) < n, inverse_row, 0.0)

    def transform(k, _):
        product[...] = jnp.dot(segments[...], waves[k], preferred_element_type=F32)
        real = jnp.zeros((PITCH, SPAN), F32)
        imag = jnp.zeros((PITCH, SPAN), F32)
        for i in range(SEGS):
            wc = table_c[k, 32 + i : 33 + i, :]
            ws = table_s[k, 32 + i : 33 + i, :]
            yc = product[i * PITCH : (i + 1) * PITCH, 0:SPAN]
            ys = product[i * PITCH : (i + 1) * PITCH, SPAN : 2 * SPAN]
            real = real + (yc * wc - ys * ws)
            imag = imag + (yc * ws + ys * wc)
        scale = scale_of(k)
        fourier[k, 0] = real * scale
        fourier[k, 1] = imag * scale
        return 0

    lax.fori_loop(0, WAVES, transform, 0)

    for c in range(2):
        for q in range(PARTS):
            r = c * PARTS + q
            parts[r, 120:128, :] = jnp.zeros((8, SPAN), F32)
            for k in range(WAVES):
                parts[r, k * PART : (k + 1) * PART, :] = fourier[
                    k, c, q * PART : (q + 1) * PART, :
                ]
            packed32[pl.ds(r, LATS, stride=PACKED), :] = parts[r].T

    half_rows = CHIPS * PACKED
    core_send[...] = packed32[pl.ds(pl.multiple_of((1 - core) * half_rows, 8), half_rows), :].astype(
        BF16
    )
    core_copy = remote(core_send, core_got, core_ss, core_rs, sibling)
    core_copy.start()
    mine = packed32[pl.ds(pl.multiple_of(core * half_rows, 8), half_rows), :].reshape(
        CHIPS, PACKED, SPAN
    )
    ins[2].wait()
    ins[9].wait()
    for copy in flux_copies:
        copy.wait_recv()
    flux_got32[...] = flux_got[...].astype(F32)
    two = lax.broadcasted_iota(jnp.int32, (16, SPAN), 0)
    forced[...] = jnp.zeros_like(forced)
    for line in range(LINES):
        total = jnp.zeros((16, SPAN), F32)
        for k in range(2):
            span = air_ref[0, k, line]
            source = lax.div(span, SPANS)
            block = lax.rem(span, SPANS)
            first = flux_got32[source, pl.ds(block, 1), :]
            second = flux_got32[source, pl.ds(block + 24, 1), :]
            pair = jnp.where(
                two == 0, jnp.broadcast_to(first, (16, SPAN)), jnp.broadcast_to(second, (16, SPAN))
            )
            total = total + dot_t(pair.astype(BF16), a2sv[line, k])
        forced[line : line + 1, :] = COUPLE * total[0:1, :]
        forced[32 + line : 33 + line, :] = COUPLE * total[1:2, :]

    has_top = jnp.where(strip > 0, 1.0, 0.0).astype(F32)
    has_bottom = jnp.where(strip < NX * NROW - 1, 1.0, 0.0).astype(F32)
    has_left = jnp.where(col > 0, 1.0, 0.0).astype(F32)
    has_right = jnp.where(col < NCOL - 1, 1.0, 0.0).astype(F32)
    line_of = lax.broadcasted_iota(jnp.int32, (TRACER_ROWS, SPAN), 0) & 3
    lane_of = lax.broadcasted_iota(jnp.int32, (TRACER_ROWS, SPAN), 1)

    def from_above(value, edge):
        shifted[8:72, :] = value
        tops[pl.ds(0, 16, stride=4), :] = edge
        return jnp.where(line_of == 0, tops[...], shifted[7:71, :])

    def from_below(value, edge):
        shifted[8:72, :] = value
        bottoms[pl.ds(3, 16, stride=4), :] = edge
        return jnp.where(line_of == 3, bottoms[...], shifted[9:73, :])

    def from_left(value, tile):
        return jnp.where(lane_of == 0, pltpu.roll(tile, 1, 1), pltpu.roll(value, 1, 1))

    def from_right(value, tile):
        return jnp.where(
            lane_of == SPAN - 1, pltpu.roll(tile, SPAN - 1, 1), pltpu.roll(value, SPAN - 1, 1)
        )

    def twice(value):
        return jnp.concatenate([value, value], axis=0)

    for copy in halo_copies:
        copy.wait_recv()
    shifted[...] = jnp.zeros_like(shifted)
    tops[...] = jnp.zeros_like(tops)
    bottoms[...] = jnp.zeros_like(bottoms)
    top = top1[...].astype(F32) * has_top
    bottom = bottom1[...].astype(F32) * has_bottom
    left = left1[...].astype(F32) * has_left
    right = right1[...].astype(F32) * has_right
    wet64 = cells32[96:160, :]
    east = twice(courant_ref[0:32, :])
    north = twice(courant_ref[32:64, :])
    east_up = from_above(east, twice(top[16:24, :]))
    north_left = from_left(north, twice(left[64:96, :]))
    pair_up = wet64 * from_above(wet64, jnp.broadcast_to(top[24:25, :], (16, SPAN)))
    pair_down = wet64 * from_below(wet64, jnp.broadcast_to(bottom[24:25, :], (16, SPAN)))
    pair_left = wet64 * from_left(wet64, left[96:160, :])
    pair_right = wet64 * from_right(wet64, right[96:160, :])

    def flow(pair, speed, low, high):
        return pair * (
            jnp.maximum(speed, 0.0) * low
            + jnp.minimum(speed, 0.0) * high
            - DIFFUSION * (high - low)
        )

    def advance(q, edge_top, edge_bottom, tile_left, tile_right):
        spread = (
            flow(pair_down, east, q, from_below(q, edge_bottom))
            - flow(pair_up, east_up, from_above(q, edge_top), q)
            + flow(pair_right, north, q, from_right(q, tile_right))
            - flow(pair_left, north_left, from_left(q, tile_left), q)
        )
        return q + wet64 * (forced[...] - spread)

    state = advance(
        tracer_ref[...], top[0:16, :], bottom[0:16, :], left[0:64, :], right[0:64, :]
    )
    tracer_out_ref[...] = state
    cells2_send[...] = state.astype(BF16)
    down2_send[...] = tracer_out_ref[pl.ds(3, 16, stride=4), :].astype(BF16)
    up2_send[...] = tracer_out_ref[pl.ds(0, 16, stride=4), :].astype(BF16)
    halo2_copies = [
        remote(down2_send, top2, halo2_ss.at[0], halo2_rs.at[0], below),
        remote(up2_send, bottom2, halo2_ss.at[1], halo2_rs.at[1], above),
        remote(cells2_send, left2, halo2_ss.at[2], halo2_rs.at[2], after),
        remote(cells2_send, right2, halo2_ss.at[3], halo2_rs.at[3], before),
    ]
    for copy in halo2_copies:
        copy.start()

    core_copy.wait_recv()
    theirs = core_got[...].astype(F32).reshape(CHIPS, PACKED, SPAN)
    is_first = core == 0
    out32[:, 0:PACKED, :] = jnp.where(is_first, mine, theirs)
    out32[:, PACKED : 2 * PACKED, :] = jnp.where(is_first, theirs, mine)
    outbox[...] = out32[...].astype(BF16)
    pl.semaphore_wait(ready, NY - 1)
    for device in x_ring:
        pl.semaphore_signal(ready2, inc=1, device_id=device, device_id_type=MESH)

    def post_group(j):
        yy = lax.rem(y + j, NY)

        def post(i, _):
            zz = lax.rem(z + i, NZ)
            remote(
                outbox.at[zz * NY + yy],
                inbox.at[0, y, z],
                all_ss,
                all_rs.at[j],
                at(x, yy, zz, core),
            ).start()
            return 0

        lax.fori_loop(1, NZ, post, 0)
        if j:
            post(0, 0)

    post_group(0)
    post_group(1)
    inbox[0, pl.ds(y, 1), pl.ds(z, 1)] = outbox[pl.ds(z * NY + y, 1)][None]

    ins[1].wait()
    for k in range(WAVES):
        turned = pv[k].astype(F32).T.astype(BF16)
        for g in range(NX):
            poly_t[g, k * DEGREES : (k + 1) * DEGREES, :] = turned[g * DEGREES : (g + 1) * DEGREES]
    poly_got[0] = poly_t[x]
    poly_copies = [
        remote(
            poly_t.at[lax.rem(x + i, NX)],
            poly_got.at[i],
            poly_ss.at[i - 1],
            poly_rs.at[i - 1],
            x_ring[i - 1],
        )
        for i in range(1, NX)
    ]
    for copy in poly_copies:
        copy.start()

    rows_b = lax.broadcasted_iota(jnp.int32, (8 * SPAN, SPAN), 0)
    lanes_b = lax.broadcasted_iota(jnp.int32, (8 * SPAN, SPAN), 1)
    lane_in = rows_b & 127
    wanted = (rows_b >> 8) * 32 + (lane_in >> 3) * 2 + ((rows_b >> 7) & 1)
    chosen = ((lane_in & 7) == core * 4 + y) & (lanes_b == wanted)
    select_y[...] = jnp.where(chosen, 1.0, 0.0).astype(BF16)

    for copy in halo2_copies:
        copy.wait_recv()
    state = advance(
        tracer_out_ref[...],
        top2[...].astype(F32) * has_top,
        bottom2[...].astype(F32) * has_bottom,
        left2[...].astype(F32) * has_left,
        right2[...].astype(F32) * has_right,
    )
    tracer_out_ref[...] = state
    tracer_leave = pltpu.make_async_copy(tracer_out_ref, tracer_out_hbm, local_sem.at[11])
    tracer_leave.start()
    sst_send[...] = state[0:16, :].astype(BF16)
    sst_got[pl.ds(col, 1)] = sst_send[...][None]
    sst_copies = [
        remote(sst_send, sst_got.at[col], sst_ss.at[i], sst_rs.at[i], device)
        for i, device in enumerate(band)
    ]
    for copy in sst_copies:
        copy.start()

    next_x = x_ring[0]
    last_x = x_ring[-1]
    ring_right = []
    ring_left = []
    ring_on = []

    def circulate(j):
        count = NZ - 1 if j == 0 else NZ
        arrived = remote(
            outbox.at[pl.ds(0, count)],
            inbox.at[0, 0, pl.ds(0, count)],
            all_ss,
            all_rs.at[j],
            sibling,
        )
        arrived.wait_recv()
        yy = lax.rem(y + NY - j, NY)
        to_right = remote(
            inbox.at[0, yy], inbox.at[1, yy], ring_ss.at[0, j], ring_rs.at[0, j], next_x
        )
        to_left = remote(
            inbox.at[0, yy], inbox.at[3, yy], ring_ss.at[1, j], ring_rs.at[1, j], last_x
        )
        to_right.start()
        to_left.start()
        ring_right.append(to_right)
        ring_left.append(to_left)

    def pass_on(j):
        yy = lax.rem(y + NY - j, NY)
        ring_right[j].wait_recv()
        ring_left[j].wait_recv()
        slot, device = (1, next_x) if j % 2 == 0 else (3, last_x)
        copy = remote(
            inbox.at[slot, yy], inbox.at[2, yy], ring_ss.at[2, j], ring_rs.at[2, j], device
        )
        copy.start()
        ring_on.append(copy)

    post_group(2)
    post_group(3)
    circulate(0)
    circulate(1)

    ins[3].wait()
    ins[10].wait()
    for copy in sst_copies:
        copy.wait_recv()
    sst_got32[...] = sst_got[...].astype(F32)
    row0[...] = jnp.zeros_like(row0)
    for b in range(SPANS):
        span = sea_ref[0, b]
        source = lax.div(span, LINES)
        line = lax.rem(span, LINES)
        warmth = jnp.broadcast_to(sst_got32[source, pl.ds(line, 1), :], (16, SPAN))
        sampled = dot_t(warmth.astype(BF16), s2av[0, b])[0:1, :]
        plane = x32[0:1, b * SPAN : (b + 1) * SPAN] + sampled
        plane = jnp.where(lane + b * SPAN < n, plane, 0.0)
        half = (b % 2) * SPAN
        row0[b // 2 : b // 2 + 1, half : half + SPAN] = plane
    surface = row0[...].astype(BF16)
    plane32[...] = jnp.zeros_like(plane32)
    for k in range(WAVES):
        part = jnp.dot(surface, waves[k], preferred_element_type=F32)
        wc = table_c[k, 32:48, :]
        ws = table_s[k, 32:48, :]
        yc = part[:, 0:SPAN]
        ys = part[:, SPAN : 2 * SPAN]
        scale = scale_of(k)
        plane32[2 * k : 2 * k + 1, :] = jnp.sum(yc * wc - ys * ws, axis=0, keepdims=True) * scale
        plane32[2 * k + 1 : 2 * k + 2, :] = (
            jnp.sum(yc * ws + ys * wc, axis=0, keepdims=True) * scale
        )

    plane_send[...] = plane32[...].astype(BF16)
    plane_got[pl.ds(z, 1)] = plane_send[...][None]
    for device in z_ring:
        remote(plane_send, plane_got.at[z], plane_ss, plane_rs, device).start()

    circulate(2)
    pass_on(0)
    circulate(3)
    pass_on(1)

    def many(copies, device):
        return remote(
            plane_got.at[pl.ds(0, copies)],
            plane_got.at[pl.ds(0, copies)],
            plane_ss,
            plane_rs,
            device,
        )

    pass_on(2)
    pass_on(3)
    def unpack(slot):
        got32[...] = inbox[slot].astype(F32).reshape(CHIPS * 2 * PACKED, SPAN)

        def spread_row(r, _):
            columns = pl.ds(pl.multiple_of(r * SPAN, SPAN), SPAN)
            right_hand[slot * LATS : (slot + 1) * LATS, columns] = got32[
                pl.ds(r, LATS, stride=PACKED), :
            ].astype(BF16)
            return 0

        lax.fori_loop(0, PACKED, spread_row, 0)

    unpack(0)
    many(NZ - 1, sibling).wait_recv()
    stretch = plane_got[...].astype(F32).reshape(NZ * 16, SPAN)
    stretch = pltpu.roll(stretch, lax.rem(SPAN - NY * z, SPAN), 1)
    place = lax.broadcasted_iota(jnp.int32, (16, SPAN), 1) >> 2
    mixed = jnp.zeros((16, SPAN), F32)
    for i in range(NZ):
        tile = stretch[i * 16 : (i + 1) * 16, :]
        low = pltpu.roll(tile, 8 * i, 1) if i else tile
        high = pltpu.roll(tile, (8 * i + 4 + CHIPS) % SPAN, 1)
        mixed = jnp.where(place == 2 * i, low, jnp.where(place == 2 * i + 1, high, mixed))
    mixed = mixed.astype(BF16)
    mixed_send[...] = mixed
    pl.semaphore_wait(ready2, NX - 1)
    mixed_got[pl.ds(y * 2 + core, 1)] = mixed[None]
    steps = [(i // 8, (i // 2) % 4, i % 2) for i in range(1, NX * NY * NCORE)]
    hops = (0, 1, 2, 1)
    for dx, dy, dc in sorted(steps, key=lambda t: -hops[t[0]] - hops[t[1]]):
        cc = 1 - core if dc else core
        remote(
            mixed_send,
            mixed_got.at[dx * 8 + y * 2 + core],
            mixed_ss,
            mixed_rs,
            at(lax.rem(x + dx, NX), lax.rem(y + dy, NY), z, cc),
        ).start()

    unpack(1)
    unpack(3)
    for copy in poly_copies:
        copy.wait_recv()
    degrees = jnp.concatenate([poly_got[i] for i in range(NX)], axis=1)
    for copy in ring_on:
        copy.wait_recv()
    unpack(2)

    degrees_all[...] = degrees

    def legendre(i, _):
        columns = pl.ds(pl.multiple_of(i * 2 * SPAN, 2 * SPAN), 2 * SPAN)
        product2[:, columns] = jnp.dot(
            degrees_all[...], right_hand[:, columns], preferred_element_type=F32
        )
        return 0

    lax.fori_loop(0, 4, legendre, 0)
    lanes = lax.broadcasted_iota(jnp.int32, (DEGREES, SPAN), 1)
    for c in range(2):
        for k in range(WAVES):
            total = jnp.zeros((DEGREES, SPAN), F32)
            for q in range(PARTS):
                r = c * PARTS + q
                block = product2[k * DEGREES : (k + 1) * DEGREES, r * SPAN : (r + 1) * SPAN]
                turn = (PART * (q - k)) % SPAN
                if turn:
                    block = pltpu.roll(block, turn, 1)
                keep = (lanes >= q * PART) & (lanes < (q + 1) * PART)
                total = jnp.where(keep, block, total)
            bulk[c, k] = total

    remote(
        mixed_got.at[pl.ds(0, 31)], mixed_got.at[pl.ds(0, 31)], mixed_ss, mixed_rs, sibling
    ).wait_recv()
    stacked = jnp.concatenate(
        [
            jnp.concatenate([mixed_got[slot * 8 + i] for i in range(8)], axis=1)
            for slot in range(NX)
        ],
        axis=0,
    )
    sorted_rows = jnp.dot(stacked, select_y[...], preferred_element_type=F32).astype(BF16)
    surface_rows = jnp.concatenate(
        [sorted_rows[slot * 16 : (slot + 1) * 16, :] for slot in range(NX)], axis=1
    )
    surface_rows = jnp.concatenate(
        [surface_rows, jnp.zeros((SPAN - 16, NX * LATS), BF16)], axis=0
    )
    product0[...] = dot_t(degrees, surface_rows)
    leaves = [tracer_leave]
    for c in range(2):
        for k in range(WAVES):
            block = product0[k * DEGREES : (k + 1) * DEGREES, :]
            turn = (-(2 * k + c)) % SPAN
            if turn:
                block = pltpu.roll(block, turn, 1)
            total = jnp.where(lanes == 0, block, bulk[c, k])
            spectral_ref[c, k] = total[:, 0:PLANES].astype(BF16)
        leave = pltpu.make_async_copy(
            spectral_ref.at[c], spectral_hbm.at[c], local_sem.at[12 + c]
        )
        leave.start()
        leaves.append(leave)

    for copy in flux_copies + halo_copies + halo2_copies + sst_copies + poly_copies:
        copy.wait_send()
    core_copy.wait_send()
    remote(
        outbox.at[pl.ds(0, CHIPS - 1)],
        outbox.at[pl.ds(0, CHIPS - 1)],
        all_ss,
        all_rs.at[0],
        sibling,
    ).wait_send()
    many(NZ - 1, sibling).wait_send()
    remote(
        mixed_got.at[pl.ds(0, 31)], mixed_got.at[pl.ds(0, 31)], mixed_ss, mixed_rs, sibling
    ).wait_send()
    for copy in ring_right + ring_left + ring_on:
        copy.wait_send()
    for copy in leaves:
        copy.wait()


def local(
    physical_values,
    samples_per_parallel,
    associated_polynomials,
    heat_salt_anomalies,
    courant_numbers,
    water_indicator,
    air_to_sea_coefficients,
    air_partner_span,
    sea_to_air_coefficients,
    sea_partner_span,
):
    hbm = pl.BlockSpec(memory_space=pltpu.HBM)
    dma = pltpu.SemaphoreType.DMA
    scratch = [
        pltpu.VMEM((2, WAVES, DEGREES, PLANES), BF16),
        pltpu.VMEM((TRACER_ROWS, SPAN), F32),
        pltpu.VMEM((TRACER_ROWS, SPAN), F32),
        pltpu.VMEM((TRACER_ROWS, SPAN), F32),
        pltpu.VMEM((LINES, SPAN), jnp.int32),
        pltpu.SMEM((512,), jnp.int32),
        pltpu.SMEM((1, 2, LINES), jnp.int32),
        pltpu.SMEM((1, SPANS), jnp.int32),
        pltpu.VMEM((1, PLANES, POINTS), BF16),
        pltpu.VMEM((32, POINTS), BF16),
        pltpu.VMEM((WAVES, LATS, NX * DEGREES), BF16),
        pltpu.VMEM((1, SPANS, SPAN, SPAN), BF16),
        pltpu.VMEM((LINES, 2, SPAN, SPAN), BF16),
        pltpu.VMEM((32, POINTS), F32),
        pltpu.VMEM((48, SPAN), F32),
        pltpu.VMEM((NCOL, 48, SPAN), F32),
        pltpu.VMEM((NCOL, 16, SPAN), F32),
        pltpu.VMEM((32, SPAN), F32),
        pltpu.VMEM((160, SPAN), F32),
        pltpu.VMEM((80, SPAN), F32),
        pltpu.VMEM((TRACER_ROWS, SPAN), F32),
        pltpu.VMEM((TRACER_ROWS, SPAN), F32),
        pltpu.VMEM((TRACER_ROWS, SPAN), F32),
        pltpu.VMEM((WAVES, 48, SPAN), F32),
        pltpu.VMEM((WAVES, 48, SPAN), F32),
        pltpu.VMEM((WAVES, SEG, 2 * SPAN), BF16),
        pltpu.VMEM((SEGS * PITCH, SEG), BF16),
        pltpu.VMEM((SEGS * PITCH, 2 * SPAN), F32),
        pltpu.VMEM((WAVES, 2, PITCH, SPAN), F32),
        pltpu.VMEM((16, SEG), F32),
        pltpu.VMEM((PACKED, SPAN, SPAN), F32),
        pltpu.VMEM((LATS * PACKED, SPAN), F32),
        pltpu.VMEM((CHIPS, 2 * PACKED, SPAN), F32),
        pltpu.VMEM((NX * LATS, PACKED * SPAN), BF16),
        pltpu.VMEM((LATS * PACKED, SPAN), F32),
        pltpu.VMEM((WAVES * DEGREES, PACKED * SPAN), F32),
        pltpu.VMEM((WAVES * DEGREES, SPAN), F32),
        pltpu.VMEM((WAVES * DEGREES, NX * LATS), BF16),
        pltpu.VMEM((16, SPAN), F32),
        pltpu.VMEM((8 * SPAN, SPAN), BF16),
        pltpu.VMEM((2, WAVES, DEGREES, SPAN), F32),
        pltpu.VMEM((NX, WAVES * DEGREES, LATS), BF16),
        pltpu.VMEM((48, SPAN), BF16),
        pltpu.VMEM((NCOL, 48, SPAN), BF16),
        pltpu.VMEM((32, SPAN), BF16),
        pltpu.VMEM((32, SPAN), BF16),
        pltpu.VMEM((160, SPAN), BF16),
        pltpu.VMEM((32, SPAN), BF16),
        pltpu.VMEM((32, SPAN), BF16),
        pltpu.VMEM((160, SPAN), BF16),
        pltpu.VMEM((160, SPAN), BF16),
        pltpu.VMEM((16, SPAN), BF16),
        pltpu.VMEM((16, SPAN), BF16),
        pltpu.VMEM((64, SPAN), BF16),
        pltpu.VMEM((16, SPAN), BF16),
        pltpu.VMEM((16, SPAN), BF16),
        pltpu.VMEM((64, SPAN), BF16),
        pltpu.VMEM((64, SPAN), BF16),
        pltpu.VMEM((16, SPAN), BF16),
        pltpu.VMEM((NCOL, 16, SPAN), BF16),
        pltpu.VMEM((NX, WAVES * DEGREES, LATS), BF16),
        pltpu.VMEM((CHIPS * PACKED, SPAN), BF16),
        pltpu.VMEM((CHIPS * PACKED, SPAN), BF16),
        pltpu.VMEM((CHIPS, 2 * PACKED, SPAN), BF16),
        pltpu.VMEM((NX, NY, NZ, 2 * PACKED, SPAN), BF16),
        pltpu.VMEM((16, SPAN), BF16),
        pltpu.VMEM((NZ, 16, SPAN), BF16),
        pltpu.VMEM((16, SPAN), BF16),
        pltpu.VMEM((NX * NY * NCORE, 16, SPAN), BF16),
        dma((14,)),
        dma((NCOL - 1,)),
        dma((NCOL - 1,)),
        dma((4,)),
        dma((4,)),
        dma((4,)),
        dma((4,)),
        dma((NCOL - 1,)),
        dma((NCOL - 1,)),
        dma((NX - 1,)),
        dma((NX - 1,)),
        dma,
        dma,
        dma,
        dma((NY,)),
        dma((3, NY)),
        dma((3, NY)),
        dma,
        dma,
        dma,
        dma,
        pltpu.SemaphoreType.REGULAR,
        pltpu.SemaphoreType.REGULAR,
    ]
    spectral, tracers = pl.pallas_call(
        kernel,
        out_shape=(
            jax.ShapeDtypeStruct((2, WAVES, DEGREES, PLANES), BF16),
            jax.ShapeDtypeStruct((TRACER_ROWS, SPAN), F32),
        ),
        in_specs=[hbm] * 10,
        out_specs=(hbm, hbm),
        scratch_shapes=scratch,
        compiler_params=pltpu.CompilerParams(
            collective_id=0, has_side_effects=True, vmem_limit_bytes=64 * 2**20
        ),
        cost_estimate=pl.CostEstimate(
            flops=1_000_000_000, bytes_accessed=3_000_000, transcendentals=0
        ),
    )(
        physical_values,
        associated_polynomials,
        sea_to_air_coefficients,
        air_to_sea_coefficients,
        heat_salt_anomalies.reshape(TRACER_ROWS, SPAN),
        courant_numbers.reshape(TRACER_ROWS, SPAN),
        water_indicator,
        samples_per_parallel,
        jnp.transpose(air_partner_span, (1, 2, 0)),
        sea_partner_span,
    )
    return spectral.transpose(3, 0, 1, 2), tracers.reshape(2, 8, LINES, SPAN)


def solution(mesh):
    placed = (
        P(("grp", "row", "col"), None, None),
        P(),
        P(("row", "col"), "grp", None),
        P(None, None, ("grp", "row"), "col"),
        P(None, None, ("grp", "row"), "col"),
        P(("grp", "row"), "col"),
        P(("grp", "row"), None, "col", None),
        P(("grp", "row"), "col", None),
        P(("grp", "row", "col"), None, None, None),
        P(("grp", "row", "col"), None),
    )
    return jax.shard_map(
        local,
        mesh=mesh,
        in_specs=placed,
        out_specs=(P(None, None, ("row", "col"), "grp"), P(None, None, ("grp", "row"), "col")),
        check_vma=False,
    )
```

```python
import math

import jax
import jax.numpy as jnp
from jax import lax
from jax.experimental import pallas as pl
from jax.experimental.pallas import tpu as pltpu
from jax.sharding import PartitionSpec as P

MESH = pl.DeviceIdType.MESH
F32 = jnp.float32
BF16 = jnp.bfloat16

NX, NY, NZ, NCORE = 4, 4, 16, 2
NROW, NCOL = 16, 8
CHIPS = NY * NZ

LEV = 10
PLANES = 100
POINTS = 2688
SPANS = 21
SPAN = 128
WAVES = 5
DEGREES = 160
LATS = 128
LINES = 4
TRACER_ROWS = 64
DIFFUSION = 0.07
COUPLE = 0.5

SEG = 256
SEGS = 11
PITCH = 112
PART = 25
PARTS = 4
PACKED = 8


def sincos(turns4):
    quarter = jnp.floor(turns4 + 0.5)
    y = (turns4 - quarter) * (0.5 * math.pi)
    y2 = y * y
    s = y * (1.0 + y2 * (-1.0 / 6 + y2 * (1.0 / 120 + y2 * (-1.0 / 5040 + y2 * (1.0 / 362880)))))
    c = 1.0 + y2 * (
        -0.5 + y2 * (1.0 / 24 + y2 * (-1.0 / 720 + y2 * (1.0 / 40320 + y2 * (-1.0 / 3628800))))
    )
    odd = (quarter == 1.0) | (quarter == 3.0)
    cos_sign = jnp.where((quarter == 1.0) | (quarter == 2.0), -1.0, 1.0)
    sin_sign = jnp.where((quarter == 2.0) | (quarter == 3.0), -1.0, 1.0)
    return cos_sign * jnp.where(odd, s, c), sin_sign * jnp.where(odd, c, s)


def dot_t(a, b):
    return lax.dot_general(a, b, (((1,), (1,)), ((), ())), preferred_element_type=F32)


def kernel(
    phys_hbm,
    poly_hbm,
    s2a_hbm,
    a2s_hbm,
    tracer_hbm,
    courant_hbm,
    water_hbm,
    points_hbm,
    air_hbm,
    sea_hbm,
    spectral_hbm,
    tracer_out_hbm,
    spectral_ref,
    tracer_out_ref,
    tracer_ref,
    courant_ref,
    water_ref,
    points_ref,
    air_ref,
    sea_ref,
    xv,
    xtop,
    pv,
    s2av,
    a2sv,
    x32,
    flux32,
    flux_got32,
    sst_got32,
    rows32,
    cells32,
    shifted,
    tops,
    bottoms,
    forced,
    table_c,
    table_s,
    waves,
    segments,
    product,
    fourier,
    row0,
    parts,
    packed32,
    out32,
    right_hand,
    got32,
    product2,
    product0,
    degrees_all,
    plane32,
    select_y,
    bulk,
    poly_t,
    flux_send,
    flux_got,
    down_send,
    up_send,
    cells_send,
    top1,
    bottom1,
    left1,
    right1,
    down2_send,
    up2_send,
    cells2_send,
    top2,
    bottom2,
    left2,
    right2,
    sst_send,
    sst_got,
    poly_got,
    core_send,
    core_got,
    outbox,
    inbox,
    plane_send,
    plane_got,
    mixed_send,
    mixed_got,
    local_sem,
    flux_ss,
    flux_rs,
    halo_ss,
    halo_rs,
    halo2_ss,
    halo2_rs,
    sst_ss,
    sst_rs,
    poly_ss,
    poly_rs,
    core_ss,
    core_rs,
    all_ss,
    all_rs,
    ring_ss,
    ring_rs,
    plane_ss,
    plane_rs,
    mixed_ss,
    mixed_rs,
    ready,
    ready2,
):
    x = lax.axis_index("grp")
    row = lax.axis_index("row")
    col = lax.axis_index("col")
    y = row // 4
    z = lax.rem(row, 4) * 4 + col // 2
    core = lax.rem(col, 2)
    strip = x * NROW + row

    def at(xx, yy, zz, cc):
        return (xx, yy * 4 + zz // 4, lax.rem(zz, 4) * 2 + cc)

    def remote(src, dst, ss, rs, device):
        return pltpu.make_async_remote_copy(
            src_ref=src, dst_ref=dst, send_sem=ss, recv_sem=rs, device_id=device, device_id_type=MESH
        )

    def strip_at(other):
        return (other // NROW, lax.rem(other, NROW), col)

    below = strip_at(lax.rem(strip + 1, NX * NROW))
    above = strip_at(lax.rem(strip + NX * NROW - 1, NX * NROW))
    band = [(x, row, lax.rem(col + i, NCOL)) for i in range(1, NCOL)]
    after = band[0]
    before = band[-1]
    z_ring = [
        at(x, y, lax.rem(z + i, NZ), core)
        for i in (8, 7, 9, 6, 10, 5, 11, 4, 12, 3, 13, 2, 14, 1, 15)
    ]
    y_ring = [at(x, lax.rem(y + i, NY), z, core) for i in range(1, NY)]
    x_ring = [at(lax.rem(x + i, NX), y, z, core) for i in range(1, NX)]
    sibling = at(x, y, z, 1 - core)

    moves = [
        (phys_hbm, xv),
        (poly_hbm, pv),
        (a2s_hbm, a2sv),
        (s2a_hbm, s2av),
        (points_hbm, points_ref),
        (phys_hbm.at[0, pl.ds(0, 32)], xtop),
        (tracer_hbm, tracer_ref),
        (courant_hbm, courant_ref),
        (water_hbm, water_ref),
        (air_hbm, air_ref),
        (sea_hbm, sea_ref),
    ]
    ins = [
        pltpu.make_async_copy(source, target, local_sem.at[i])
        for i, (source, target) in enumerate(moves)
    ]
    for i in (4, 5, 6, 7, 8, 0, 9, 2, 10, 3, 1):
        ins[i].start()
    barrier = pltpu.get_barrier_semaphore()
    greeted = band + [below, above, sibling] + x_ring + y_ring + z_ring
    for device in greeted:
        pl.semaphore_signal(barrier, inc=1, device_id=device, device_id_type=MESH)

    own = strip * NCOL + col
    ins[4].wait()
    n = points_ref[own]
    lane = lax.broadcasted_iota(jnp.int32, (1, SPAN), 1)

    ins[5].wait()
    x32[...] = xtop[...].astype(F32)
    flux32[...] = jnp.zeros_like(flux32)
    for b in range(SPANS):
        live = lane + b * SPAN < n
        for q in range(2):
            line = x32[(q + 1) * LEV : (q + 1) * LEV + 1, b * SPAN : (b + 1) * SPAN]
            flux32[q * 24 + b : q * 24 + b + 1, :] = jnp.where(live, line, 0.0)
    flux_send[...] = flux32[...].astype(BF16)
    flux_got[pl.ds(col, 1)] = flux_send[...][None]

    for i in (6, 7, 8):
        ins[i].wait()
    wet = water_ref[...].astype(F32)
    for i in range(16):
        cells32[96 + 4 * i : 100 + 4 * i, :] = wet
    cells32[0:64, :] = tracer_ref[...]
    cells32[64:96, :] = courant_ref[32:64, :]
    cells_send[...] = cells32[...].astype(BF16)
    rows32[...] = jnp.zeros_like(rows32)
    rows32[0:16, :] = tracer_ref[pl.ds(3, 16, stride=4), :]
    rows32[16:24, :] = courant_ref[pl.ds(3, 8, stride=4), :]
    rows32[24:25, :] = wet[3:4, :]
    down_send[...] = rows32[...].astype(BF16)
    rows32[0:16, :] = tracer_ref[pl.ds(0, 16, stride=4), :]
    rows32[24:25, :] = wet[0:1, :]
    up_send[...] = rows32[...].astype(BF16)

    pl.semaphore_wait(barrier, len(greeted))
    flux_copies = [
        remote(flux_send, flux_got.at[col], flux_ss.at[i], flux_rs.at[i], device)
        for i, device in enumerate(band)
    ]
    halo_copies = [
        remote(down_send, top1, halo_ss.at[0], halo_rs.at[0], below),
        remote(up_send, bottom1, halo_ss.at[1], halo_rs.at[1], above),
        remote(cells_send, left1, halo_ss.at[2], halo_rs.at[2], after),
        remote(cells_send, right1, halo_ss.at[3], halo_rs.at[3], before),
    ]
    for copy in flux_copies + halo_copies:
        copy.start()
    for device in y_ring:
        pl.semaphore_signal(ready, inc=1, device_id=device, device_id_type=MESH)

    shape = (WAVES, 48, SPAN)
    k_of = lax.broadcasted_iota(jnp.int32, shape, 0)
    p_row = lax.broadcasted_iota(jnp.int32, shape, 1)
    d_of = lax.broadcasted_iota(jnp.int32, shape, 2)
    owner = (d_of & 3) * 32 + ((d_of >> 2) & 15) * 2 + (d_of >> 6)
    orders = owner * WAVES + k_of
    places = jnp.where(
        p_row < 16, p_row, jnp.where(p_row < 32, (p_row - 16) * 16, (p_row - 32) * SEG)
    )
    count = jnp.full(shape, n, jnp.int32).astype(F32)
    inverse = 1.0 / count
    turns = orders.astype(F32) * places.astype(F32)
    phase = turns - jnp.floor(turns * inverse) * count
    phase = jnp.where(phase < 0.0, phase + count, phase)
    phase = jnp.where(phase >= count, phase - count, phase)
    cosine, sine = sincos(phase * (4.0 * inverse))
    table_c[...] = cosine
    table_s[...] = -sine

    def fill_waves(a, _):
        start = pl.multiple_of(a * 16, 16)
        for k in range(WAVES):
            ac = table_c[k, pl.ds(16 + a, 1), :]
            as_ = table_s[k, pl.ds(16 + a, 1), :]
            bc = table_c[k, 0:16, :]
            bs = table_s[k, 0:16, :]
            waves[k, pl.ds(start, 16), 0:SPAN] = (ac * bc - as_ * bs).astype(BF16)
            waves[k, pl.ds(start, 16), SPAN : 2 * SPAN] = (ac * bs + as_ * bc).astype(BF16)
        return 0

    lax.fori_loop(0, 16, fill_waves, 0)

    ins[0].wait()
    for i in range(SEGS):
        width = min(SEG, POINTS - i * SEG)
        pos = i * SEG + lax.broadcasted_iota(jnp.int32, (1, width), 1)
        values = xv[0, :, i * SEG : i * SEG + width].astype(F32)
        values = jnp.where(pos < n, values, 0.0).astype(BF16)
        segments[i * PITCH + 96 : (i + 1) * PITCH, :] = jnp.zeros((16, SEG), BF16)
        if width < SEG:
            segments[i * PITCH : (i + 1) * PITCH, width:SEG] = jnp.zeros((PITCH, SEG - width), BF16)
        segments[i * PITCH : i * PITCH + PLANES, 0:width] = values

    inverse_row = 1.0 / jnp.full((1, SPAN), n, jnp.int32).astype(F32)
    d_row = lax.broadcasted_iota(jnp.int32, (1, SPAN), 1)
    owner_row = (d_row & 3) * 32 + ((d_row >> 2) & 15) * 2 + (d_row >> 6)

    def scale_of(k):
        return jnp.where(2 * (owner_row * WAVES + k) < n, inverse_row, 0.0)

    def transform(k, _):
        product[...] = jnp.dot(segments[...], waves[k], preferred_element_type=F32)
        real = jnp.zeros((PITCH, SPAN), F32)
        imag = jnp.zeros((PITCH, SPAN), F32)
        for i in range(SEGS):
            wc = table_c[k, 32 + i : 33 + i, :]
            ws = table_s[k, 32 + i : 33 + i, :]
            yc = product[i * PITCH : (i + 1) * PITCH, 0:SPAN]
            ys = product[i * PITCH : (i + 1) * PITCH, SPAN : 2 * SPAN]
            real = real + (yc * wc - ys * ws)
            imag = imag + (yc * ws + ys * wc)
        scale = scale_of(k)
        fourier[k, 0] = real * scale
        fourier[k, 1] = imag * scale
        return 0

    lax.fori_loop(0, WAVES, transform, 0)

    for c in range(2):
        for q in range(PARTS):
            r = c * PARTS + q
            parts[r, 120:128, :] = jnp.zeros((8, SPAN), F32)
            for k in range(WAVES):
                parts[r, k * PART : (k + 1) * PART, :] = fourier[
                    k, c, q * PART : (q + 1) * PART, :
                ]
            packed32[pl.ds(r, LATS, stride=PACKED), :] = parts[r].T

    half_rows = CHIPS * PACKED
    core_send[...] = packed32[pl.ds(pl.multiple_of((1 - core) * half_rows, 8), half_rows), :].astype(
        BF16
    )
    core_copy = remote(core_send, core_got, core_ss, core_rs, sibling)
    core_copy.start()
    mine = packed32[pl.ds(pl.multiple_of(core * half_rows, 8), half_rows), :].reshape(
        CHIPS, PACKED, SPAN
    )
    ins[2].wait()
    ins[9].wait()
    for copy in flux_copies:
        copy.wait_recv()
    flux_got32[...] = flux_got[...].astype(F32)
    two = lax.broadcasted_iota(jnp.int32, (16, SPAN), 0)
    forced[...] = jnp.zeros_like(forced)
    for line in range(LINES):
        total = jnp.zeros((16, SPAN), F32)
        for k in range(2):
            span = air_ref[0, k, line]
            source = lax.div(span, SPANS)
            block = lax.rem(span, SPANS)
            first = flux_got32[source, pl.ds(block, 1), :]
            second = flux_got32[source, pl.ds(block + 24, 1), :]
            pair = jnp.where(
                two == 0, jnp.broadcast_to(first, (16, SPAN)), jnp.broadcast_to(second, (16, SPAN))
            )
            total = total + dot_t(pair.astype(BF16), a2sv[line, k])
        forced[line : line + 1, :] = COUPLE * total[0:1, :]
        forced[32 + line : 33 + line, :] = COUPLE * total[1:2, :]

    has_top = jnp.where(strip > 0, 1.0, 0.0).astype(F32)
    has_bottom = jnp.where(strip < NX * NROW - 1, 1.0, 0.0).astype(F32)
    has_left = jnp.where(col > 0, 1.0, 0.0).astype(F32)
    has_right = jnp.where(col < NCOL - 1, 1.0, 0.0).astype(F32)
    line_of = lax.broadcasted_iota(jnp.int32, (TRACER_ROWS, SPAN), 0) & 3
    lane_of = lax.broadcasted_iota(jnp.int32, (TRACER_ROWS, SPAN), 1)

    def from_above(value, edge):
        shifted[8:72, :] = value
        tops[pl.ds(0, 16, stride=4), :] = edge
        return jnp.where(line_of == 0, tops[...], shifted[7:71, :])

    def from_below(value, edge):
        shifted[8:72, :] = value
        bottoms[pl.ds(3, 16, stride=4), :] = edge
        return jnp.where(line_of == 3, bottoms[...], shifted[9:73, :])

    def from_left(value, tile):
        return jnp.where(lane_of == 0, pltpu.roll(tile, 1, 1), pltpu.roll(value, 1, 1))

    def from_right(value, tile):
        return jnp.where(
            lane_of == SPAN - 1, pltpu.roll(tile, SPAN - 1, 1), pltpu.roll(value, SPAN - 1, 1)
        )

    def twice(value):
        return jnp.concatenate([value, value], axis=0)

    for copy in halo_copies:
        copy.wait_recv()
    shifted[...] = jnp.zeros_like(shifted)
    tops[...] = jnp.zeros_like(tops)
    bottoms[...] = jnp.zeros_like(bottoms)
    top = top1[...].astype(F32) * has_top
    bottom = bottom1[...].astype(F32) * has_bottom
    left = left1[...].astype(F32) * has_left
    right = right1[...].astype(F32) * has_right
    wet64 = cells32[96:160, :]
    east = twice(courant_ref[0:32, :])
    north = twice(courant_ref[32:64, :])
    east_up = from_above(east, twice(top[16:24, :]))
    north_left = from_left(north, twice(left[64:96, :]))
    pair_up = wet64 * from_above(wet64, jnp.broadcast_to(top[24:25, :], (16, SPAN)))
    pair_down = wet64 * from_below(wet64, jnp.broadcast_to(bottom[24:25, :], (16, SPAN)))
    pair_left = wet64 * from_left(wet64, left[96:160, :])
    pair_right = wet64 * from_right(wet64, right[96:160, :])

    def flow(pair, speed, low, high):
        return pair * (
            jnp.maximum(speed, 0.0) * low
            + jnp.minimum(speed, 0.0) * high
            - DIFFUSION * (high - low)
        )

    def advance(q, edge_top, edge_bottom, tile_left, tile_right):
        spread = (
            flow(pair_down, east, q, from_below(q, edge_bottom))
            - flow(pair_up, east_up, from_above(q, edge_top), q)
            + flow(pair_right, north, q, from_right(q, tile_right))
            - flow(pair_left, north_left, from_left(q, tile_left), q)
        )
        return q + wet64 * (forced[...] - spread)

    state = advance(
        tracer_ref[...], top[0:16, :], bottom[0:16, :], left[0:64, :], right[0:64, :]
    )
    tracer_out_ref[...] = state
    cells2_send[...] = state.astype(BF16)
    down2_send[...] = tracer_out_ref[pl.ds(3, 16, stride=4), :].astype(BF16)
    up2_send[...] = tracer_out_ref[pl.ds(0, 16, stride=4), :].astype(BF16)
    halo2_copies = [
        remote(down2_send, top2, halo2_ss.at[0], halo2_rs.at[0], below),
        remote(up2_send, bottom2, halo2_ss.at[1], halo2_rs.at[1], above),
        remote(cells2_send, left2, halo2_ss.at[2], halo2_rs.at[2], after),
        remote(cells2_send, right2, halo2_ss.at[3], halo2_rs.at[3], before),
    ]
    for copy in halo2_copies:
        copy.start()

    core_copy.wait_recv()
    theirs = core_got[...].astype(F32).reshape(CHIPS, PACKED, SPAN)
    is_first = core == 0
    out32[:, 0:PACKED, :] = jnp.where(is_first, mine, theirs)
    out32[:, PACKED : 2 * PACKED, :] = jnp.where(is_first, theirs, mine)
    outbox[...] = out32[...].astype(BF16)
    pl.semaphore_wait(ready, NY - 1)
    for device in x_ring:
        pl.semaphore_signal(ready2, inc=1, device_id=device, device_id_type=MESH)

    for j in range(NY):
        yy = lax.rem(y + j, NY)

        def post(i, _, j=j, yy=yy):
            zz = lax.rem(z + i, NZ)
            remote(
                outbox.at[zz * NY + yy],
                inbox.at[0, y, z],
                all_ss,
                all_rs.at[j],
                at(x, yy, zz, core),
            ).start()
            return 0

        lax.fori_loop(1, NZ, post, 0)
        if j:
            post(0, 0)
    inbox[0, pl.ds(y, 1), pl.ds(z, 1)] = outbox[pl.ds(z * NY + y, 1)][None]

    ins[1].wait()
    for k in range(WAVES):
        turned = pv[k].astype(F32).T.astype(BF16)
        for g in range(NX):
            poly_t[g, k * DEGREES : (k + 1) * DEGREES, :] = turned[g * DEGREES : (g + 1) * DEGREES]
    poly_got[0] = poly_t[x]
    poly_copies = [
        remote(
            poly_t.at[lax.rem(x + i, NX)],
            poly_got.at[i],
            poly_ss.at[i - 1],
            poly_rs.at[i - 1],
            x_ring[i - 1],
        )
        for i in range(1, NX)
    ]
    for copy in poly_copies:
        copy.start()

    rows_b = lax.broadcasted_iota(jnp.int32, (8 * SPAN, SPAN), 0)
    lanes_b = lax.broadcasted_iota(jnp.int32, (8 * SPAN, SPAN), 1)
    lane_in = rows_b & 127
    wanted = (rows_b >> 8) * 32 + (lane_in >> 3) * 2 + ((rows_b >> 7) & 1)
    chosen = ((lane_in & 7) == core * 4 + y) & (lanes_b == wanted)
    select_y[...] = jnp.where(chosen, 1.0, 0.0).astype(BF16)

    for copy in halo2_copies:
        copy.wait_recv()
    state = advance(
        tracer_out_ref[...],
        top2[...].astype(F32) * has_top,
        bottom2[...].astype(F32) * has_bottom,
        left2[...].astype(F32) * has_left,
        right2[...].astype(F32) * has_right,
    )
    tracer_out_ref[...] = state
    tracer_leave = pltpu.make_async_copy(tracer_out_ref, tracer_out_hbm, local_sem.at[11])
    tracer_leave.start()
    sst_send[...] = state[0:16, :].astype(BF16)
    sst_got[pl.ds(col, 1)] = sst_send[...][None]
    sst_copies = [
        remote(sst_send, sst_got.at[col], sst_ss.at[i], sst_rs.at[i], device)
        for i, device in enumerate(band)
    ]
    for copy in sst_copies:
        copy.start()

    next_x = x_ring[0]
    last_x = x_ring[-1]
    ring_right = []
    ring_left = []
    ring_on = []

    def circulate(j):
        count = NZ - 1 if j == 0 else NZ
        arrived = remote(
            outbox.at[pl.ds(0, count)],
            inbox.at[0, 0, pl.ds(0, count)],
            all_ss,
            all_rs.at[j],
            sibling,
        )
        arrived.wait_recv()
        yy = lax.rem(y + NY - j, NY)
        to_right = remote(
            inbox.at[0, yy], inbox.at[1, yy], ring_ss.at[0, j], ring_rs.at[0, j], next_x
        )
        to_left = remote(
            inbox.at[0, yy], inbox.at[3, yy], ring_ss.at[1, j], ring_rs.at[1, j], last_x
        )
        to_right.start()
        to_left.start()
        ring_right.append(to_right)
        ring_left.append(to_left)

    def pass_on(j):
        yy = lax.rem(y + NY - j, NY)
        ring_right[j].wait_recv()
        ring_left[j].wait_recv()
        slot, device = (1, next_x) if j % 2 == 0 else (3, last_x)
        copy = remote(
            inbox.at[slot, yy], inbox.at[2, yy], ring_ss.at[2, j], ring_rs.at[2, j], device
        )
        copy.start()
        ring_on.append(copy)

    circulate(0)
    circulate(1)

    ins[3].wait()
    ins[10].wait()
    for copy in sst_copies:
        copy.wait_recv()
    sst_got32[...] = sst_got[...].astype(F32)
    row0[...] = jnp.zeros_like(row0)
    for b in range(SPANS):
        span = sea_ref[0, b]
        source = lax.div(span, LINES)
        line = lax.rem(span, LINES)
        warmth = jnp.broadcast_to(sst_got32[source, pl.ds(line, 1), :], (16, SPAN))
        sampled = dot_t(warmth.astype(BF16), s2av[0, b])[0:1, :]
        plane = x32[0:1, b * SPAN : (b + 1) * SPAN] + sampled
        plane = jnp.where(lane + b * SPAN < n, plane, 0.0)
        half = (b % 2) * SPAN
        row0[b // 2 : b // 2 + 1, half : half + SPAN] = plane
    surface = row0[...].astype(BF16)
    plane32[...] = jnp.zeros_like(plane32)
    for k in range(WAVES):
        part = jnp.dot(surface, waves[k], preferred_element_type=F32)
        wc = table_c[k, 32:48, :]
        ws = table_s[k, 32:48, :]
        yc = part[:, 0:SPAN]
        ys = part[:, SPAN : 2 * SPAN]
        scale = scale_of(k)
        plane32[2 * k : 2 * k + 1, :] = jnp.sum(yc * wc - ys * ws, axis=0, keepdims=True) * scale
        plane32[2 * k + 1 : 2 * k + 2, :] = (
            jnp.sum(yc * ws + ys * wc, axis=0, keepdims=True) * scale
        )

    plane_send[...] = plane32[...].astype(BF16)
    plane_got[pl.ds(z, 1)] = plane_send[...][None]
    for device in z_ring:
        remote(plane_send, plane_got.at[z], plane_ss, plane_rs, device).start()

    circulate(2)
    pass_on(0)
    circulate(3)
    pass_on(1)

    def many(copies, device):
        return remote(
            plane_got.at[pl.ds(0, copies)],
            plane_got.at[pl.ds(0, copies)],
            plane_ss,
            plane_rs,
            device,
        )

    pass_on(2)
    pass_on(3)
    def unpack(slot):
        got32[...] = inbox[slot].astype(F32).reshape(CHIPS * 2 * PACKED, SPAN)

        def spread_row(r, _):
            columns = pl.ds(pl.multiple_of(r * SPAN, SPAN), SPAN)
            right_hand[slot * LATS : (slot + 1) * LATS, columns] = got32[
                pl.ds(r, LATS, stride=PACKED), :
            ].astype(BF16)
            return 0

        lax.fori_loop(0, PACKED, spread_row, 0)

    unpack(0)
    many(NZ - 1, sibling).wait_recv()
    stretch = plane_got[...].astype(F32).reshape(NZ * 16, SPAN)
    stretch = pltpu.roll(stretch, lax.rem(SPAN - NY * z, SPAN), 1)
    place = lax.broadcasted_iota(jnp.int32, (16, SPAN), 1) >> 2
    mixed = jnp.zeros((16, SPAN), F32)
    for i in range(NZ):
        tile = stretch[i * 16 : (i + 1) * 16, :]
        low = pltpu.roll(tile, 8 * i, 1) if i else tile
        high = pltpu.roll(tile, (8 * i + 4 + CHIPS) % SPAN, 1)
        mixed = jnp.where(place == 2 * i, low, jnp.where(place == 2 * i + 1, high, mixed))
    mixed = mixed.astype(BF16)
    mixed_send[...] = mixed
    pl.semaphore_wait(ready2, NX - 1)
    mixed_got[pl.ds(y * 2 + core, 1)] = mixed[None]
    steps = [(i // 8, (i // 2) % 4, i % 2) for i in range(1, NX * NY * NCORE)]
    hops = (0, 1, 2, 1)
    for dx, dy, dc in sorted(steps, key=lambda t: -hops[t[0]] - hops[t[1]]):
        cc = 1 - core if dc else core
        remote(
            mixed_send,
            mixed_got.at[dx * 8 + y * 2 + core],
            mixed_ss,
            mixed_rs,
            at(lax.rem(x + dx, NX), lax.rem(y + dy, NY), z, cc),
        ).start()

    unpack(1)
    unpack(3)
    for copy in poly_copies:
        copy.wait_recv()
    degrees = jnp.concatenate([poly_got[i] for i in range(NX)], axis=1)
    for copy in ring_on:
        copy.wait_recv()
    unpack(2)

    degrees_all[...] = degrees

    def legendre(i, _):
        columns = pl.ds(pl.multiple_of(i * 2 * SPAN, 2 * SPAN), 2 * SPAN)
        product2[:, columns] = jnp.dot(
            degrees_all[...], right_hand[:, columns], preferred_element_type=F32
        )
        return 0

    lax.fori_loop(0, 4, legendre, 0)
    lanes = lax.broadcasted_iota(jnp.int32, (DEGREES, SPAN), 1)
    for c in range(2):
        for k in range(WAVES):
            total = jnp.zeros((DEGREES, SPAN), F32)
            for q in range(PARTS):
                r = c * PARTS + q
                block = product2[k * DEGREES : (k + 1) * DEGREES, r * SPAN : (r + 1) * SPAN]
                turn = (PART * (q - k)) % SPAN
                if turn:
                    block = pltpu.roll(block, turn, 1)
                keep = (lanes >= q * PART) & (lanes < (q + 1) * PART)
                total = jnp.where(keep, block, total)
            bulk[c, k] = total

    remote(
        mixed_got.at[pl.ds(0, 31)], mixed_got.at[pl.ds(0, 31)], mixed_ss, mixed_rs, sibling
    ).wait_recv()
    stacked = jnp.concatenate(
        [
            jnp.concatenate([mixed_got[slot * 8 + i] for i in range(8)], axis=1)
            for slot in range(NX)
        ],
        axis=0,
    )
    sorted_rows = jnp.dot(stacked, select_y[...], preferred_element_type=F32).astype(BF16)
    surface_rows = jnp.concatenate(
        [sorted_rows[slot * 16 : (slot + 1) * 16, :] for slot in range(NX)], axis=1
    )
    surface_rows = jnp.concatenate(
        [surface_rows, jnp.zeros((SPAN - 16, NX * LATS), BF16)], axis=0
    )
    product0[...] = dot_t(degrees, surface_rows)
    leaves = [tracer_leave]
    for c in range(2):
        for k in range(WAVES):
            block = product0[k * DEGREES : (k + 1) * DEGREES, :]
            turn = (-(2 * k + c)) % SPAN
            if turn:
                block = pltpu.roll(block, turn, 1)
            total = jnp.where(lanes == 0, block, bulk[c, k])
            spectral_ref[c, k] = total[:, 0:PLANES].astype(BF16)
        leave = pltpu.make_async_copy(
            spectral_ref.at[c], spectral_hbm.at[c], local_sem.at[12 + c]
        )
        leave.start()
        leaves.append(leave)

    for copy in flux_copies + halo_copies + halo2_copies + sst_copies + poly_copies:
        copy.wait_send()
    core_copy.wait_send()
    remote(
        outbox.at[pl.ds(0, CHIPS - 1)],
        outbox.at[pl.ds(0, CHIPS - 1)],
        all_ss,
        all_rs.at[0],
        sibling,
    ).wait_send()
    many(NZ - 1, sibling).wait_send()
    remote(
        mixed_got.at[pl.ds(0, 31)], mixed_got.at[pl.ds(0, 31)], mixed_ss, mixed_rs, sibling
    ).wait_send()
    for copy in ring_right + ring_left + ring_on:
        copy.wait_send()
    for copy in leaves:
        copy.wait()


def local(
    physical_values,
    samples_per_parallel,
    associated_polynomials,
    heat_salt_anomalies,
    courant_numbers,
    water_indicator,
    air_to_sea_coefficients,
    air_partner_span,
    sea_to_air_coefficients,
    sea_partner_span,
):
    hbm = pl.BlockSpec(memory_space=pltpu.HBM)
    dma = pltpu.SemaphoreType.DMA
    scratch = [
        pltpu.VMEM((2, WAVES, DEGREES, PLANES), BF16),
        pltpu.VMEM((TRACER_ROWS, SPAN), F32),
        pltpu.VMEM((TRACER_ROWS, SPAN), F32),
        pltpu.VMEM((TRACER_ROWS, SPAN), F32),
        pltpu.VMEM((LINES, SPAN), jnp.int32),
        pltpu.SMEM((512,), jnp.int32),
        pltpu.SMEM((1, 2, LINES), jnp.int32),
        pltpu.SMEM((1, SPANS), jnp.int32),
        pltpu.VMEM((1, PLANES, POINTS), BF16),
        pltpu.VMEM((32, POINTS), BF16),
        pltpu.VMEM((WAVES, LATS, NX * DEGREES), BF16),
        pltpu.VMEM((1, SPANS, SPAN, SPAN), BF16),
        pltpu.VMEM((LINES, 2, SPAN, SPAN), BF16),
        pltpu.VMEM((32, POINTS), F32),
        pltpu.VMEM((48, SPAN), F32),
        pltpu.VMEM((NCOL, 48, SPAN), F32),
        pltpu.VMEM((NCOL, 16, SPAN), F32),
        pltpu.VMEM((32, SPAN), F32),
        pltpu.VMEM((160, SPAN), F32),
        pltpu.VMEM((80, SPAN), F32),
        pltpu.VMEM((TRACER_ROWS, SPAN), F32),
        pltpu.VMEM((TRACER_ROWS, SPAN), F32),
        pltpu.VMEM((TRACER_ROWS, SPAN), F32),
        pltpu.VMEM((WAVES, 48, SPAN), F32),
        pltpu.VMEM((WAVES, 48, SPAN), F32),
        pltpu.VMEM((WAVES, SEG, 2 * SPAN), BF16),
        pltpu.VMEM((SEGS * PITCH, SEG), BF16),
        pltpu.VMEM((SEGS * PITCH, 2 * SPAN), F32),
        pltpu.VMEM((WAVES, 2, PITCH, SPAN), F32),
        pltpu.VMEM((16, SEG), F32),
        pltpu.VMEM((PACKED, SPAN, SPAN), F32),
        pltpu.VMEM((LATS * PACKED, SPAN), F32),
        pltpu.VMEM((CHIPS, 2 * PACKED, SPAN), F32),
        pltpu.VMEM((NX * LATS, PACKED * SPAN), BF16),
        pltpu.VMEM((LATS * PACKED, SPAN), F32),
        pltpu.VMEM((WAVES * DEGREES, PACKED * SPAN), F32),
        pltpu.VMEM((WAVES * DEGREES, SPAN), F32),
        pltpu.VMEM((WAVES * DEGREES, NX * LATS), BF16),
        pltpu.VMEM((16, SPAN), F32),
        pltpu.VMEM((8 * SPAN, SPAN), BF16),
        pltpu.VMEM((2, WAVES, DEGREES, SPAN), F32),
        pltpu.VMEM((NX, WAVES * DEGREES, LATS), BF16),
        pltpu.VMEM((48, SPAN), BF16),
        pltpu.VMEM((NCOL, 48, SPAN), BF16),
        pltpu.VMEM((32, SPAN), BF16),
        pltpu.VMEM((32, SPAN), BF16),
        pltpu.VMEM((160, SPAN), BF16),
        pltpu.VMEM((32, SPAN), BF16),
        pltpu.VMEM((32, SPAN), BF16),
        pltpu.VMEM((160, SPAN), BF16),
        pltpu.VMEM((160, SPAN), BF16),
        pltpu.VMEM((16, SPAN), BF16),
        pltpu.VMEM((16, SPAN), BF16),
        pltpu.VMEM((64, SPAN), BF16),
        pltpu.VMEM((16, SPAN), BF16),
        pltpu.VMEM((16, SPAN), BF16),
        pltpu.VMEM((64, SPAN), BF16),
        pltpu.VMEM((64, SPAN), BF16),
        pltpu.VMEM((16, SPAN), BF16),
        pltpu.VMEM((NCOL, 16, SPAN), BF16),
        pltpu.VMEM((NX, WAVES * DEGREES, LATS), BF16),
        pltpu.VMEM((CHIPS * PACKED, SPAN), BF16),
        pltpu.VMEM((CHIPS * PACKED, SPAN), BF16),
        pltpu.VMEM((CHIPS, 2 * PACKED, SPAN), BF16),
        pltpu.VMEM((NX, NY, NZ, 2 * PACKED, SPAN), BF16),
        pltpu.VMEM((16, SPAN), BF16),
        pltpu.VMEM((NZ, 16, SPAN), BF16),
        pltpu.VMEM((16, SPAN), BF16),
        pltpu.VMEM((NX * NY * NCORE, 16, SPAN), BF16),
        dma((14,)),
        dma((NCOL - 1,)),
        dma((NCOL - 1,)),
        dma((4,)),
        dma((4,)),
        dma((4,)),
        dma((4,)),
        dma((NCOL - 1,)),
        dma((NCOL - 1,)),
        dma((NX - 1,)),
        dma((NX - 1,)),
        dma,
        dma,
        dma,
        dma((NY,)),
        dma((3, NY)),
        dma((3, NY)),
        dma,
        dma,
        dma,
        dma,
        pltpu.SemaphoreType.REGULAR,
        pltpu.SemaphoreType.REGULAR,
    ]
    spectral, tracers = pl.pallas_call(
        kernel,
        out_shape=(
            jax.ShapeDtypeStruct((2, WAVES, DEGREES, PLANES), BF16),
            jax.ShapeDtypeStruct((TRACER_ROWS, SPAN), F32),
        ),
        in_specs=[hbm] * 10,
        out_specs=(hbm, hbm),
        scratch_shapes=scratch,
        compiler_params=pltpu.CompilerParams(
            collective_id=0, has_side_effects=True, vmem_limit_bytes=64 * 2**20
        ),
        cost_estimate=pl.CostEstimate(
            flops=1_000_000_000, bytes_accessed=3_000_000, transcendentals=0
        ),
    )(
        physical_values,
        associated_polynomials,
        sea_to_air_coefficients,
        air_to_sea_coefficients,
        heat_salt_anomalies.reshape(TRACER_ROWS, SPAN),
        courant_numbers.reshape(TRACER_ROWS, SPAN),
        water_indicator,
        samples_per_parallel,
        jnp.transpose(air_partner_span, (1, 2, 0)),
        sea_partner_span,
    )
    return spectral.transpose(3, 0, 1, 2), tracers.reshape(2, 8, LINES, SPAN)


def solution(mesh):
    placed = (
        P(("grp", "row", "col"), None, None),
        P(),
        P(("row", "col"), "grp", None),
        P(None, None, ("grp", "row"), "col"),
        P(None, None, ("grp", "row"), "col"),
        P(("grp", "row"), "col"),
        P(("grp", "row"), None, "col", None),
        P(("grp", "row"), "col", None),
        P(("grp", "row", "col"), None, None, None),
        P(("grp", "row", "col"), None),
    )
    return jax.shard_map(
        local,
        mesh=mesh,
        in_specs=placed,
        out_specs=(P(None, None, ("row", "col"), "grp"), P(None, None, ("grp", "row"), "col")),
        check_vma=False,
    )
```

```python
import math

import jax
import jax.numpy as jnp
from jax import lax
from jax.experimental import pallas as pl
from jax.experimental.pallas import tpu as pltpu
from jax.sharding import PartitionSpec as P

MESH = pl.DeviceIdType.MESH
F32 = jnp.float32
BF16 = jnp.bfloat16

NX, NY, NZ, NCORE = 4, 4, 16, 2
NROW, NCOL = 16, 8
CHIPS = NY * NZ

LEV = 10
PLANES = 100
POINTS = 2688
SPANS = 21
SPAN = 128
WAVES = 5
DEGREES = 160
LATS = 128
LINES = 4
TRACER_ROWS = 64
DIFFUSION = 0.07
COUPLE = 0.5

SEG = 256
SEGS = 11
PITCH = 112
PART = 25
PARTS = 4
PACKED = 8


def sincos(turns4):
    quarter = jnp.floor(turns4 + 0.5)
    y = (turns4 - quarter) * (0.5 * math.pi)
    y2 = y * y
    s = y * (1.0 + y2 * (-1.0 / 6 + y2 * (1.0 / 120 + y2 * (-1.0 / 5040 + y2 * (1.0 / 362880)))))
    c = 1.0 + y2 * (
        -0.5 + y2 * (1.0 / 24 + y2 * (-1.0 / 720 + y2 * (1.0 / 40320 + y2 * (-1.0 / 3628800))))
    )
    odd = (quarter == 1.0) | (quarter == 3.0)
    cos_sign = jnp.where((quarter == 1.0) | (quarter == 2.0), -1.0, 1.0)
    sin_sign = jnp.where((quarter == 2.0) | (quarter == 3.0), -1.0, 1.0)
    return cos_sign * jnp.where(odd, s, c), sin_sign * jnp.where(odd, c, s)


def dot_t(a, b):
    return lax.dot_general(a, b, (((1,), (1,)), ((), ())), preferred_element_type=F32)


def kernel(
    phys_hbm,
    poly_hbm,
    s2a_hbm,
    a2s_hbm,
    tracer_hbm,
    courant_hbm,
    water_hbm,
    points_hbm,
    air_hbm,
    sea_hbm,
    spectral_hbm,
    tracer_out_hbm,
    spectral_ref,
    tracer_out_ref,
    tracer_ref,
    courant_ref,
    water_ref,
    points_ref,
    air_ref,
    sea_ref,
    xv,
    xtop,
    pv,
    s2av,
    a2sv,
    x32,
    flux32,
    flux_got32,
    sst_got32,
    rows32,
    cells32,
    shifted,
    tops,
    bottoms,
    forced,
    table_c,
    table_s,
    waves,
    segments,
    product,
    fourier,
    row0,
    parts,
    packed32,
    out32,
    right_hand,
    got32,
    product2,
    product0,
    degrees_all,
    plane32,
    select_y,
    bulk,
    poly_t,
    flux_send,
    flux_got,
    down_send,
    up_send,
    cells_send,
    top1,
    bottom1,
    left1,
    right1,
    down2_send,
    up2_send,
    cells2_send,
    top2,
    bottom2,
    left2,
    right2,
    sst_send,
    sst_got,
    poly_got,
    core_send,
    core_got,
    outbox,
    inbox,
    plane_send,
    plane_got,
    mixed_send,
    mixed_got,
    local_sem,
    flux_ss,
    flux_rs,
    halo_ss,
    halo_rs,
    halo2_ss,
    halo2_rs,
    sst_ss,
    sst_rs,
    poly_ss,
    poly_rs,
    core_ss,
    core_rs,
    all_ss,
    all_rs,
    ring_ss,
    ring_rs,
    plane_ss,
    plane_rs,
    mixed_ss,
    mixed_rs,
    ready,
    ready2,
):
    x = lax.axis_index("grp")
    row = lax.axis_index("row")
    col = lax.axis_index("col")
    y = row // 4
    z = lax.rem(row, 4) * 4 + col // 2
    core = lax.rem(col, 2)
    strip = x * NROW + row

    def at(xx, yy, zz, cc):
        return (xx, yy * 4 + zz // 4, lax.rem(zz, 4) * 2 + cc)

    def remote(src, dst, ss, rs, device):
        return pltpu.make_async_remote_copy(
            src_ref=src, dst_ref=dst, send_sem=ss, recv_sem=rs, device_id=device, device_id_type=MESH
        )

    def strip_at(other):
        return (other // NROW, lax.rem(other, NROW), col)

    below = strip_at(lax.rem(strip + 1, NX * NROW))
    above = strip_at(lax.rem(strip + NX * NROW - 1, NX * NROW))
    band = [(x, row, lax.rem(col + i, NCOL)) for i in range(1, NCOL)]
    after = band[0]
    before = band[-1]
    z_ring = [
        at(x, y, lax.rem(z + i, NZ), core)
        for i in (8, 7, 9, 6, 10, 5, 11, 4, 12, 3, 13, 2, 14, 1, 15)
    ]
    y_ring = [at(x, lax.rem(y + i, NY), z, core) for i in range(1, NY)]
    x_ring = [at(lax.rem(x + i, NX), y, z, core) for i in range(1, NX)]
    sibling = at(x, y, z, 1 - core)

    moves = [
        (phys_hbm, xv),
        (poly_hbm, pv),
        (a2s_hbm, a2sv),
        (s2a_hbm, s2av),
        (points_hbm, points_ref),
        (phys_hbm.at[0, pl.ds(0, 32)], xtop),
        (tracer_hbm, tracer_ref),
        (courant_hbm, courant_ref),
        (water_hbm, water_ref),
        (air_hbm, air_ref),
        (sea_hbm, sea_ref),
    ]
    ins = [
        pltpu.make_async_copy(source, target, local_sem.at[i])
        for i, (source, target) in enumerate(moves)
    ]
    for i in (4, 5, 6, 7, 8, 0, 9, 2, 10, 3, 1):
        ins[i].start()
    barrier = pltpu.get_barrier_semaphore()
    greeted = band + [below, above, sibling] + x_ring + y_ring + z_ring
    for device in greeted:
        pl.semaphore_signal(barrier, inc=1, device_id=device, device_id_type=MESH)

    own = strip * NCOL + col
    ins[4].wait()
    n = points_ref[own]
    lane = lax.broadcasted_iota(jnp.int32, (1, SPAN), 1)

    ins[5].wait()
    x32[...] = xtop[...].astype(F32)
    flux32[...] = jnp.zeros_like(flux32)
    for b in range(SPANS):
        live = lane + b * SPAN < n
        for q in range(2):
            line = x32[(q + 1) * LEV : (q + 1) * LEV + 1, b * SPAN : (b + 1) * SPAN]
            flux32[q * 24 + b : q * 24 + b + 1, :] = jnp.where(live, line, 0.0)
    flux_send[...] = flux32[...].astype(BF16)
    flux_got[pl.ds(col, 1)] = flux_send[...][None]

    for i in (6, 7, 8):
        ins[i].wait()
    wet = water_ref[...].astype(F32)
    for i in range(16):
        cells32[96 + 4 * i : 100 + 4 * i, :] = wet
    cells32[0:64, :] = tracer_ref[...]
    cells32[64:96, :] = courant_ref[32:64, :]
    cells_send[...] = cells32[...].astype(BF16)
    rows32[...] = jnp.zeros_like(rows32)
    rows32[0:16, :] = tracer_ref[pl.ds(3, 16, stride=4), :]
    rows32[16:24, :] = courant_ref[pl.ds(3, 8, stride=4), :]
    rows32[24:25, :] = wet[3:4, :]
    down_send[...] = rows32[...].astype(BF16)
    rows32[0:16, :] = tracer_ref[pl.ds(0, 16, stride=4), :]
    rows32[24:25, :] = wet[0:1, :]
    up_send[...] = rows32[...].astype(BF16)

    pl.semaphore_wait(barrier, len(greeted))
    flux_copies = [
        remote(flux_send, flux_got.at[col], flux_ss.at[i], flux_rs.at[i], device)
        for i, device in enumerate(band)
    ]
    halo_copies = [
        remote(down_send, top1, halo_ss.at[0], halo_rs.at[0], below),
        remote(up_send, bottom1, halo_ss.at[1], halo_rs.at[1], above),
        remote(cells_send, left1, halo_ss.at[2], halo_rs.at[2], after),
        remote(cells_send, right1, halo_ss.at[3], halo_rs.at[3], before),
    ]
    for copy in flux_copies + halo_copies:
        copy.start()
    for device in y_ring:
        pl.semaphore_signal(ready, inc=1, device_id=device, device_id_type=MESH)

    shape = (WAVES, 48, SPAN)
    k_of = lax.broadcasted_iota(jnp.int32, shape, 0)
    p_row = lax.broadcasted_iota(jnp.int32, shape, 1)
    d_of = lax.broadcasted_iota(jnp.int32, shape, 2)
    owner = (d_of & 3) * 32 + ((d_of >> 2) & 15) * 2 + (d_of >> 6)
    orders = owner * WAVES + k_of
    places = jnp.where(
        p_row < 16, p_row, jnp.where(p_row < 32, (p_row - 16) * 16, (p_row - 32) * SEG)
    )
    count = jnp.full(shape, n, jnp.int32).astype(F32)
    inverse = 1.0 / count
    turns = orders.astype(F32) * places.astype(F32)
    phase = turns - jnp.floor(turns * inverse) * count
    phase = jnp.where(phase < 0.0, phase + count, phase)
    phase = jnp.where(phase >= count, phase - count, phase)
    cosine, sine = sincos(phase * (4.0 * inverse))
    table_c[...] = cosine
    table_s[...] = -sine

    def fill_waves(a, _):
        start = pl.multiple_of(a * 16, 16)
        for k in range(WAVES):
            ac = table_c[k, pl.ds(16 + a, 1), :]
            as_ = table_s[k, pl.ds(16 + a, 1), :]
            bc = table_c[k, 0:16, :]
            bs = table_s[k, 0:16, :]
            waves[k, pl.ds(start, 16), 0:SPAN] = (ac * bc - as_ * bs).astype(BF16)
            waves[k, pl.ds(start, 16), SPAN : 2 * SPAN] = (ac * bs + as_ * bc).astype(BF16)
        return 0

    lax.fori_loop(0, 16, fill_waves, 0)

    ins[0].wait()
    for i in range(SEGS):
        width = min(SEG, POINTS - i * SEG)
        pos = i * SEG + lax.broadcasted_iota(jnp.int32, (1, width), 1)
        values = xv[0, :, i * SEG : i * SEG + width].astype(F32)
        values = jnp.where(pos < n, values, 0.0).astype(BF16)
        segments[i * PITCH + 96 : (i + 1) * PITCH, :] = jnp.zeros((16, SEG), BF16)
        if width < SEG:
            segments[i * PITCH : (i + 1) * PITCH, width:SEG] = jnp.zeros((PITCH, SEG - width), BF16)
        segments[i * PITCH : i * PITCH + PLANES, 0:width] = values

    inverse_row = 1.0 / jnp.full((1, SPAN), n, jnp.int32).astype(F32)
    d_row = lax.broadcasted_iota(jnp.int32, (1, SPAN), 1)
    owner_row = (d_row & 3) * 32 + ((d_row >> 2) & 15) * 2 + (d_row >> 6)

    def scale_of(k):
        return jnp.where(2 * (owner_row * WAVES + k) < n, inverse_row, 0.0)

    def transform(k, _):
        product[...] = jnp.dot(segments[...], waves[k], preferred_element_type=F32)
        real = jnp.zeros((PITCH, SPAN), F32)
        imag = jnp.zeros((PITCH, SPAN), F32)
        for i in range(SEGS):
            wc = table_c[k, 32 + i : 33 + i, :]
            ws = table_s[k, 32 + i : 33 + i, :]
            yc = product[i * PITCH : (i + 1) * PITCH, 0:SPAN]
            ys = product[i * PITCH : (i + 1) * PITCH, SPAN : 2 * SPAN]
            real = real + (yc * wc - ys * ws)
            imag = imag + (yc * ws + ys * wc)
        scale = scale_of(k)
        fourier[k, 0] = real * scale
        fourier[k, 1] = imag * scale
        return 0

    lax.fori_loop(0, WAVES, transform, 0)

    for c in range(2):
        for q in range(PARTS):
            r = c * PARTS + q
            parts[r, 120:128, :] = jnp.zeros((8, SPAN), F32)
            for k in range(WAVES):
                parts[r, k * PART : (k + 1) * PART, :] = fourier[
                    k, c, q * PART : (q + 1) * PART, :
                ]
            packed32[pl.ds(r, LATS, stride=PACKED), :] = parts[r].T

    half_rows = CHIPS * PACKED
    core_send[...] = packed32[pl.ds(pl.multiple_of((1 - core) * half_rows, 8), half_rows), :].astype(
        BF16
    )
    core_copy = remote(core_send, core_got, core_ss, core_rs, sibling)
    core_copy.start()
    mine = packed32[pl.ds(pl.multiple_of(core * half_rows, 8), half_rows), :].reshape(
        CHIPS, PACKED, SPAN
    )
    ins[2].wait()
    ins[9].wait()
    for copy in flux_copies:
        copy.wait_recv()
    flux_got32[...] = flux_got[...].astype(F32)
    two = lax.broadcasted_iota(jnp.int32, (16, SPAN), 0)
    forced[...] = jnp.zeros_like(forced)
    for line in range(LINES):
        total = jnp.zeros((16, SPAN), F32)
        for k in range(2):
            span = air_ref[0, k, line]
            source = lax.div(span, SPANS)
            block = lax.rem(span, SPANS)
            first = flux_got32[source, pl.ds(block, 1), :]
            second = flux_got32[source, pl.ds(block + 24, 1), :]
            pair = jnp.where(
                two == 0, jnp.broadcast_to(first, (16, SPAN)), jnp.broadcast_to(second, (16, SPAN))
            )
            total = total + dot_t(pair.astype(BF16), a2sv[line, k])
        forced[line : line + 1, :] = COUPLE * total[0:1, :]
        forced[32 + line : 33 + line, :] = COUPLE * total[1:2, :]

    has_top = jnp.where(strip > 0, 1.0, 0.0).astype(F32)
    has_bottom = jnp.where(strip < NX * NROW - 1, 1.0, 0.0).astype(F32)
    has_left = jnp.where(col > 0, 1.0, 0.0).astype(F32)
    has_right = jnp.where(col < NCOL - 1, 1.0, 0.0).astype(F32)
    line_of = lax.broadcasted_iota(jnp.int32, (TRACER_ROWS, SPAN), 0) & 3
    lane_of = lax.broadcasted_iota(jnp.int32, (TRACER_ROWS, SPAN), 1)

    def from_above(value, edge):
        shifted[8:72, :] = value
        tops[pl.ds(0, 16, stride=4), :] = edge
        return jnp.where(line_of == 0, tops[...], shifted[7:71, :])

    def from_below(value, edge):
        shifted[8:72, :] = value
        bottoms[pl.ds(3, 16, stride=4), :] = edge
        return jnp.where(line_of == 3, bottoms[...], shifted[9:73, :])

    def from_left(value, tile):
        return jnp.where(lane_of == 0, pltpu.roll(tile, 1, 1), pltpu.roll(value, 1, 1))

    def from_right(value, tile):
        return jnp.where(
            lane_of == SPAN - 1, pltpu.roll(tile, SPAN - 1, 1), pltpu.roll(value, SPAN - 1, 1)
        )

    def twice(value):
        return jnp.concatenate([value, value], axis=0)

    for copy in halo_copies:
        copy.wait_recv()
    shifted[...] = jnp.zeros_like(shifted)
    tops[...] = jnp.zeros_like(tops)
    bottoms[...] = jnp.zeros_like(bottoms)
    top = top1[...].astype(F32) * has_top
    bottom = bottom1[...].astype(F32) * has_bottom
    left = left1[...].astype(F32) * has_left
    right = right1[...].astype(F32) * has_right
    wet64 = cells32[96:160, :]
    east = twice(courant_ref[0:32, :])
    north = twice(courant_ref[32:64, :])
    east_up = from_above(east, twice(top[16:24, :]))
    north_left = from_left(north, twice(left[64:96, :]))
    pair_up = wet64 * from_above(wet64, jnp.broadcast_to(top[24:25, :], (16, SPAN)))
    pair_down = wet64 * from_below(wet64, jnp.broadcast_to(bottom[24:25, :], (16, SPAN)))
    pair_left = wet64 * from_left(wet64, left[96:160, :])
    pair_right = wet64 * from_right(wet64, right[96:160, :])

    def flow(pair, speed, low, high):
        return pair * (
            jnp.maximum(speed, 0.0) * low
            + jnp.minimum(speed, 0.0) * high
            - DIFFUSION * (high - low)
        )

    def advance(q, edge_top, edge_bottom, tile_left, tile_right):
        spread = (
            flow(pair_down, east, q, from_below(q, edge_bottom))
            - flow(pair_up, east_up, from_above(q, edge_top), q)
            + flow(pair_right, north, q, from_right(q, tile_right))
            - flow(pair_left, north_left, from_left(q, tile_left), q)
        )
        return q + wet64 * (forced[...] - spread)

    state = advance(
        tracer_ref[...], top[0:16, :], bottom[0:16, :], left[0:64, :], right[0:64, :]
    )
    tracer_out_ref[...] = state
    cells2_send[...] = state.astype(BF16)
    down2_send[...] = tracer_out_ref[pl.ds(3, 16, stride=4), :].astype(BF16)
    up2_send[...] = tracer_out_ref[pl.ds(0, 16, stride=4), :].astype(BF16)
    halo2_copies = [
        remote(down2_send, top2, halo2_ss.at[0], halo2_rs.at[0], below),
        remote(up2_send, bottom2, halo2_ss.at[1], halo2_rs.at[1], above),
        remote(cells2_send, left2, halo2_ss.at[2], halo2_rs.at[2], after),
        remote(cells2_send, right2, halo2_ss.at[3], halo2_rs.at[3], before),
    ]
    for copy in halo2_copies:
        copy.start()

    core_copy.wait_recv()
    theirs = core_got[...].astype(F32).reshape(CHIPS, PACKED, SPAN)
    is_first = core == 0
    out32[:, 0:PACKED, :] = jnp.where(is_first, mine, theirs)
    out32[:, PACKED : 2 * PACKED, :] = jnp.where(is_first, theirs, mine)
    outbox[...] = out32[...].astype(BF16)
    pl.semaphore_wait(ready, NY - 1)
    for device in x_ring:
        pl.semaphore_signal(ready2, inc=1, device_id=device, device_id_type=MESH)

    for j in range(NY):
        yy = lax.rem(y + j, NY)

        def post(i, _, j=j, yy=yy):
            zz = lax.rem(z + i, NZ)
            remote(
                outbox.at[zz * NY + yy],
                inbox.at[0, y, z],
                all_ss,
                all_rs.at[j],
                at(x, yy, zz, core),
            ).start()
            return 0

        lax.fori_loop(1, NZ, post, 0)
        if j:
            post(0, 0)
    inbox[0, pl.ds(y, 1), pl.ds(z, 1)] = outbox[pl.ds(z * NY + y, 1)][None]

    ins[1].wait()
    for k in range(WAVES):
        turned = pv[k].astype(F32).T.astype(BF16)
        for g in range(NX):
            poly_t[g, k * DEGREES : (k + 1) * DEGREES, :] = turned[g * DEGREES : (g + 1) * DEGREES]
    poly_got[0] = poly_t[x]
    poly_copies = [
        remote(
            poly_t.at[lax.rem(x + i, NX)],
            poly_got.at[i],
            poly_ss.at[i - 1],
            poly_rs.at[i - 1],
            x_ring[i - 1],
        )
        for i in range(1, NX)
    ]
    for copy in poly_copies:
        copy.start()

    rows_b = lax.broadcasted_iota(jnp.int32, (8 * SPAN, SPAN), 0)
    lanes_b = lax.broadcasted_iota(jnp.int32, (8 * SPAN, SPAN), 1)
    lane_in = rows_b & 127
    wanted = (rows_b >> 8) * 32 + (lane_in >> 3) * 2 + ((rows_b >> 7) & 1)
    chosen = ((lane_in & 7) == core * 4 + y) & (lanes_b == wanted)
    select_y[...] = jnp.where(chosen, 1.0, 0.0).astype(BF16)

    for copy in halo2_copies:
        copy.wait_recv()
    state = advance(
        tracer_out_ref[...],
        top2[...].astype(F32) * has_top,
        bottom2[...].astype(F32) * has_bottom,
        left2[...].astype(F32) * has_left,
        right2[...].astype(F32) * has_right,
    )
    tracer_out_ref[...] = state
    tracer_leave = pltpu.make_async_copy(tracer_out_ref, tracer_out_hbm, local_sem.at[11])
    tracer_leave.start()
    sst_send[...] = state[0:16, :].astype(BF16)
    sst_got[pl.ds(col, 1)] = sst_send[...][None]
    sst_copies = [
        remote(sst_send, sst_got.at[col], sst_ss.at[i], sst_rs.at[i], device)
        for i, device in enumerate(band)
    ]
    for copy in sst_copies:
        copy.start()

    next_x = x_ring[0]
    last_x = x_ring[-1]
    ring_right = []
    ring_left = []
    ring_on = []

    def circulate(j):
        count = NZ - 1 if j == 0 else NZ
        arrived = remote(
            outbox.at[pl.ds(0, count)],
            inbox.at[0, 0, pl.ds(0, count)],
            all_ss,
            all_rs.at[j],
            sibling,
        )
        arrived.wait_recv()
        yy = lax.rem(y + NY - j, NY)
        to_right = remote(
            inbox.at[0, yy], inbox.at[1, yy], ring_ss.at[0, j], ring_rs.at[0, j], next_x
        )
        to_left = remote(
            inbox.at[0, yy], inbox.at[3, yy], ring_ss.at[1, j], ring_rs.at[1, j], last_x
        )
        to_right.start()
        to_left.start()
        ring_right.append(to_right)
        ring_left.append(to_left)

    def pass_on(j):
        yy = lax.rem(y + NY - j, NY)
        ring_right[j].wait_recv()
        ring_left[j].wait_recv()
        slot, device = (1, next_x) if j % 2 == 0 else (3, last_x)
        copy = remote(
            inbox.at[slot, yy], inbox.at[2, yy], ring_ss.at[2, j], ring_rs.at[2, j], device
        )
        copy.start()
        ring_on.append(copy)

    circulate(0)
    circulate(1)

    ins[3].wait()
    ins[10].wait()
    for copy in sst_copies:
        copy.wait_recv()
    sst_got32[...] = sst_got[...].astype(F32)
    row0[...] = jnp.zeros_like(row0)
    for b in range(SPANS):
        span = sea_ref[0, b]
        source = lax.div(span, LINES)
        line = lax.rem(span, LINES)
        warmth = jnp.broadcast_to(sst_got32[source, pl.ds(line, 1), :], (16, SPAN))
        sampled = dot_t(warmth.astype(BF16), s2av[0, b])[0:1, :]
        plane = x32[0:1, b * SPAN : (b + 1) * SPAN] + sampled
        plane = jnp.where(lane + b * SPAN < n, plane, 0.0)
        half = (b % 2) * SPAN
        row0[b // 2 : b // 2 + 1, half : half + SPAN] = plane
    surface = row0[...].astype(BF16)
    plane32[...] = jnp.zeros_like(plane32)
    for k in range(WAVES):
        part = jnp.dot(surface, waves[k], preferred_element_type=F32)
        wc = table_c[k, 32:48, :]
        ws = table_s[k, 32:48, :]
        yc = part[:, 0:SPAN]
        ys = part[:, SPAN : 2 * SPAN]
        scale = scale_of(k)
        plane32[2 * k : 2 * k + 1, :] = jnp.sum(yc * wc - ys * ws, axis=0, keepdims=True) * scale
        plane32[2 * k + 1 : 2 * k + 2, :] = (
            jnp.sum(yc * ws + ys * wc, axis=0, keepdims=True) * scale
        )

    plane_send[...] = plane32[...].astype(BF16)
    plane_got[pl.ds(z, 1)] = plane_send[...][None]
    for device in z_ring:
        remote(plane_send, plane_got.at[z], plane_ss, plane_rs, device).start()

    circulate(2)
    pass_on(0)
    circulate(3)
    pass_on(1)

    def many(copies, device):
        return remote(
            plane_got.at[pl.ds(0, copies)],
            plane_got.at[pl.ds(0, copies)],
            plane_ss,
            plane_rs,
            device,
        )

    pass_on(2)
    pass_on(3)
    order = (0, 1, 3, 2)
    early = 3 * LATS

    def unpack(slot):
        place = order.index(slot)
        got32[...] = inbox[slot].astype(F32).reshape(CHIPS * 2 * PACKED, SPAN)

        def spread_row(r, _):
            columns = pl.ds(pl.multiple_of(r * SPAN, SPAN), SPAN)
            right_hand[place * LATS : (place + 1) * LATS, columns] = got32[
                pl.ds(r, LATS, stride=PACKED), :
            ].astype(BF16)
            return 0

        lax.fori_loop(0, PACKED, spread_row, 0)

    unpack(0)
    many(NZ - 1, sibling).wait_recv()
    stretch = plane_got[...].astype(F32).reshape(NZ * 16, SPAN)
    stretch = pltpu.roll(stretch, lax.rem(SPAN - NY * z, SPAN), 1)
    place = lax.broadcasted_iota(jnp.int32, (16, SPAN), 1) >> 2
    mixed = jnp.zeros((16, SPAN), F32)
    for i in range(NZ):
        tile = stretch[i * 16 : (i + 1) * 16, :]
        low = pltpu.roll(tile, 8 * i, 1) if i else tile
        high = pltpu.roll(tile, (8 * i + 4 + CHIPS) % SPAN, 1)
        mixed = jnp.where(place == 2 * i, low, jnp.where(place == 2 * i + 1, high, mixed))
    mixed = mixed.astype(BF16)
    mixed_send[...] = mixed
    pl.semaphore_wait(ready2, NX - 1)
    mixed_got[pl.ds(y * 2 + core, 1)] = mixed[None]
    steps = [(i // 8, (i // 2) % 4, i % 2) for i in range(1, NX * NY * NCORE)]
    hops = (0, 1, 2, 1)
    for dx, dy, dc in sorted(steps, key=lambda t: -hops[t[0]] - hops[t[1]]):
        cc = 1 - core if dc else core
        remote(
            mixed_send,
            mixed_got.at[dx * 8 + y * 2 + core],
            mixed_ss,
            mixed_rs,
            at(lax.rem(x + dx, NX), lax.rem(y + dy, NY), z, cc),
        ).start()

    unpack(1)
    unpack(3)
    for copy in poly_copies:
        copy.wait_recv()
    degrees = jnp.concatenate([poly_got[i] for i in order], axis=1)
    degrees_all[...] = degrees

    def legendre(i, _):
        columns = pl.ds(pl.multiple_of(i * 2 * SPAN, 2 * SPAN), 2 * SPAN)
        product2[:, columns] = jnp.dot(
            degrees_all[:, :early], right_hand[:early, columns], preferred_element_type=F32
        )
        return 0

    lax.fori_loop(0, 4, legendre, 0)
    for copy in ring_on:
        copy.wait_recv()
    unpack(2)

    def legendre_last(i, _):
        columns = pl.ds(pl.multiple_of(i * 2 * SPAN, 2 * SPAN), 2 * SPAN)
        product2[:, columns] += jnp.dot(
            degrees_all[:, early:], right_hand[early:, columns], preferred_element_type=F32
        )
        return 0

    lax.fori_loop(0, 4, legendre_last, 0)
    lanes = lax.broadcasted_iota(jnp.int32, (DEGREES, SPAN), 1)
    for c in range(2):
        for k in range(WAVES):
            total = jnp.zeros((DEGREES, SPAN), F32)
            for q in range(PARTS):
                r = c * PARTS + q
                block = product2[k * DEGREES : (k + 1) * DEGREES, r * SPAN : (r + 1) * SPAN]
                turn = (PART * (q - k)) % SPAN
                if turn:
                    block = pltpu.roll(block, turn, 1)
                keep = (lanes >= q * PART) & (lanes < (q + 1) * PART)
                total = jnp.where(keep, block, total)
            bulk[c, k] = total

    remote(
        mixed_got.at[pl.ds(0, 31)], mixed_got.at[pl.ds(0, 31)], mixed_ss, mixed_rs, sibling
    ).wait_recv()
    stacked = jnp.concatenate(
        [
            jnp.concatenate([mixed_got[slot * 8 + i] for i in range(8)], axis=1)
            for slot in range(NX)
        ],
        axis=0,
    )
    sorted_rows = jnp.dot(stacked, select_y[...], preferred_element_type=F32).astype(BF16)
    surface_rows = jnp.concatenate(
        [sorted_rows[slot * 16 : (slot + 1) * 16, :] for slot in order], axis=1
    )
    surface_rows = jnp.concatenate(
        [surface_rows, jnp.zeros((SPAN - 16, NX * LATS), BF16)], axis=0
    )
    product0[...] = dot_t(degrees, surface_rows)
    leaves = [tracer_leave]
    for c in range(2):
        for k in range(WAVES):
            block = product0[k * DEGREES : (k + 1) * DEGREES, :]
            turn = (-(2 * k + c)) % SPAN
            if turn:
                block = pltpu.roll(block, turn, 1)
            total = jnp.where(lanes == 0, block, bulk[c, k])
            spectral_ref[c, k] = total[:, 0:PLANES].astype(BF16)
        leave = pltpu.make_async_copy(
            spectral_ref.at[c], spectral_hbm.at[c], local_sem.at[12 + c]
        )
        leave.start()
        leaves.append(leave)

    for copy in flux_copies + halo_copies + halo2_copies + sst_copies + poly_copies:
        copy.wait_send()
    core_copy.wait_send()
    remote(
        outbox.at[pl.ds(0, CHIPS - 1)],
        outbox.at[pl.ds(0, CHIPS - 1)],
        all_ss,
        all_rs.at[0],
        sibling,
    ).wait_send()
    many(NZ - 1, sibling).wait_send()
    remote(
        mixed_got.at[pl.ds(0, 31)], mixed_got.at[pl.ds(0, 31)], mixed_ss, mixed_rs, sibling
    ).wait_send()
    for copy in ring_right + ring_left + ring_on:
        copy.wait_send()
    for copy in leaves:
        copy.wait()


def local(
    physical_values,
    samples_per_parallel,
    associated_polynomials,
    heat_salt_anomalies,
    courant_numbers,
    water_indicator,
    air_to_sea_coefficients,
    air_partner_span,
    sea_to_air_coefficients,
    sea_partner_span,
):
    hbm = pl.BlockSpec(memory_space=pltpu.HBM)
    dma = pltpu.SemaphoreType.DMA
    scratch = [
        pltpu.VMEM((2, WAVES, DEGREES, PLANES), BF16),
        pltpu.VMEM((TRACER_ROWS, SPAN), F32),
        pltpu.VMEM((TRACER_ROWS, SPAN), F32),
        pltpu.VMEM((TRACER_ROWS, SPAN), F32),
        pltpu.VMEM((LINES, SPAN), jnp.int32),
        pltpu.SMEM((512,), jnp.int32),
        pltpu.SMEM((1, 2, LINES), jnp.int32),
        pltpu.SMEM((1, SPANS), jnp.int32),
        pltpu.VMEM((1, PLANES, POINTS), BF16),
        pltpu.VMEM((32, POINTS), BF16),
        pltpu.VMEM((WAVES, LATS, NX * DEGREES), BF16),
        pltpu.VMEM((1, SPANS, SPAN, SPAN), BF16),
        pltpu.VMEM((LINES, 2, SPAN, SPAN), BF16),
        pltpu.VMEM((32, POINTS), F32),
        pltpu.VMEM((48, SPAN), F32),
        pltpu.VMEM((NCOL, 48, SPAN), F32),
        pltpu.VMEM((NCOL, 16, SPAN), F32),
        pltpu.VMEM((32, SPAN), F32),
        pltpu.VMEM((160, SPAN), F32),
        pltpu.VMEM((80, SPAN), F32),
        pltpu.VMEM((TRACER_ROWS, SPAN), F32),
        pltpu.VMEM((TRACER_ROWS, SPAN), F32),
        pltpu.VMEM((TRACER_ROWS, SPAN), F32),
        pltpu.VMEM((WAVES, 48, SPAN), F32),
        pltpu.VMEM((WAVES, 48, SPAN), F32),
        pltpu.VMEM((WAVES, SEG, 2 * SPAN), BF16),
        pltpu.VMEM((SEGS * PITCH, SEG), BF16),
        pltpu.VMEM((SEGS * PITCH, 2 * SPAN), F32),
        pltpu.VMEM((WAVES, 2, PITCH, SPAN), F32),
        pltpu.VMEM((16, SEG), F32),
        pltpu.VMEM((PACKED, SPAN, SPAN), F32),
        pltpu.VMEM((LATS * PACKED, SPAN), F32),
        pltpu.VMEM((CHIPS, 2 * PACKED, SPAN), F32),
        pltpu.VMEM((NX * LATS, PACKED * SPAN), BF16),
        pltpu.VMEM((LATS * PACKED, SPAN), F32),
        pltpu.VMEM((WAVES * DEGREES, PACKED * SPAN), F32),
        pltpu.VMEM((WAVES * DEGREES, SPAN), F32),
        pltpu.VMEM((WAVES * DEGREES, NX * LATS), BF16),
        pltpu.VMEM((16, SPAN), F32),
        pltpu.VMEM((8 * SPAN, SPAN), BF16),
        pltpu.VMEM((2, WAVES, DEGREES, SPAN), F32),
        pltpu.VMEM((NX, WAVES * DEGREES, LATS), BF16),
        pltpu.VMEM((48, SPAN), BF16),
        pltpu.VMEM((NCOL, 48, SPAN), BF16),
        pltpu.VMEM((32, SPAN), BF16),
        pltpu.VMEM((32, SPAN), BF16),
        pltpu.VMEM((160, SPAN), BF16),
        pltpu.VMEM((32, SPAN), BF16),
        pltpu.VMEM((32, SPAN), BF16),
        pltpu.VMEM((160, SPAN), BF16),
        pltpu.VMEM((160, SPAN), BF16),
        pltpu.VMEM((16, SPAN), BF16),
        pltpu.VMEM((16, SPAN), BF16),
        pltpu.VMEM((64, SPAN), BF16),
        pltpu.VMEM((16, SPAN), BF16),
        pltpu.VMEM((16, SPAN), BF16),
        pltpu.VMEM((64, SPAN), BF16),
        pltpu.VMEM((64, SPAN), BF16),
        pltpu.VMEM((16, SPAN), BF16),
        pltpu.VMEM((NCOL, 16, SPAN), BF16),
        pltpu.VMEM((NX, WAVES * DEGREES, LATS), BF16),
        pltpu.VMEM((CHIPS * PACKED, SPAN), BF16),
        pltpu.VMEM((CHIPS * PACKED, SPAN), BF16),
        pltpu.VMEM((CHIPS, 2 * PACKED, SPAN), BF16),
        pltpu.VMEM((NX, NY, NZ, 2 * PACKED, SPAN), BF16),
        pltpu.VMEM((16, SPAN), BF16),
        pltpu.VMEM((NZ, 16, SPAN), BF16),
        pltpu.VMEM((16, SPAN), BF16),
        pltpu.VMEM((NX * NY * NCORE, 16, SPAN), BF16),
        dma((14,)),
        dma((NCOL - 1,)),
        dma((NCOL - 1,)),
        dma((4,)),
        dma((4,)),
        dma((4,)),
        dma((4,)),
        dma((NCOL - 1,)),
        dma((NCOL - 1,)),
        dma((NX - 1,)),
        dma((NX - 1,)),
        dma,
        dma,
        dma,
        dma((NY,)),
        dma((3, NY)),
        dma((3, NY)),
        dma,
        dma,
        dma,
        dma,
        pltpu.SemaphoreType.REGULAR,
        pltpu.SemaphoreType.REGULAR,
    ]
    spectral, tracers = pl.pallas_call(
        kernel,
        out_shape=(
            jax.ShapeDtypeStruct((2, WAVES, DEGREES, PLANES), BF16),
            jax.ShapeDtypeStruct((TRACER_ROWS, SPAN), F32),
        ),
        in_specs=[hbm] * 10,
        out_specs=(hbm, hbm),
        scratch_shapes=scratch,
        compiler_params=pltpu.CompilerParams(
            collective_id=0, has_side_effects=True, vmem_limit_bytes=64 * 2**20
        ),
        cost_estimate=pl.CostEstimate(
            flops=1_000_000_000, bytes_accessed=3_000_000, transcendentals=0
        ),
    )(
        physical_values,
        associated_polynomials,
        sea_to_air_coefficients,
        air_to_sea_coefficients,
        heat_salt_anomalies.reshape(TRACER_ROWS, SPAN),
        courant_numbers.reshape(TRACER_ROWS, SPAN),
        water_indicator,
        samples_per_parallel,
        jnp.transpose(air_partner_span, (1, 2, 0)),
        sea_partner_span,
    )
    return spectral.transpose(3, 0, 1, 2), tracers.reshape(2, 8, LINES, SPAN)


def solution(mesh):
    placed = (
        P(("grp", "row", "col"), None, None),
        P(),
        P(("row", "col"), "grp", None),
        P(None, None, ("grp", "row"), "col"),
        P(None, None, ("grp", "row"), "col"),
        P(("grp", "row"), "col"),
        P(("grp", "row"), None, "col", None),
        P(("grp", "row"), "col", None),
        P(("grp", "row", "col"), None, None, None),
        P(("grp", "row", "col"), None),
    )
    return jax.shard_map(
        local,
        mesh=mesh,
        in_specs=placed,
        out_specs=(P(None, None, ("row", "col"), "grp"), P(None, None, ("grp", "row"), "col")),
        check_vma=False,
    )
```
